32 devices in a mesh: dp: 16 (over z, y, x), heads: 2 (over core).
Axes of the slice: x: 2, y: 2, z: 4, core: 2. Of those that a mesh axis runs over, the one named last changes fastest.
Arguments:
- tokens: bfloat16 [128, 64, 768], P(('dp', 'heads')), may hold values from -6 to 6
- images: bfloat16 [32, 256, 768], P(('dp', 'heads')), may hold values from -6 to 6
- segment_labels: int32 [128, 64], P('dp'), may hold values from 0 to 4, as said below
- image_index: int32 [128, 5], P('dp'), may hold values from 0 to 1
- cotangent: bfloat16 [128, 64, 768], P(('dp', 'heads')), may hold values from -6 to 6
- norm_gain: bfloat16 [5, 768], P(None, ('dp', 'heads')), may hold values from 0.099609375 to 1.8984375
- vector_bias: bfloat16 [16, 768], P(None, ('dp', 'heads')), may hold values from -1.796875 to 1.796875
- up_bias: bfloat16 [2, 3072], P(None, ('dp', 'heads')), may hold values from -3 to 3
- self_weight: bfloat16 [2, 768, 2304], P(None, ('dp', 'heads')), may hold values from -0.21875 to 0.21875
- self_out_weight: bfloat16 [2, 768, 768], P(None, ('dp', 'heads')), may hold values from -0.625 to 0.625
- up_weight: bfloat16 [2, 768, 3072], P(None, ('dp', 'heads')), may hold values from -0.21875 to 0.21875
- down_weight: bfloat16 [2, 3072, 768], P(None, ('dp', 'heads')), may hold values from -0.109375 to 0.109375
- query_weight: bfloat16 [768, 768], P(('dp', 'heads')), may hold values from -0.21875 to 0.21875
- pair_weight: bfloat16 [768, 1536], P(('dp', 'heads')), may hold values from -0.21875 to 0.21875
- cross_out_weight: bfloat16 [768, 768], P(('dp', 'heads')), may hold values from -2.5 to 2.5
Outputs:
- layer_out: float32 [128, 64, 768], P(('dp', 'heads'))
- token_gradient: float32 [128, 64, 768], P(('dp', 'heads'))
- image_gradient: float32 [32, 256, 768], P(('dp', 'heads'))
- norm_gain_gradient: float32 [5, 768], P(None, ('dp', 'heads'))
- vector_bias_gradient: float32 [16, 768], P(None, ('dp', 'heads'))
- up_bias_gradient: float32 [2, 3072], P(None, ('dp', 'heads'))
- self_weight_gradient: float32 [2, 768, 2304], P(None, ('dp', 'heads'))
- self_out_gradient: float32 [2, 768, 768], P(None, ('dp', 'heads'))
- up_gradient: float32 [2, 768, 3072], P(None, ('dp', 'heads'))
- down_gradient: float32 [2, 3072, 768], P(None, ('dp', 'heads'))
- query_gradient: float32 [768, 768], P(('dp', 'heads'))
- pair_gradient: float32 [768, 1536], P(('dp', 'heads'))
- cross_out_gradient: float32 [768, 768], P(('dp', 'heads'))
The draws below stay inside these ranges and needn't reach their ends.
Inputs may be any that keep to these rules, and one draw needn't show every extreme that they name: `segment_labels`: each row holds 4 captions numbered 1 to 4 in order, each of 8 to 15 tokens, then padding numbered 0. `image_index`: entry s of a row is the image of its caption s, entry 0 that of its padding, counted among the 2 images of the row's group.
All inputs are finite; a program needn't handle non-finite values.
Results may differ from the reference program's by a relative error of at most 0.025.
Values may be sent and summed in bfloat16 or wider, within the bound.
A program may use at most 320 MiB of HBM per device.

```python
import jax
import jax.numpy as jnp
from jax import lax

D = 768
HEADS = 12
HEAD = 64
FF = 3072
IMG_TOK = 256
ROW_LEN = 64
NSEG = 4
ROWS = 128
IMAGES = 32
GROUP_ROWS = 8
GROUP_IMAGES = 2


def draw_segment_labels(key, part):
    key = jax.random.fold_in(key, 7)
    lengths = jax.random.randint(key, (ROWS, NSEG), ROW_LEN // 8, ROW_LEN // NSEG)
    boundary = jnp.cumsum(lengths, axis=1)
    position = jnp.arange(ROW_LEN)
    passed = jnp.sum((position[None, :, None] >= boundary[:, None, :]).astype(jnp.int32), axis=2)
    return jnp.where(passed < NSEG, passed + 1, 0).astype(jnp.int32)


def place_ends(values, own_key, least, high):
    place = [jax.random.randint(jax.random.fold_in(own_key, axis), (), 0, length) for axis, length in enumerate(values.shape)]
    widest = values.shape.index(max(values.shape))
    next_to = place[:widest] + [(place[widest] + 1) % values.shape[widest]] + place[widest + 1:]
    return values.at[tuple(place)].set(least).at[tuple(next_to)].set(high)


def with_spikes(values, stream_key, source, target, blocks, factor):
    def block_of(dim):
        return (jnp.arange(values.shape[dim]) // (values.shape[dim] // blocks)).reshape((-1,) + (1,) * (values.ndim - 1 - dim))

    near = jax.random.permutation(stream_key, blocks)[block_of(target)]
    second = (block_of(target) + blocks // 2) % blocks
    return jnp.where((block_of(source) == near) | (block_of(source) == second), factor * values, values)


def level_of(key, extent, cuts, low, high):
    factor_of = 1.0
    for dim, blocks in cuts:
        heights = jax.random.uniform(jax.random.fold_in(jax.random.fold_in(key, 6), dim), (blocks,), jnp.float32, low / len(cuts), high / len(cuts))
        factor_of = factor_of * jnp.repeat(jnp.exp(heights), extent[dim] // blocks).reshape((-1,) + (1,) * (len(extent) - 1 - dim))
    return factor_of


def noise(own_key, extent, scale, bound, cuts=(), kind=jnp.bfloat16):
    array = scale * jax.random.normal(own_key, extent, jnp.float32)
    if cuts:
        array = array * level_of(own_key, extent, cuts, -0.22, 0.18)
    return jnp.clip(array, -bound, bound).astype(kind)


def bell_draw_with(own_key, dims, scale, most, shards, heavy, dtype=jnp.bfloat16):
    result = scale * jax.random.normal(own_key, dims, jnp.float32)
    if shards:
        result = result * level_of(own_key, dims, shards, -0.22, 0.18)
    return jnp.clip(with_spikes(result, jax.random.fold_in(own_key, 3), *heavy), -most, most).astype(dtype)


def setup_inputs(seed: int = 0) -> dict:
    key_of = jax.random.split(jax.random.key(seed), 16)
    return {
        "tokens": bell_draw_with(key_of[0], (ROWS, ROW_LEN, D), 1.0, 6.0, ((0, 32),), (0, 2, 32, 2.75)),
        "images": noise(key_of[1], (IMAGES, IMG_TOK, D), 1.0, 6.0, ((0, 32),)),
        "segment_labels": draw_segment_labels(jax.random.fold_in(key_of[15], 71), 0),
        "image_index": place_ends(jax.random.randint(key_of[3], (ROWS, NSEG + 1), 0, GROUP_IMAGES), jax.random.fold_in(key_of[3], 1), 0, GROUP_IMAGES - 1).astype(jnp.int32),
        "cotangent": bell_draw_with(key_of[4], (ROWS, ROW_LEN, D), 1.0, 6.0, ((0, 32),), (0, 2, 32, 2.75)),
        "norm_gain": jnp.clip(1.0 + 0.18 * jax.random.normal(key_of[5], (5, D), jnp.float32), 0.099609375, 1.8984375).astype(jnp.bfloat16),
        "vector_bias": noise(key_of[6], (16, D), 0.3, 1.796875, ((1, 32),)),
        "up_bias": noise(key_of[7], (2, FF), 0.5, 3.0, ((1, 32),)),
        "self_weight": noise(key_of[8], (2, D, 3 * D), D ** -0.5, 0.21875, ((1, 32),)),
        "self_out_weight": noise(key_of[9], (2, D, D), (D // 8) ** -0.5, 0.625, ((1, 32),)),
        "up_weight": noise(key_of[10], (2, D, FF), D ** -0.5, 0.21875, ((1, 32),)),
        "down_weight": noise(key_of[11], (2, FF, D), FF ** -0.5, 0.109375, ((1, 32),)),
        "query_weight": noise(key_of[12], (D, D), D ** -0.5, 0.21875, ((0, 32),)),
        "pair_weight": noise(key_of[13], (D, 2 * D), D ** -0.5, 0.21875, ((0, 32),)),
        "cross_out_weight": noise(key_of[14], (D, D), (D // 128) ** -0.5, 2.5, ((0, 32),)),
    }


@jax.custom_vjp
def low(v):
    return lax.optimization_barrier(v.astype(jnp.bfloat16)).astype(jnp.float32)

@jax.custom_vjp
def low_back(v):
    return v

def low_keep(v):
    return (low(v), None)

def low_pass(kept, grad):
    return (grad,)

def back_keep(v):
    return (v, None)

def back_low(kept, grad):
    return (low(grad),)
low.defvjp(low_keep, low_pass)
low_back.defvjp(back_keep, back_low)
highest = lax.Precision.HIGHEST

def narrowed(value):
    return low_back(low(value))

def layer_norm(residual, gain, shift):
    center = residual - lax.optimization_barrier(jnp.mean(residual, axis=-1, keepdims=True))
    variance = lax.optimization_barrier(jnp.mean(center * center, axis=-1, keepdims=True))
    return center * lax.rsqrt(variance + 1e-05) * gain + shift

def project(left, weight):
    return jnp.einsum('rld,de->rle', left, weight, precision=highest, preferred_element_type=jnp.float32)

def self_attention(residual, allowed, gain, shift, weight, query_bias, value_bias, out_weight, out_bias):
    rows, length, width = residual.shape
    normed = low(layer_norm(residual, gain, shift))
    offset = jnp.concatenate([query_bias, jnp.zeros_like(query_bias), value_bias])
    mixed = narrowed(project(normed, weight) + offset).reshape(rows, length, 3, HEADS, HEAD)
    scores = jnp.einsum('rqhd,rkhd->rhqk', mixed[:, :, 0], mixed[:, :, 1], precision=highest, preferred_element_type=jnp.float32)
    scores = low_back(scores * HEAD ** (-0.5))
    scores = jnp.where(allowed[:, None], scores, -1e+30)
    weights = low(jax.nn.softmax(scores, axis=-1))
    attended = jnp.einsum('rhqk,rkhd->rqhd', weights, mixed[:, :, 2], precision=highest, preferred_element_type=jnp.float32)
    attended = narrowed(attended).reshape(rows, length, width)
    return residual + low_back(project(attended, out_weight) + out_bias)

def cross_attention(residual, image_keys, image_values, chosen, gain, shift, weight, query_bias, out_weight, out_bias):
    rows, length, width = residual.shape
    normed = low(layer_norm(residual, gain, shift))
    queries = narrowed(project(normed, weight) + query_bias).reshape(rows, length, HEADS, HEAD)
    scores = jnp.einsum('rqhd,gkhd->rhqgk', queries, image_keys, precision=highest, preferred_element_type=jnp.float32)
    scores = low_back(scores * HEAD ** (-0.5))
    scores = jnp.where(chosen[:, None, :, :, None], scores, -1e+30)
    count = image_keys.shape[0] * image_keys.shape[1]
    weights = low(jax.nn.softmax(scores.reshape(rows, HEADS, length, count), axis=-1))
    flat_values = image_values.reshape(count, HEADS, HEAD)
    attended = jnp.einsum('rhqc,chd->rqhd', weights, flat_values, precision=highest, preferred_element_type=jnp.float32)
    attended = narrowed(attended).reshape(rows, length, width)
    return residual + low_back(project(attended, out_weight) + out_bias)

def feed_forward(residual, gain, shift, up_matrix, up_shift, down_matrix, down_shift):
    normed = low(layer_norm(residual, gain, shift))
    hidden = low_back(project(normed, up_matrix) + up_shift)
    active = low(jax.nn.gelu(hidden, approximate=True))
    return residual + low_back(project(active, down_matrix) + down_shift)

def group_forward(params, residual, pictures, segments, caption_image):
    norm_gain, vector_bias, up_bias, self_weight, self_out_weight, up_weight, down_weight, query_weight, pair_weight, cross_out_weight = params
    width = residual.shape[2]
    position = jnp.arange(residual.shape[1])
    allowed = (segments[:, :, None] == segments[:, None, :]) & (position[:, None] >= position[None, :])[None]
    chosen = caption_image[:, :, None] == jnp.arange(pictures.shape[0])[None, None, :]
    offset = jnp.concatenate([jnp.zeros_like(vector_bias[14]), vector_bias[14]])
    pair = narrowed(project(pictures, pair_weight) + offset)
    layout = (pictures.shape[0], pictures.shape[1], HEADS, HEAD)
    image_keys = pair[:, :, :width].reshape(layout)
    image_values = pair[:, :, width:].reshape(layout)
    residual = self_attention(residual, allowed, norm_gain[0], vector_bias[0], self_weight[0], vector_bias[5], vector_bias[6], self_out_weight[0], vector_bias[7])
    residual = feed_forward(residual, norm_gain[1], vector_bias[1], up_weight[0], up_bias[0], down_weight[0], vector_bias[8])
    residual = self_attention(residual, allowed, norm_gain[2], vector_bias[2], self_weight[1], vector_bias[9], vector_bias[10], self_out_weight[1], vector_bias[11])
    residual = cross_attention(residual, image_keys, image_values, chosen, norm_gain[3], vector_bias[3], query_weight, vector_bias[13], cross_out_weight, vector_bias[15])
    residual = feed_forward(residual, norm_gain[4], vector_bias[4], up_weight[1], up_bias[1], down_weight[1], vector_bias[12])
    return residual

def reference(tokens, images, segment_labels, image_index, cotangent, norm_gain, vector_bias, up_bias, self_weight, self_out_weight, up_weight, down_weight, query_weight, pair_weight, cross_out_weight):
    params = tuple((weight.astype(jnp.float32) for weight in (norm_gain, vector_bias, up_bias, self_weight, self_out_weight, up_weight, down_weight, query_weight, pair_weight, cross_out_weight)))
    caption_image = jnp.take_along_axis(image_index, segment_labels, axis=1)
    count = ROWS // GROUP_ROWS

    def one_group(totals, inputs):
        residual, pictures, segments, picked, adjoint = inputs

        def forward(weights, start, shown):
            return group_forward(weights, start, shown, segments, picked)
        output, pull = jax.vjp(forward, params, residual.astype(jnp.float32), pictures.astype(jnp.float32))
        weight_parts, residual_part, picture_part = pull(adjoint.astype(jnp.float32))
        totals = jax.tree.map(jnp.add, totals, weight_parts)
        return (totals, (output, residual_part, picture_part))
    zeros = jax.tree.map(jnp.zeros_like, params)
    inputs = (tokens.reshape(count, GROUP_ROWS, ROW_LEN, D), images.reshape(count, GROUP_IMAGES, IMG_TOK, D), segment_labels.reshape(count, GROUP_ROWS, ROW_LEN), caption_image.reshape(count, GROUP_ROWS, ROW_LEN), cotangent.reshape(count, GROUP_ROWS, ROW_LEN, D))
    totals, (output, residual_part, picture_part) = lax.scan(one_group, zeros, inputs)
    return (output.reshape(ROWS, ROW_LEN, D), residual_part.reshape(ROWS, ROW_LEN, D), picture_part.reshape(IMAGES, IMG_TOK, D), totals[0], totals[1], totals[2], totals[3], totals[4], totals[5], totals[6], totals[7], totals[8], totals[9])
```

```python
from functools import partial
import math

import jax
import jax.numpy as jnp
from jax import lax
from jax.experimental import pallas as pl
from jax.experimental.pallas import tpu as pltpu
from jax.sharding import PartitionSpec as P

HEADS = 12
HEAD = 64


masked_score = -1e30


def layer_norm(residual, gain, shift):
    center = residual - jnp.mean(residual, axis=-1, keepdims=True)
    variance = jnp.mean(center * center, axis=-1, keepdims=True)
    return center * lax.rsqrt(variance + 1e-05) * gain + shift


def project(left, weight):
    return jnp.einsum("rld,de->rle", left, weight, preferred_element_type=jnp.float32)


def weight_adjoint(left, adjoint):
    return jnp.einsum("rld,rle->de", left, adjoint, preferred_element_type=jnp.float32)


def project_back(adjoint, weight):
    return jnp.einsum("rle,de->rld", adjoint, weight, preferred_element_type=jnp.float32)


def column_total(adjoint):
    return jnp.sum(adjoint, axis=(0, 1), dtype=jnp.float32)


def norm_back(residual, gain, shift, adjoint):
    unused, pull = jax.vjp(layer_norm, residual, gain, shift)
    return pull(adjoint)


def rows_to_heads(pieces):
    return lax.all_to_all(pieces, "heads", split_axis=3, concat_axis=0, tiled=True)


def heads_to_rows(pieces):
    return lax.all_to_all(pieces, "heads", split_axis=0, concat_axis=3, tiled=True)


def adjoint_to_heads(pieces):
    return lax.all_to_all(pieces, "heads", split_axis=3, concat_axis=0, tiled=True)


def adjoint_to_rows(pieces):
    return lax.all_to_all(pieces, "heads", split_axis=0, concat_axis=3, tiled=True)


def softmax_parts(scores):
    peak = jnp.max(scores, axis=-1, keepdims=True)
    log_total = peak + jnp.log(jnp.sum(jnp.exp(scores - peak), axis=-1, keepdims=True))
    return (jnp.exp(scores - log_total), log_total)


def softmax_back(shares, adjoint):
    return (shares * (adjoint - jnp.sum(shares * adjoint, axis=-1, keepdims=True))).astype(
        jnp.bfloat16
    )


def self_scores(queries, keys, allowed):
    scores = jnp.einsum(
        "rqhd,rkhd->rhqk", queries, keys, preferred_element_type=jnp.float32
    ) * HEAD ** (-0.5)
    return jnp.where(allowed[:, None], scores, masked_score)


def self_heads_forward(queries, keys, values, allowed):
    shares, log_total = softmax_parts(self_scores(queries, keys, allowed))
    attended = jnp.einsum(
        "rhqk,rkhd->rqhd", shares.astype(jnp.bfloat16), values, preferred_element_type=jnp.float32
    )
    return (attended.astype(jnp.bfloat16), log_total)


def self_heads_back(queries, keys, values, allowed, log_total, adjoint):
    shares = jnp.exp(self_scores(queries, keys, allowed) - log_total)
    value_adjoint = jnp.einsum(
        "rhqk,rqhd->rkhd", shares.astype(jnp.bfloat16), adjoint, preferred_element_type=jnp.float32
    )
    share_adjoint = jnp.einsum(
        "rqhd,rkhd->rhqk", adjoint, values, preferred_element_type=jnp.float32
    )
    score_adjoint = softmax_back(shares, share_adjoint)
    scale = HEAD ** (-0.5)
    query_adjoint = (
        jnp.einsum("rhqk,rkhd->rqhd", score_adjoint, keys, preferred_element_type=jnp.float32)
        * scale
    )
    key_adjoint = (
        jnp.einsum("rhqk,rqhd->rkhd", score_adjoint, queries, preferred_element_type=jnp.float32)
        * scale
    )
    return (
        query_adjoint.astype(jnp.bfloat16),
        key_adjoint.astype(jnp.bfloat16),
        value_adjoint.astype(jnp.bfloat16),
    )


def cross_scores(queries, image_keys, chosen):
    rows, length, heads, head_size = queries.shape
    scores = jnp.einsum(
        "rqhd,gkhd->rhqgk", queries, image_keys, preferred_element_type=jnp.float32
    ) * HEAD ** (-0.5)
    scores = jnp.where(chosen[:, None, :, :, None], scores, masked_score)
    return scores.reshape(rows, heads, length, -1)


def block_rows(rows, length):
    return math.gcd(rows, max(1, 512 // length))


def cross_heads_forward(queries, image_keys, image_values, chosen):
    rows, length, heads, head_size = queries.shape
    block = block_rows(rows, length)
    flat_values = image_values.reshape(-1, heads, head_size)

    def one_block(inputs):
        block_queries, block_chosen = inputs
        shares, log_total = softmax_parts(cross_scores(block_queries, image_keys, block_chosen))
        attended = jnp.einsum(
            "rhqc,chd->rqhd",
            shares.astype(jnp.bfloat16),
            flat_values,
            preferred_element_type=jnp.float32,
        )
        return (attended.astype(jnp.bfloat16), log_total)

    blocked = (
        queries.reshape(rows // block, block, length, heads, head_size),
        chosen.reshape(rows // block, block, length, -1),
    )
    attended, log_total = lax.map(one_block, blocked)
    return (attended.reshape(queries.shape), log_total)


def cross_heads_back(queries, image_keys, image_values, chosen, log_total, adjoint):
    rows, length, heads, head_size = queries.shape
    block = block_rows(rows, length)
    flat_keys = image_keys.reshape(-1, heads, head_size)
    flat_values = image_values.reshape(-1, heads, head_size)
    scale = HEAD ** (-0.5)

    def one_block(carry, inputs):
        key_total, value_total = carry
        block_queries, block_chosen, block_log, block_adjoint = inputs
        shares = jnp.exp(cross_scores(block_queries, image_keys, block_chosen) - block_log)
        value_total = value_total + jnp.einsum(
            "rhqc,rqhd->chd",
            shares.astype(jnp.bfloat16),
            block_adjoint,
            preferred_element_type=jnp.float32,
        )
        share_adjoint = jnp.einsum(
            "rqhd,chd->rhqc", block_adjoint, flat_values, preferred_element_type=jnp.float32
        )
        score_adjoint = softmax_back(shares, share_adjoint)
        key_total = (
            key_total
            + jnp.einsum(
                "rhqc,rqhd->chd", score_adjoint, block_queries, preferred_element_type=jnp.float32
            )
            * scale
        )
        query_adjoint = (
            jnp.einsum(
                "rhqc,chd->rqhd", score_adjoint, flat_keys, preferred_element_type=jnp.float32
            )
            * scale
        )
        return ((key_total, value_total), query_adjoint.astype(jnp.bfloat16))

    start = jnp.zeros(flat_keys.shape, jnp.float32)
    blocked = (
        queries.reshape(rows // block, block, length, heads, head_size),
        chosen.reshape(rows // block, block, length, -1),
        log_total,
        adjoint.reshape(rows // block, block, length, heads, head_size),
    )
    (key_total, value_total), query_adjoint = lax.scan(one_block, (start, start), blocked)
    return (
        query_adjoint.reshape(queries.shape),
        key_total.astype(jnp.bfloat16),
        value_total.astype(jnp.bfloat16),
    )


def self_forward(
    residual, allowed, gain, shift, weight, query_bias, value_bias, out_weight, out_bias, groups
):
    rows, length, width = residual.shape
    span = width // groups
    normed = layer_norm(residual, gain, shift).astype(jnp.bfloat16)
    offset = jnp.concatenate([query_bias, jnp.zeros_like(query_bias), value_bias])
    mixed = (project(normed, weight) + offset).astype(jnp.bfloat16)
    gathered = rows_to_heads(mixed.reshape(rows, length, 3, groups, span))
    gathered = gathered.reshape(rows * groups, length, 3, HEADS // groups, HEAD)
    queries, keys, values = (gathered[:, :, 0], gathered[:, :, 1], gathered[:, :, 2])
    attended, log_total = self_heads_forward(queries, keys, values, allowed)
    merged = heads_to_rows(attended.reshape(rows * groups, length, 1, 1, span)).reshape(
        rows, length, width
    )
    kept = (residual, normed, queries, keys, values, log_total, merged)
    return (residual + project(merged, out_weight) + out_bias, kept)


def self_backward(adjoint, kept, gain, shift, weight, out_weight, allowed, groups):
    residual, normed, queries, keys, values, log_total, merged = kept
    rows, length, width = residual.shape
    span = width // groups
    branch = adjoint.astype(jnp.bfloat16)
    out_bias_adjoint = column_total(branch)
    merged_adjoint = project_back(branch, out_weight).astype(jnp.bfloat16)
    head_adjoint = adjoint_to_heads(merged_adjoint.reshape(rows, length, 1, groups, span))
    head_adjoint = head_adjoint.reshape(rows * groups, length, HEADS // groups, HEAD)
    query_adjoint, key_adjoint, value_adjoint = self_heads_back(
        queries, keys, values, allowed, log_total, head_adjoint
    )
    stacked = jnp.stack([query_adjoint, key_adjoint, value_adjoint], axis=2).reshape(
        rows * groups, length, 3, 1, span
    )
    mixed_adjoint = adjoint_to_rows(stacked).reshape(rows, length, 3 * width)
    offset_adjoint = column_total(mixed_adjoint)
    residual_adjoint, gain_adjoint, shift_adjoint = norm_back(
        residual, gain, shift, project_back(mixed_adjoint, weight)
    )
    pairs = ((normed, mixed_adjoint), (merged, branch))
    small = (
        gain_adjoint,
        shift_adjoint,
        offset_adjoint[:width],
        offset_adjoint[2 * width :],
        out_bias_adjoint,
    )
    return (adjoint + residual_adjoint, pairs, small)


def cross_forward(
    residual,
    pictures,
    chosen,
    gain,
    shift,
    weight,
    query_bias,
    pair_matrix,
    value_bias,
    out_weight,
    out_bias,
    groups,
    member,
):
    rows, length, width = residual.shape
    span = width // groups
    key_weight = lax.dynamic_slice_in_dim(pair_matrix, member * span, span, 1)
    value_weight = lax.dynamic_slice_in_dim(pair_matrix, width + member * span, span, 1)
    value_shift = lax.dynamic_slice_in_dim(value_bias, member * span, span, 0)
    layout = (pictures.shape[0], pictures.shape[1], HEADS // groups, HEAD)
    image_keys = project(pictures, key_weight).astype(jnp.bfloat16).reshape(layout)
    image_values = (
        (project(pictures, value_weight) + value_shift).astype(jnp.bfloat16).reshape(layout)
    )
    normed = layer_norm(residual, gain, shift).astype(jnp.bfloat16)
    query_rows = (project(normed, weight) + query_bias).astype(jnp.bfloat16)
    queries = rows_to_heads(query_rows.reshape(rows, length, 1, groups, span))
    queries = queries.reshape(rows * groups, length, HEADS // groups, HEAD)
    attended, log_total = cross_heads_forward(queries, image_keys, image_values, chosen)
    merged = heads_to_rows(attended.reshape(rows * groups, length, 1, 1, span)).reshape(
        rows, length, width
    )
    kept = (residual, normed, queries, image_keys, image_values, log_total, merged)
    return (residual + project(merged, out_weight) + out_bias, kept)


def cross_backward(
    adjoint, kept, pictures, chosen, gain, shift, weight, pair_matrix, out_weight, groups, member
):
    residual, normed, queries, image_keys, image_values, log_total, merged = kept
    rows, length, width = residual.shape
    span = width // groups
    key_weight = lax.dynamic_slice_in_dim(pair_matrix, member * span, span, 1)
    value_weight = lax.dynamic_slice_in_dim(pair_matrix, width + member * span, span, 1)
    branch = adjoint.astype(jnp.bfloat16)
    out_bias_adjoint = column_total(branch)
    merged_adjoint = project_back(branch, out_weight).astype(jnp.bfloat16)
    head_adjoint = adjoint_to_heads(merged_adjoint.reshape(rows, length, 1, groups, span))
    head_adjoint = head_adjoint.reshape(rows * groups, length, HEADS // groups, HEAD)
    query_adjoint, key_adjoint, value_adjoint = cross_heads_back(
        queries, image_keys, image_values, chosen, log_total, head_adjoint
    )
    query_rows = adjoint_to_rows(query_adjoint.reshape(rows * groups, length, 1, 1, span)).reshape(
        rows, length, width
    )
    query_bias_adjoint = column_total(query_rows)
    residual_adjoint, gain_adjoint, shift_adjoint = norm_back(
        residual, gain, shift, project_back(query_rows, weight)
    )
    layout = (pictures.shape[0], pictures.shape[1], span)
    key_adjoint = key_adjoint.reshape(layout)
    value_adjoint = value_adjoint.reshape(layout)
    value_bias_adjoint = lax.dynamic_update_slice_in_dim(
        jnp.zeros((width,), jnp.float32), column_total(value_adjoint), member * span, 0
    )
    picture_adjoint = project_back(key_adjoint, key_weight) + project_back(
        value_adjoint, value_weight
    )
    pairs = ((normed, query_rows), (merged, branch), (key_adjoint, value_adjoint))
    small = (gain_adjoint, shift_adjoint, query_bias_adjoint, value_bias_adjoint, out_bias_adjoint)
    return (adjoint + residual_adjoint, pairs, small, picture_adjoint)


def feed_forward(residual, gain, shift, up_matrix, up_shift, down_matrix, down_shift):
    normed = layer_norm(residual, gain, shift).astype(jnp.bfloat16)
    hidden = project(normed, up_matrix) + up_shift
    active = jax.nn.gelu(hidden, approximate=True).astype(jnp.bfloat16)
    return (
        residual + project(active, down_matrix) + down_shift,
        (residual, normed, hidden, active),
    )


def feed_backward(adjoint, kept, gain, shift, up_matrix, down_matrix):
    residual, normed, hidden, active = kept
    branch = adjoint.astype(jnp.bfloat16)
    down_shift_adjoint = column_total(branch)
    unused, pull = jax.vjp(partial(jax.nn.gelu, approximate=True), hidden)
    hidden_adjoint = pull(project_back(branch, down_matrix))[0].astype(jnp.bfloat16)
    up_shift_adjoint = column_total(hidden_adjoint)
    residual_adjoint, gain_adjoint, shift_adjoint = norm_back(
        residual, gain, shift, project_back(hidden_adjoint, up_matrix)
    )
    pairs = ((normed, hidden_adjoint), (active, branch))
    small = (gain_adjoint, shift_adjoint, up_shift_adjoint, down_shift_adjoint)
    return (adjoint + residual_adjoint, pairs, small)


def per_device(
    tokens,
    images,
    segment_labels,
    image_index,
    cotangent,
    norm_gain,
    vector_bias,
    up_bias,
    self_weight,
    self_out_weight,
    up_weight,
    down_weight,
    query_weight,
    pair_weight,
    cross_out_weight,
):
    groups = lax.axis_size("heads")
    member = lax.axis_index("heads")
    everyone = lax.axis_size(("dp", "heads"))
    length = segment_labels.shape[1]
    position = jnp.arange(length)
    allowed = (segment_labels[:, :, None] == segment_labels[:, None, :]) & (
        position[:, None] >= position[None, :]
    )[None]
    labels = jnp.arange(image_index.shape[1])
    caption_image = jnp.sum(
        jnp.where(segment_labels[:, :, None] == labels[None, None, :], image_index[:, None, :], 0),
        axis=-1,
        dtype=jnp.int32,
    )
    pictures = lax.all_gather(images, "heads", axis=0, tiled=True)
    chosen = caption_image[:, :, None] == jnp.arange(pictures.shape[0])[None, None, :]
    first = (
        lax.all_gather(self_weight[0], ("dp", "heads"), axis=0, tiled=True),
        lax.all_gather(self_out_weight[0], ("dp", "heads"), axis=0, tiled=True),
        lax.all_gather(up_weight[0], ("dp", "heads"), axis=0, tiled=True),
        lax.all_gather(down_weight[0], ("dp", "heads"), axis=0, tiled=True),
        lax.all_gather(norm_gain, ("dp", "heads"), axis=1, tiled=True),
        lax.all_gather(vector_bias, ("dp", "heads"), axis=1, tiled=True),
        lax.all_gather(up_bias, ("dp", "heads"), axis=1, tiled=True),
    )
    gains = first[4].astype(jnp.float32)
    biases = first[5].astype(jnp.float32)
    up_biases = first[6].astype(jnp.float32)
    residual = tokens.astype(jnp.float32)
    residual, kept_self_one = self_forward(
        residual,
        allowed,
        gains[0],
        biases[0],
        first[0],
        biases[5],
        biases[6],
        first[1],
        biases[7],
        groups,
    )
    residual, kept_feed_one = feed_forward(
        residual, gains[1], biases[1], first[2], up_biases[0], first[3], biases[8]
    )
    second = (
        lax.all_gather(self_weight[1], ("dp", "heads"), axis=0, tiled=True),
        lax.all_gather(self_out_weight[1], ("dp", "heads"), axis=0, tiled=True),
        lax.all_gather(up_weight[1], ("dp", "heads"), axis=0, tiled=True),
        lax.all_gather(down_weight[1], ("dp", "heads"), axis=0, tiled=True),
        lax.all_gather(query_weight, ("dp", "heads"), axis=0, tiled=True),
        lax.all_gather(pair_weight, ("dp", "heads"), axis=0, tiled=True),
        lax.all_gather(cross_out_weight, ("dp", "heads"), axis=0, tiled=True),
    )
    residual, kept_self_two = self_forward(
        residual,
        allowed,
        gains[2],
        biases[2],
        second[0],
        biases[9],
        biases[10],
        second[1],
        biases[11],
        groups,
    )
    residual, kept_cross = cross_forward(
        residual,
        pictures,
        chosen,
        gains[3],
        biases[3],
        second[4],
        biases[13],
        second[5],
        biases[14],
        second[6],
        biases[15],
        groups,
        member,
    )
    residual, kept_feed_two = feed_forward(
        residual, gains[4], biases[4], second[2], up_biases[1], second[3], biases[12]
    )
    second = (
        lax.all_gather(self_weight[1], ("dp", "heads"), axis=0, tiled=True),
        lax.all_gather(self_out_weight[1], ("dp", "heads"), axis=0, tiled=True),
        lax.all_gather(up_weight[1], ("dp", "heads"), axis=0, tiled=True),
        lax.all_gather(down_weight[1], ("dp", "heads"), axis=0, tiled=True),
        lax.all_gather(query_weight, ("dp", "heads"), axis=0, tiled=True),
        lax.all_gather(pair_weight, ("dp", "heads"), axis=0, tiled=True),
        lax.all_gather(cross_out_weight, ("dp", "heads"), axis=0, tiled=True),
    )
    adjoint = cotangent.astype(jnp.float32)
    adjoint, feed_two, feed_two_small = feed_backward(
        adjoint, kept_feed_two, gains[4], biases[4], second[2], second[3]
    )
    adjoint, cross_pairs, cross_small, picture_adjoint = cross_backward(
        adjoint,
        kept_cross,
        pictures,
        chosen,
        gains[3],
        biases[3],
        second[4],
        second[5],
        second[6],
        groups,
        member,
    )
    image_gradient = lax.psum_scatter(
        picture_adjoint.astype(jnp.bfloat16), "heads", scatter_dimension=0, tiled=True
    ).astype(jnp.float32)
    adjoint, self_two, self_two_small = self_backward(
        adjoint, kept_self_two, gains[2], biases[2], second[0], second[1], allowed, groups
    )
    first = (
        lax.all_gather(self_weight[0], ("dp", "heads"), axis=0, tiled=True),
        lax.all_gather(self_out_weight[0], ("dp", "heads"), axis=0, tiled=True),
        lax.all_gather(up_weight[0], ("dp", "heads"), axis=0, tiled=True),
        lax.all_gather(down_weight[0], ("dp", "heads"), axis=0, tiled=True),
        lax.all_gather(norm_gain, ("dp", "heads"), axis=1, tiled=True),
    )
    back_gains = first[4].astype(jnp.float32)
    adjoint, feed_one, feed_one_small = feed_backward(
        adjoint, kept_feed_one, back_gains[1], biases[1], first[2], first[3]
    )
    adjoint, self_one, self_one_small = self_backward(
        adjoint, kept_self_one, back_gains[0], biases[0], first[0], first[1], allowed, groups
    )
    width = tokens.shape[2]
    hidden_width = feed_one[0][1].shape[2]
    span = width // groups
    row_pairs = (
        self_one[0],
        self_one[1],
        feed_one[0],
        self_two[0],
        self_two[1],
        feed_two[0],
        cross_pairs[0],
    )
    key_adjoint, value_adjoint = cross_pairs[2]
    blocks = []
    for left, right in row_pairs:
        blocks.append(weight_adjoint(left, right))
    pair_block = jnp.zeros(
        (width // everyone * lax.axis_size(("dp", "heads")), 2 * width), jnp.float32
    )
    pair_block = lax.dynamic_update_slice_in_dim(
        pair_block, weight_adjoint(pictures, key_adjoint), member * span, 1
    )
    pair_block = lax.dynamic_update_slice_in_dim(
        pair_block, weight_adjoint(pictures, value_adjoint), width + member * span, 1
    )
    blocks.append(pair_block)
    left, right = cross_pairs[1]
    blocks.append(weight_adjoint(left, right))
    row_sums = lax.psum_scatter(
        jnp.concatenate(blocks, axis=1), ("dp", "heads"), scatter_dimension=0, tiled=True
    )
    blocks = []
    for left, right in (feed_one[1], feed_two[1]):
        blocks.append(weight_adjoint(left, right))
    down_sums = lax.psum_scatter(
        jnp.concatenate(blocks, axis=1), ("dp", "heads"), scatter_dimension=0, tiled=True
    )
    down_sums = jnp.transpose(down_sums.reshape(down_sums.shape[0], 2, width), (1, 0, 2))
    columns = (
        3 * width,
        width,
        hidden_width,
        3 * width,
        width,
        hidden_width,
        width,
        2 * width,
        width,
    )
    pieces = []
    offset = 0
    for span_width in columns:
        pieces.append(row_sums[:, offset : offset + span_width])
        offset = offset + span_width
    gain_rows = jnp.stack(
        [self_one_small[0], feed_one_small[0], self_two_small[0], cross_small[0], feed_two_small[0]]
    )
    bias_rows = jnp.stack(
        [
            self_one_small[1],
            feed_one_small[1],
            self_two_small[1],
            cross_small[1],
            feed_two_small[1],
            self_one_small[2],
            self_one_small[3],
            self_one_small[4],
            feed_one_small[3],
            self_two_small[2],
            self_two_small[3],
            self_two_small[4],
            feed_two_small[3],
            cross_small[2],
            cross_small[3],
            cross_small[4],
        ]
    )
    up_rows = jnp.stack([feed_one_small[2], feed_two_small[2]])
    small_sums = (
        lax.psum_scatter(gain_rows, ("dp", "heads"), scatter_dimension=1, tiled=True),
        lax.psum_scatter(bias_rows, ("dp", "heads"), scatter_dimension=1, tiled=True),
        lax.psum_scatter(up_rows, ("dp", "heads"), scatter_dimension=1, tiled=True),
    )
    return (
        residual,
        adjoint,
        image_gradient,
        small_sums[0],
        small_sums[1],
        small_sums[2],
        jnp.stack([pieces[0], pieces[3]]),
        jnp.stack([pieces[1], pieces[4]]),
        jnp.stack([pieces[2], pieces[5]]),
        down_sums,
        pieces[6],
        pieces[7],
        pieces[8],
    )


MESH = pl.DeviceIdType.MESH
CHIPS = 16
UNITS = 14
SMALL = UNITS
ROUTES = ("zxy", "zyx", "yxz", "zxy", "zyx", "zxy", "zyx", "yxz", "zxy", "zyx", "zxy", "yxz", "zyx", "zxy", "zxy")
ROUNDS = 6


class Place:
    def __init__(self):
        dp = lax.axis_index("dp")
        self.dp = dp
        self.h = lax.axis_index("heads")
        self.x = lax.rem(dp, 2)
        self.y = lax.rem(dp // 2, 2)
        self.z = dp // 4
        self.to_x = (dp + 1 - 2 * self.x, self.h)
        self.to_y = (dp + 2 - 4 * self.y, self.h)
        self.above = (dp + 4, self.h)
        self.below = (dp - 4, self.h)
        self.sibling = (dp, 1 - self.h)

    def barrier(self, sibling=False):
        bar = pltpu.get_barrier_semaphore()

        def greet(device):
            pl.semaphore_signal(bar, inc=1, device_id=device, device_id_type=MESH)

        greet(self.to_x)
        greet(self.to_y)
        if sibling:
            greet(self.sibling)
        pl.when(self.z < 3)(lambda: greet(self.above))
        pl.when(self.z > 0)(lambda: greet(self.below))
        peers = (3 if sibling else 2) + jnp.where(self.z < 3, 1, 0) + jnp.where(self.z > 0, 1, 0)
        pl.semaphore_wait(bar, peers)


def remote(source, target, send, recv, device):
    return pltpu.make_async_remote_copy(
        src_ref=source,
        dst_ref=target,
        send_sem=send,
        recv_sem=recv,
        device_id=device,
        device_id_type=MESH,
    )


class Gather:
    def __init__(self, at, views, send, recv):
        self.at, self.views, self.send, self.recv = at, views, send, recv

    def hop(self, u, slot, piece, device):
        return remote(piece, piece, self.send.at[u, slot], self.recv.at[u, slot], device)

    def line(self, u, step, piece_of, act):
        at = self.at
        z = at.z
        if act == "send":

            @pl.when((z < 3) & (z >= step - 1))
            def _():
                self.hop(u, step - 1, piece_of(z - (step - 1)), at.above).start()

            @pl.when((z > 0) & (z + step - 1 <= 3))
            def _():
                self.hop(u, step + 2, piece_of(z + (step - 1)), at.below).start()

        elif act == "recv":

            @pl.when(z >= step)
            def _():
                self.hop(u, step - 1, piece_of(z - step), at.below).wait_recv()

            @pl.when(z + step <= 3)
            def _():
                self.hop(u, step + 2, piece_of(z + step), at.above).wait_recv()

        else:

            @pl.when((z < 3) & (z >= step - 1))
            def _():
                self.hop(u, step - 1, piece_of(z - (step - 1)), at.above).wait_send()

            @pl.when((z > 0) & (z + step - 1 <= 3))
            def _():
                self.hop(u, step + 2, piece_of(z + (step - 1)), at.below).wait_send()

    def cross(self, u, axis, first, act):
        at, view = self.at, self.views(u)
        x, y, z = at.x, at.y, at.z
        route = ROUTES[u]
        if route[0] == "z":
            if axis == route[1]:
                mine, its = view.at[:, y, x], (view.at[:, y, 1 - x] if axis == "x" else view.at[:, 1 - y, x])
            elif axis == "x":
                mine, its = view.at[:, :, x], view.at[:, :, 1 - x]
            else:
                mine, its = view.at[:, y], view.at[:, 1 - y]
        elif axis == route[0]:
            mine, its = view.at[z, y, x], (view.at[z, y, 1 - x] if axis == "x" else view.at[z, 1 - y, x])
        elif axis == "x":
            mine, its = view.at[z, :, x], view.at[z, :, 1 - x]
        else:
            mine, its = view.at[z, y], view.at[z, 1 - y]
        slot, device = (6, at.to_x) if axis == "x" else (7, at.to_y)
        if act == "recv":
            self.hop(u, slot, its, device).wait_recv()
        elif act == "send":
            self.hop(u, slot, mine, device).start()
        else:
            self.hop(u, slot, mine, device).wait_send()

    def stages(self, u):
        at, view, route = self.at, self.views(u), ROUTES[u]
        if route[0] == "z":
            along = partial(self.line, u, piece_of=lambda k: view.at[k, at.y, at.x])
            lines = [partial(along, step) for step in (1, 2, 3)]
            return lines + [partial(self.cross, u, route[1], None), partial(self.cross, u, route[2], None)]
        along = partial(self.line, u, piece_of=lambda k: view.at[k])
        lines = [partial(along, step) for step in (1, 2, 3)]
        return [partial(self.cross, u, route[0], None), partial(self.cross, u, route[1], None)] + lines

    def round(self, u, k):
        stages = self.stages(u)
        if k > 0:
            stages[k - 1](act="recv")
        if k < 5:
            stages[k](act="send")

    def drain(self, u):
        for stage in self.stages(u):
            stage(act="sent")


def add_blocks(total, extra, count):
    @pl.loop(0, count)
    def _(i):
        left, right = total(i), extra(i)
        left[...] = (left[...].astype(jnp.float32) + right[...].astype(jnp.float32)).astype(left.dtype)


class Scatter:
    def __init__(self, at, views, spare, outs, send, recv):
        self.at, self.views, self.spare, self.outs, self.send, self.recv = at, views, spare, outs, send, recv

    def hop(self, u, slot, source, target, device):
        return remote(source, target, self.send.at[u, slot], self.recv.at[u, slot], device)

    def line(self, u, step, act):
        at = self.at
        z = at.z
        wide = ROUTES[u][0] != "z"
        view, up, down = self.views(u), self.spare(u, "up"), self.spare(u, "down")

        def piece(k):
            return view.at[k] if wide else view.at[k, at.y, at.x]

        def send_up():
            return self.hop(u, step - 1, piece(z + 4 - step), up.at[step - 1], at.above)

        def send_down():
            return self.hop(u, step + 2, piece(z + step - 4), down.at[step - 1], at.below)

        if act == "send":
            pl.when((z < 3) & (z <= step - 1))(lambda: send_up().start())
            pl.when((z > 0) & (z >= 4 - step))(lambda: send_down().start())
        elif act == "sent":
            pl.when((z < 3) & (z <= step - 1))(lambda: send_up().wait_send())
            pl.when((z > 0) & (z >= 4 - step))(lambda: send_down().wait_send())
        else:
            shape = (2, 2) if wide else (1,)

            def take(k, slots):
                if wide:
                    for i in (0, 1):
                        add_blocks(lambda j: view.at[k, i, j], lambda j: slots.at[step - 1, i, j], 2)
                else:
                    add_blocks(lambda j: view.at[k, at.y, at.x], lambda j: slots.at[step - 1], 1)

            @pl.when((z >= 1) & (z <= step))
            def _():
                self.hop(u, step - 1, piece(z), up.at[step - 1], at.below).wait_recv()
                take(z + 3 - step, up)

            @pl.when((z < 3) & (z >= 3 - step))
            def _():
                self.hop(u, step + 2, piece(z), down.at[step - 1], at.above).wait_recv()
                take(z + step - 3, down)

    def cross(self, u, axis, act):
        at, view, spare = self.at, self.views(u), self.spare(u, axis)
        x, y, z = at.x, at.y, at.z
        route = ROUTES[u]
        slot, device = (6, at.to_x) if axis == "x" else (7, at.to_y)
        if route[0] == "z":
            if axis == route[2]:
                its = view.at[:, :, 1 - x] if axis == "x" else view.at[:, 1 - y]

                def add():
                    for j in (0, 1):
                        if axis == "x":
                            add_blocks(lambda i: view.at[i, j, x], lambda i: spare.at[i, j], 4)
                        else:
                            add_blocks(lambda i: view.at[i, y, j], lambda i: spare.at[i, j], 4)
            else:
                its = view.at[:, y, 1 - x] if axis == "x" else view.at[:, 1 - y, x]

                def add():
                    add_blocks(lambda i: view.at[i, y, x], lambda i: spare.at[i], 4)
        elif axis == route[1]:
            its = view.at[z, :, 1 - x] if axis == "x" else view.at[z, 1 - y]

            def add():
                if axis == "x":
                    add_blocks(lambda i: view.at[z, i, x], lambda i: spare.at[i], 2)
                else:
                    add_blocks(lambda i: view.at[z, y, i], lambda i: spare.at[i], 2)
        else:
            its = view.at[z, y, 1 - x] if axis == "x" else view.at[z, 1 - y, x]

            def add():
                add_blocks(lambda i: view.at[z, y, x], lambda i: spare, 1)

        hop = self.hop(u, slot, its, spare, device)
        if act == "send":
            hop.start()
        elif act == "sent":
            hop.wait_send()
        else:
            hop.wait_recv()
            add()

    def stages(self, u):
        route = ROUTES[u]
        lines = [partial(self.line, u, step) for step in (1, 2, 3)]
        if route[0] == "z":
            return [partial(self.cross, u, route[2]), partial(self.cross, u, route[1])] + lines
        return lines + [partial(self.cross, u, route[1]), partial(self.cross, u, route[0])]

    def round(self, u, k):
        stages = self.stages(u)
        if k > 0:
            stages[k - 1](act="recv")
        if k < 5:
            stages[k](act="send")
        else:
            at = self.at
            out = self.outs(u)
            out[...] = self.views(u)[at.z, at.y, at.x].astype(jnp.float32)

    def drain(self, u):
        for stage in self.stages(u):
            stage(act="sent")


def spare_shapes(rows, width, small):
    narrow = [u for u in range(UNITS) if ROUTES[u][0] == "z"]
    wide = [u for u in range(UNITS) if ROUTES[u][0] != "z"]

    def of(count, tail, kind):
        return [
            pltpu.VMEM((count, 4, 2) + tail, kind),
            pltpu.VMEM((count, 4) + tail, kind),
            pltpu.VMEM((count, 3) + tail, kind),
            pltpu.VMEM((count, 3) + tail, kind),
        ]

    shapes = of(len(narrow), (rows, width), jnp.bfloat16)
    tail = (rows, width)
    shapes += [
        pltpu.VMEM((len(wide), 2) + tail, jnp.bfloat16),
        pltpu.VMEM((len(wide),) + tail, jnp.bfloat16),
        pltpu.VMEM((len(wide), 3, 2, 2) + tail, jnp.bfloat16),
        pltpu.VMEM((len(wide), 3, 2, 2) + tail, jnp.bfloat16),
    ]
    shapes += of(1, (rows, small), jnp.float32)

    def pick(refs):
        def spare(u, what):
            route = ROUTES[u]
            if u == SMALL:
                base, index = 8, 0
            elif route[0] == "z":
                base, index = 0, narrow.index(u)
            else:
                base, index = 4, wide.index(u)
            if what in "xy":
                first = route[2] if route[0] == "z" else route[1]
                slot = 0 if what == first else 1
            else:
                slot = 2 if what == "up" else 3
            return refs[base + slot].at[index]

        return spare

    return shapes, pick


def gather_order():
    events = [(u + 0.7 * k, u, k) for u in range(UNITS + 1) for k in range(ROUNDS)]
    return [(u, k) for key, u, k in sorted(events)]


def gather_kernel(blocks, small, full, full_small, send, recv, local):
    at = Place()
    at.barrier()

    def views(u):
        return full_small if u == SMALL else full.at[u]

    copies = [
        pltpu.make_async_copy(blocks, full.at[:, at.z, at.y, at.x], local.at[0]),
        pltpu.make_async_copy(small, full_small.at[at.z, at.y, at.x], local.at[1]),
    ]
    for copy in copies:
        copy.start()
    for copy in copies:
        copy.wait()
    gather = Gather(at, views, send, recv)
    for u, k in gather_order():
        gather.round(u, k)
    for u in range(UNITS + 1):
        gather.drain(u)


def gather_units(blocks, small):
    units, rows, width = blocks.shape
    return pl.pallas_call(
        gather_kernel,
        out_shape=(
            jax.ShapeDtypeStruct((units, 4, 2, 2, rows, width), blocks.dtype),
            jax.ShapeDtypeStruct((4, 2, 2) + small.shape, small.dtype),
        ),
        in_specs=[pl.BlockSpec(memory_space=pl.ANY)] * 2,
        out_specs=[pl.BlockSpec(memory_space=pl.ANY)] * 2,
        scratch_shapes=[
            pltpu.SemaphoreType.DMA((units + 1, 8)),
            pltpu.SemaphoreType.DMA((units + 1, 8)),
            pltpu.SemaphoreType.DMA((2,)),
        ],
        compiler_params=pltpu.CompilerParams(collective_id=0, has_side_effects=True, vmem_limit_bytes=8 << 20),
    )(blocks, small)


SCATTER_UNITS = (14, 12, 13, 10, 11, 8, 9, 7, 6, 4, 5, 2, 3, 1, 0)


def scatter_kernel(grads, small, out, out_small, total, total_small, *rest, pick, spares):
    at = Place()
    spare = pick(rest[:spares])
    send, recv, local = rest[spares:]
    at.barrier()

    def views(u):
        return total_small if u == SMALL else total.at[u]

    def outs(u):
        return out_small if u == SMALL else out.at[u]

    def load(u):
        if u == SMALL:
            return pltpu.make_async_copy(small, total_small, local.at[u])
        return pltpu.make_async_copy(grads.at[u], total.at[u], local.at[u])

    for u in SCATTER_UNITS:
        load(u).start()
    scatter = Scatter(at, views, spare, outs, send, recv)
    events = [(i + 0.7 * k, u, k) for i, u in enumerate(SCATTER_UNITS) for k in range(ROUNDS)]
    for key, u, k in sorted(events):
        if k == 0:
            load(u).wait()
        scatter.round(u, k)
    for u in SCATTER_UNITS:
        scatter.drain(u)


def scatter_units(grads, small):
    units, rows, width = grads.shape[0], grads.shape[4], grads.shape[5]
    shapes, pick = spare_shapes(rows, width, small.shape[-1])
    return pl.pallas_call(
        partial(scatter_kernel, pick=pick, spares=len(shapes)),
        out_shape=(
            jax.ShapeDtypeStruct((units, rows, width), jnp.float32),
            jax.ShapeDtypeStruct((rows, small.shape[-1]), jnp.float32),
        ),
        in_specs=[pl.BlockSpec(memory_space=pl.ANY)] * 2,
        out_specs=[pl.BlockSpec(memory_space=pltpu.VMEM)] * 2,
        scratch_shapes=[
            pltpu.VMEM(grads.shape, jnp.bfloat16),
            pltpu.VMEM(small.shape, jnp.float32),
            *shapes,
            pltpu.SemaphoreType.DMA((units + 1, 8)),
            pltpu.SemaphoreType.DMA((units + 1, 8)),
            pltpu.SemaphoreType.DMA((units + 1,)),
        ],
        compiler_params=pltpu.CompilerParams(collective_id=1, has_side_effects=True, vmem_limit_bytes=60 << 20),
    )(grads, small)


def swap_cores(value):
    return lax.ppermute(value, "heads", [(0, 1), (1, 0)])


def both_cores(value, member):
    other = swap_cores(value)
    return jnp.stack([jnp.where(member == 0, value, other), jnp.where(member == 0, other, value)])


def core_sum(value):
    value = value.astype(jnp.bfloat16)
    return value.astype(jnp.float32) + swap_cores(value).astype(jnp.float32)


def to_units(member, self_weight, self_out_weight, up_weight, query_weight, pair_weight, cross_out_weight):
    width = self_weight.shape[1 + 1] // 3
    half = width // 2
    rows = self_weight.shape[1]
    own = slice(member * half, member * half + half)
    value = slice(width + member * half, width + member * half + half)
    units = []
    for layer in (0, 1):
        weight = self_weight[layer]
        units.append(jnp.concatenate([weight[:, own], weight[:, value]], axis=1))
        units.append(jnp.concatenate([weight[:, 2 * width + member * half : 2 * width + member * half + half], self_out_weight[layer][:, own]], axis=1))
        up = up_weight[layer].reshape(rows, CHIPS, 2, 2, -1)[:, :, member]
        units.append(up[:, :, 0].reshape(rows, width))
        units.append(up[:, :, 1].reshape(rows, width))
    units.append(jnp.concatenate([query_weight[:, own], cross_out_weight[:, own]], axis=1))
    units.append(jnp.concatenate([pair_weight[:, own], pair_weight[:, value]], axis=1))
    return jnp.stack(units)


UNIT_OF_PIECE = (0, 1, 2, 3, 6, 7, 10, 11, 8, 9)


def chip_blocks(member, pieces, down_weight):
    theirs, ours = (
        jnp.where(member == 0, pieces[1], pieces[0]),
        jnp.where(member == 0, pieces[0], pieces[1]),
    )
    rows = jnp.concatenate(list(both_rows(member, ours, swap_cores(theirs))), axis=1)
    down = down_weight.reshape(2, 2, rows.shape[1], rows.shape[2])
    order = {u: rows[i] for i, u in enumerate(UNIT_OF_PIECE)}
    order.update({4: down[0, 0], 5: down[0, 1], 12: down[1, 0], 13: down[1, 1]})
    return jnp.stack([order[u] for u in range(UNITS)])


def both_rows(member, ours, other):
    return jnp.where(member == 0, ours, other), jnp.where(member == 0, other, ours)


def split_heads(value, rows):
    return value.reshape(rows, value.shape[0] // rows, value.shape[1] // HEAD, HEAD)


def chip_program(
    tokens,
    images,
    segment_labels,
    image_index,
    cotangent,
    norm_gain,
    vector_bias,
    up_bias,
    self_weight,
    self_out_weight,
    up_weight,
    down_weight,
    query_weight,
    pair_weight,
    cross_out_weight,
):
    member = lax.axis_index("heads")
    rows, length, width = tokens.shape
    half = width // 2
    slim = self_weight.shape[1]
    matrices = (self_weight, self_out_weight, up_weight, query_weight, pair_weight, cross_out_weight)
    blocks = chip_blocks(member, [to_units(m, *matrices) for m in (0, 1)], down_weight)
    vectors = jnp.concatenate([norm_gain, vector_bias], axis=0)
    vectors = jnp.concatenate(list(both_cores(vectors, member)), axis=1)
    vectors = jnp.concatenate([vectors, up_bias.reshape(4, 2 * slim)], axis=0)
    small = jnp.pad(vectors, ((0, 128 - vectors.shape[0]), (0, 0))).T
    full, full_small = gather_units(blocks, small)
    full = full.reshape(UNITS, width, width)
    table = full_small.reshape(width, 128).T.astype(jnp.float32)
    gains, biases = table[:5], table[5:21]
    up_biases = [jnp.concatenate([table[21 + 2 * l], table[22 + 2 * l]]) for l in (0, 1)]
    out_halves = jnp.stack([full[1][:, half:], full[7][:, half:], full[8][:, half:]])
    theirs = lax.dynamic_slice_in_dim(out_halves, (1 - member) * half, half, 1)
    ours = lax.dynamic_slice_in_dim(out_halves, member * half, half, 1)
    out_rows = jnp.concatenate(list(both_rows(member, ours, swap_cores(theirs))), axis=2)
    mixes = [jnp.concatenate([full[u], full[u + 1][:, :half]], axis=1) for u in (0, 6)]
    ups = [jnp.concatenate([full[u], full[u + 1]], axis=1) for u in (2, 10)]
    downs = [jnp.concatenate([full[u], full[u + 1]], axis=0) for u in (4, 12)]
    query_matrix = full[8][:, :half]
    pair_matrix = full[9]

    carried = both_cores(jnp.stack([tokens.reshape(-1, width), images.reshape(-1, width), cotangent.reshape(-1, width)]), member)
    carried = carried.transpose(1, 0, 2, 3).reshape(3, -1, width)
    pictures = carried[1]
    chip_rows = segment_labels.shape[0]
    allowed = (segment_labels[:, :, None] == segment_labels[:, None, :]) & (
        jnp.arange(length)[:, None] >= jnp.arange(length)[None, :]
    )[None]
    labels = jnp.arange(image_index.shape[1])
    caption_image = jnp.sum(
        jnp.where(segment_labels[:, :, None] == labels[None, None, :], image_index[:, None, :], 0), axis=-1, dtype=jnp.int32
    )
    shown = 2
    chosen = caption_image[:, :, None] == jnp.arange(shown)[None, None, :]

    def dot(left, right):
        return jnp.dot(left, right, preferred_element_type=jnp.float32)

    def dot_back(left, right):
        return lax.dot_general(left, right, (((1,), (1,)), ((), ())), preferred_element_type=jnp.float32)

    def dot_rows(left, right):
        return lax.dot_general(left, right, (((0,), (0,)), ((), ())), preferred_element_type=jnp.float32)

    def own_half(vector):
        return lax.dynamic_slice_in_dim(vector, member * half, half, 0)

    def attend(residual, l, gain, shift, query_bias, value_bias, out_bias, out_weight):
        normed = layer_norm(residual, gain, shift).astype(jnp.bfloat16)
        offset = jnp.concatenate([own_half(query_bias), jnp.zeros((half,), jnp.float32), own_half(value_bias)])
        mixed = (dot(normed, mixes[l]) + offset).astype(jnp.bfloat16)
        queries, keys, values = [split_heads(mixed[:, i * half : (i + 1) * half], chip_rows) for i in range(3)]
        attended, log_total = self_heads_forward(queries, keys, values, allowed)
        attended = attended.reshape(-1, half)
        return residual + core_sum(dot(attended, out_weight)) + out_bias, (residual, normed, queries, keys, values, log_total, attended)

    def feed(residual, l, gain, shift, bias):
        normed = layer_norm(residual, gain, shift).astype(jnp.bfloat16)
        hidden = dot(normed, ups[l]) + up_biases[l]
        active = jax.nn.gelu(hidden, approximate=True).astype(jnp.bfloat16)
        return residual + core_sum(dot(active, downs[l])) + bias, (residual, normed, hidden, active)

    residual = carried[0].astype(jnp.float32)
    residual, kept_self_one = attend(residual, 0, gains[0], biases[0], biases[5], biases[6], biases[7], out_rows[0])
    residual, kept_feed_one = feed(residual, 0, gains[1], biases[1], biases[8])
    residual, kept_self_two = attend(residual, 1, gains[2], biases[2], biases[9], biases[10], biases[11], out_rows[1])
    pair_offset = jnp.concatenate([jnp.zeros((half,), jnp.float32), own_half(biases[14])])
    pair = (dot(pictures, pair_matrix) + pair_offset).astype(jnp.bfloat16)
    image_keys, image_values = split_heads(pair[:, :half], shown), split_heads(pair[:, half:], shown)
    normed_cross = layer_norm(residual, gains[3], biases[3]).astype(jnp.bfloat16)
    queries_cross = split_heads((dot(normed_cross, query_matrix) + own_half(biases[13])).astype(jnp.bfloat16), chip_rows)
    attended, log_cross = cross_heads_forward(queries_cross, image_keys, image_values, chosen)
    attended_cross = attended.reshape(-1, half)
    residual_cross = residual
    residual = residual + core_sum(dot(attended_cross, out_rows[2])) + biases[15]
    residual, kept_feed_two = feed(residual, 1, gains[4], biases[4], biases[12])
    layer_out = residual

    grads = [None] * UNITS
    small_rows = [None] * 25
    zero = jnp.zeros((width,), jnp.float32)

    def place_half(vector):
        return lax.dynamic_update_slice_in_dim(zero, vector, member * half, 0)

    def total(value):
        return jnp.sum(value, axis=0, dtype=jnp.float32)

    def feed_back(adjoint, l, n, bias, kept):
        residual, normed, hidden, active = kept
        branch = adjoint.astype(jnp.bfloat16)
        small_rows[5 + bias] = total(branch)
        unused, pull = jax.vjp(partial(jax.nn.gelu, approximate=True), hidden)
        hidden_adjoint = pull(dot_back(branch, downs[l]))[0].astype(jnp.bfloat16)
        sums = total(hidden_adjoint)
        small_rows[21 + 2 * l], small_rows[22 + 2 * l] = sums[:width], sums[width:]
        up = dot_rows(normed, hidden_adjoint).astype(jnp.bfloat16)
        down = dot_rows(active, branch).astype(jnp.bfloat16)
        base = 2 if l == 0 else 10
        grads[base], grads[base + 1] = up[:, :width], up[:, width:]
        grads[base + 2], grads[base + 3] = down[:width], down[width:]
        back, small_rows[n], small_rows[5 + n] = norm_back(residual, gains[n], biases[n], core_sum(dot_back(hidden_adjoint, ups[l])))
        return adjoint + back

    def out_halves_back(attended, branch):
        gradient = dot_rows(attended, branch).astype(jnp.bfloat16)
        ours = lax.dynamic_slice_in_dim(gradient, member * half, half, 1)
        theirs = lax.dynamic_slice_in_dim(gradient, (1 - member) * half, half, 1)
        return jnp.concatenate(list(both_rows(member, ours, swap_cores(theirs))), axis=0)

    def attend_back(adjoint, l, n, query_bias, value_bias, out_bias, kept):
        residual, normed, queries, keys, values, log_total, attended = kept
        branch = adjoint.astype(jnp.bfloat16)
        small_rows[5 + out_bias] = total(branch)
        head_adjoint = split_heads(dot_back(branch, out_rows[l]).astype(jnp.bfloat16), chip_rows)
        parts = self_heads_back(queries, keys, values, allowed, log_total, head_adjoint)
        mixed = jnp.concatenate([part.reshape(-1, half) for part in parts], axis=1)
        sums = total(mixed)
        small_rows[5 + query_bias], small_rows[5 + value_bias] = place_half(sums[:half]), place_half(sums[2 * half :])
        gradient = dot_rows(normed, mixed).astype(jnp.bfloat16)
        base = 0 if l == 0 else 6
        grads[base] = gradient[:, :width]
        grads[base + 1] = jnp.concatenate([gradient[:, width:], out_halves_back(attended, branch)], axis=1)
        back, small_rows[n], small_rows[5 + n] = norm_back(residual, gains[n], biases[n], core_sum(dot_back(mixed, mixes[l])))
        return adjoint + back

    adjoint = carried[2].astype(jnp.float32)
    adjoint = feed_back(adjoint, 1, 4, 12, kept_feed_two)
    branch = adjoint.astype(jnp.bfloat16)
    small_rows[5 + 15] = total(branch)
    head_adjoint = split_heads(dot_back(branch, out_rows[2]).astype(jnp.bfloat16), chip_rows)
    query_adjoint, key_adjoint, value_adjoint = cross_heads_back(
        queries_cross, image_keys, image_values, chosen, log_cross, head_adjoint
    )
    query_adjoint = query_adjoint.reshape(-1, half)
    pair_adjoint = jnp.concatenate([key_adjoint.reshape(-1, half), value_adjoint.reshape(-1, half)], axis=1)
    small_rows[5 + 13] = place_half(total(query_adjoint))
    small_rows[5 + 14] = place_half(total(pair_adjoint[:, half:]))
    grads[8] = jnp.concatenate([dot_rows(normed_cross, query_adjoint).astype(jnp.bfloat16), out_halves_back(attended_cross, branch)], axis=1)
    grads[9] = dot_rows(pictures, pair_adjoint).astype(jnp.bfloat16)
    picture_adjoint = dot_back(pair_adjoint, pair_matrix).astype(jnp.bfloat16).reshape(2, -1, width)
    image_gradient = picture_adjoint[member].astype(jnp.float32) + swap_cores(picture_adjoint[1 - member]).astype(jnp.float32)
    back, small_rows[3], small_rows[5 + 3] = norm_back(
        residual_cross, gains[3], biases[3], core_sum(dot_back(query_adjoint, query_matrix))
    )
    adjoint = adjoint + back
    adjoint = attend_back(adjoint, 1, 2, 9, 10, 11, kept_self_two)
    adjoint = feed_back(adjoint, 0, 1, 8, kept_feed_one)
    adjoint = attend_back(adjoint, 0, 0, 5, 6, 7, kept_self_one)

    stacked = jnp.stack(grads).reshape(UNITS, 4, 2, 2, 2 * slim, width)
    vectors = jnp.pad(jnp.stack(small_rows), ((0, 128 - 25), (0, 0))).T.reshape(4, 2, 2, 2 * slim, 128)
    sums, small_sums = scatter_units(stacked, vectors)
    outs = finish(member, sums, small_sums, slim, width)
    mine = (layer_out.reshape(2, rows, length, width)[member], adjoint.reshape(2, rows, length, width)[member])
    return mine + (image_gradient[None],) + outs


def finish(member, sums, small_sums, slim, width):
    half = width // 2
    pieces = jnp.stack([sums[u] for u in UNIT_OF_PIECE]).reshape(len(UNIT_OF_PIECE), 2, slim, width)
    ours, theirs = pieces[:, member], pieces[:, 1 - member]
    both = jnp.stack(list(both_rows(member, ours, swap_cores(theirs))))

    def halves(piece, side):
        return jnp.concatenate([both[0, piece][:, side * half : (side + 1) * half], both[1, piece][:, side * half : (side + 1) * half]], axis=1)

    def up(piece):
        parts = [both[:, piece + s].reshape(2, slim, CHIPS, 2 * slim) for s in (0, 1)]
        return jnp.stack(parts, axis=0).transpose(2, 3, 1, 0, 4).reshape(slim, 4 * width)

    self_weight = jnp.stack([jnp.concatenate([halves(p, 0), halves(p, 1), halves(p + 1, 0)], axis=1) for p in (0, 4)])
    self_out = jnp.stack([halves(p, 1) for p in (1, 5)])
    up_gradient = jnp.stack([up(2), up(6)])
    down = jnp.stack([jnp.concatenate([sums[u], sums[u + 1]]) for u in (4, 12)])
    pair = jnp.concatenate([halves(9, 0), halves(9, 1)], axis=1)
    table = small_sums.T
    shared = table[:21]
    other = swap_cores(shared)
    split = jnp.zeros((21, 1), bool).at[jnp.array([5 + n for n in (5, 6, 9, 10, 13, 14)])].set(True)
    shared = jnp.where(split, shared + other, shared)
    shared = lax.dynamic_slice_in_dim(shared, member * slim, slim, 1)
    up_bias = table[21:25].reshape(2, 4 * slim)
    return (shared[:5], shared[5:], up_bias, self_weight, self_out, up_gradient, down, halves(8, 0), pair, halves(8, 1))


def solution(mesh):
    in_specs = (
        P(("dp", "heads"), None, None),
        P(("dp", "heads"), None, None),
        P("dp", None),
        P("dp", None),
        P(("dp", "heads"), None, None),
        P(None, ("dp", "heads")),
        P(None, ("dp", "heads")),
        P(None, ("dp", "heads")),
        P(None, ("dp", "heads"), None),
        P(None, ("dp", "heads"), None),
        P(None, ("dp", "heads"), None),
        P(None, ("dp", "heads"), None),
        P(("dp", "heads"), None),
        P(("dp", "heads"), None),
        P(("dp", "heads"), None),
    )
    out_specs = (
        P(("dp", "heads"), None, None),
        P(("dp", "heads"), None, None),
        P(("dp", "heads"), None, None),
        P(None, ("dp", "heads")),
        P(None, ("dp", "heads")),
        P(None, ("dp", "heads")),
        P(None, ("dp", "heads"), None),
        P(None, ("dp", "heads"), None),
        P(None, ("dp", "heads"), None),
        P(None, ("dp", "heads"), None),
        P(("dp", "heads"), None),
        P(("dp", "heads"), None),
        P(("dp", "heads"), None),
    )
    dp, cores = mesh.shape["dp"], mesh.shape["heads"]
    program = chip_program if (dp, cores) == (CHIPS, 2) else per_device
    return jax.shard_map(
        program, mesh=mesh, in_specs=in_specs, out_specs=out_specs, check_vma=False
    )
```

```python
from functools import partial
import math
from typing import Any, NamedTuple

import jax
import jax.numpy as jnp
from jax import lax
from jax.experimental import pallas as pl
from jax.experimental.pallas import tpu as pltpu
from jax.sharding import PartitionSpec as P

HEADS = 12
HEAD = 64


masked_score = -1e30


def layer_norm(residual, gain, shift):
    center = residual - jnp.mean(residual, axis=-1, keepdims=True)
    variance = jnp.mean(center * center, axis=-1, keepdims=True)
    return center * lax.rsqrt(variance + 1e-05) * gain + shift


def project(left, weight):
    return jnp.einsum("rld,de->rle", left, weight, preferred_element_type=jnp.float32)


def weight_adjoint(left, adjoint):
    return jnp.einsum("rld,rle->de", left, adjoint, preferred_element_type=jnp.float32)


def project_back(adjoint, weight):
    return jnp.einsum("rle,de->rld", adjoint, weight, preferred_element_type=jnp.float32)


def column_total(adjoint):
    return jnp.sum(adjoint, axis=(0, 1), dtype=jnp.float32)


def norm_back(residual, gain, shift, adjoint):
    unused, pull = jax.vjp(layer_norm, residual, gain, shift)
    return pull(adjoint)


def rows_to_heads(pieces):
    return lax.all_to_all(pieces, "heads", split_axis=3, concat_axis=0, tiled=True)


def heads_to_rows(pieces):
    return lax.all_to_all(pieces, "heads", split_axis=0, concat_axis=3, tiled=True)


def adjoint_to_heads(pieces):
    return lax.all_to_all(pieces, "heads", split_axis=3, concat_axis=0, tiled=True)


def adjoint_to_rows(pieces):
    return lax.all_to_all(pieces, "heads", split_axis=0, concat_axis=3, tiled=True)


def softmax_parts(scores):
    peak = jnp.max(scores, axis=-1, keepdims=True)
    log_total = peak + jnp.log(jnp.sum(jnp.exp(scores - peak), axis=-1, keepdims=True))
    return (jnp.exp(scores - log_total), log_total)


def softmax_back(shares, adjoint):
    return (shares * (adjoint - jnp.sum(shares * adjoint, axis=-1, keepdims=True))).astype(
        jnp.bfloat16
    )


def self_scores(queries, keys, allowed):
    scores = jnp.einsum(
        "rqhd,rkhd->rhqk", queries, keys, preferred_element_type=jnp.float32
    ) * HEAD ** (-0.5)
    return jnp.where(allowed[:, None], scores, masked_score)


def self_heads_forward(queries, keys, values, allowed):
    shares, log_total = softmax_parts(self_scores(queries, keys, allowed))
    attended = jnp.einsum(
        "rhqk,rkhd->rqhd", shares.astype(jnp.bfloat16), values, preferred_element_type=jnp.float32
    )
    return (attended.astype(jnp.bfloat16), log_total)


def self_heads_back(queries, keys, values, allowed, log_total, adjoint):
    shares = jnp.exp(self_scores(queries, keys, allowed) - log_total)
    value_adjoint = jnp.einsum(
        "rhqk,rqhd->rkhd", shares.astype(jnp.bfloat16), adjoint, preferred_element_type=jnp.float32
    )
    share_adjoint = jnp.einsum(
        "rqhd,rkhd->rhqk", adjoint, values, preferred_element_type=jnp.float32
    )
    score_adjoint = softmax_back(shares, share_adjoint)
    scale = HEAD ** (-0.5)
    query_adjoint = (
        jnp.einsum("rhqk,rkhd->rqhd", score_adjoint, keys, preferred_element_type=jnp.float32)
        * scale
    )
    key_adjoint = (
        jnp.einsum("rhqk,rqhd->rkhd", score_adjoint, queries, preferred_element_type=jnp.float32)
        * scale
    )
    return (
        query_adjoint.astype(jnp.bfloat16),
        key_adjoint.astype(jnp.bfloat16),
        value_adjoint.astype(jnp.bfloat16),
    )


def cross_scores(queries, image_keys, chosen):
    rows, length, heads, head_size = queries.shape
    scores = jnp.einsum(
        "rqhd,gkhd->rhqgk", queries, image_keys, preferred_element_type=jnp.float32
    ) * HEAD ** (-0.5)
    scores = jnp.where(chosen[:, None, :, :, None], scores, masked_score)
    return scores.reshape(rows, heads, length, -1)


def block_rows(rows, length):
    return math.gcd(rows, max(1, 512 // length))


def cross_heads_forward(queries, image_keys, image_values, chosen):
    rows, length, heads, head_size = queries.shape
    block = block_rows(rows, length)
    flat_values = image_values.reshape(-1, heads, head_size)

    def one_block(inputs):
        block_queries, block_chosen = inputs
        shares, log_total = softmax_parts(cross_scores(block_queries, image_keys, block_chosen))
        attended = jnp.einsum(
            "rhqc,chd->rqhd",
            shares.astype(jnp.bfloat16),
            flat_values,
            preferred_element_type=jnp.float32,
        )
        return (attended.astype(jnp.bfloat16), log_total)

    blocked = (
        queries.reshape(rows // block, block, length, heads, head_size),
        chosen.reshape(rows // block, block, length, -1),
    )
    attended, log_total = lax.map(one_block, blocked)
    return (attended.reshape(queries.shape), log_total)


def cross_heads_back(queries, image_keys, image_values, chosen, log_total, adjoint):
    rows, length, heads, head_size = queries.shape
    block = block_rows(rows, length)
    flat_keys = image_keys.reshape(-1, heads, head_size)
    flat_values = image_values.reshape(-1, heads, head_size)
    scale = HEAD ** (-0.5)

    def one_block(carry, inputs):
        key_total, value_total = carry
        block_queries, block_chosen, block_log, block_adjoint = inputs
        shares = jnp.exp(cross_scores(block_queries, image_keys, block_chosen) - block_log)
        value_total = value_total + jnp.einsum(
            "rhqc,rqhd->chd",
            shares.astype(jnp.bfloat16),
            block_adjoint,
            preferred_element_type=jnp.float32,
        )
        share_adjoint = jnp.einsum(
            "rqhd,chd->rhqc", block_adjoint, flat_values, preferred_element_type=jnp.float32
        )
        score_adjoint = softmax_back(shares, share_adjoint)
        key_total = (
            key_total
            + jnp.einsum(
                "rhqc,rqhd->chd", score_adjoint, block_queries, preferred_element_type=jnp.float32
            )
            * scale
        )
        query_adjoint = (
            jnp.einsum(
                "rhqc,chd->rqhd", score_adjoint, flat_keys, preferred_element_type=jnp.float32
            )
            * scale
        )
        return ((key_total, value_total), query_adjoint.astype(jnp.bfloat16))

    start = jnp.zeros(flat_keys.shape, jnp.float32)
    blocked = (
        queries.reshape(rows // block, block, length, heads, head_size),
        chosen.reshape(rows // block, block, length, -1),
        log_total,
        adjoint.reshape(rows // block, block, length, heads, head_size),
    )
    (key_total, value_total), query_adjoint = lax.scan(one_block, (start, start), blocked)
    return (
        query_adjoint.reshape(queries.shape),
        key_total.astype(jnp.bfloat16),
        value_total.astype(jnp.bfloat16),
    )


def self_forward(
    residual, allowed, gain, shift, weight, query_bias, value_bias, out_weight, out_bias, groups
):
    rows, length, width = residual.shape
    span = width // groups
    normed = layer_norm(residual, gain, shift).astype(jnp.bfloat16)
    offset = jnp.concatenate([query_bias, jnp.zeros_like(query_bias), value_bias])
    mixed = (project(normed, weight) + offset).astype(jnp.bfloat16)
    gathered = rows_to_heads(mixed.reshape(rows, length, 3, groups, span))
    gathered = gathered.reshape(rows * groups, length, 3, HEADS // groups, HEAD)
    queries, keys, values = (gathered[:, :, 0], gathered[:, :, 1], gathered[:, :, 2])
    attended, log_total = self_heads_forward(queries, keys, values, allowed)
    merged = heads_to_rows(attended.reshape(rows * groups, length, 1, 1, span)).reshape(
        rows, length, width
    )
    kept = (residual, normed, queries, keys, values, log_total, merged)
    return (residual + project(merged, out_weight) + out_bias, kept)


def self_backward(adjoint, kept, gain, shift, weight, out_weight, allowed, groups):
    residual, normed, queries, keys, values, log_total, merged = kept
    rows, length, width = residual.shape
    span = width // groups
    branch = adjoint.astype(jnp.bfloat16)
    out_bias_adjoint = column_total(branch)
    merged_adjoint = project_back(branch, out_weight).astype(jnp.bfloat16)
    head_adjoint = adjoint_to_heads(merged_adjoint.reshape(rows, length, 1, groups, span))
    head_adjoint = head_adjoint.reshape(rows * groups, length, HEADS // groups, HEAD)
    query_adjoint, key_adjoint, value_adjoint = self_heads_back(
        queries, keys, values, allowed, log_total, head_adjoint
    )
    stacked = jnp.stack([query_adjoint, key_adjoint, value_adjoint], axis=2).reshape(
        rows * groups, length, 3, 1, span
    )
    mixed_adjoint = adjoint_to_rows(stacked).reshape(rows, length, 3 * width)
    offset_adjoint = column_total(mixed_adjoint)
    residual_adjoint, gain_adjoint, shift_adjoint = norm_back(
        residual, gain, shift, project_back(mixed_adjoint, weight)
    )
    pairs = ((normed, mixed_adjoint), (merged, branch))
    small = (
        gain_adjoint,
        shift_adjoint,
        offset_adjoint[:width],
        offset_adjoint[2 * width :],
        out_bias_adjoint,
    )
    return (adjoint + residual_adjoint, pairs, small)


def cross_forward(
    residual,
    pictures,
    chosen,
    gain,
    shift,
    weight,
    query_bias,
    pair_matrix,
    value_bias,
    out_weight,
    out_bias,
    groups,
    member,
):
    rows, length, width = residual.shape
    span = width // groups
    key_weight = lax.dynamic_slice_in_dim(pair_matrix, member * span, span, 1)
    value_weight = lax.dynamic_slice_in_dim(pair_matrix, width + member * span, span, 1)
    value_shift = lax.dynamic_slice_in_dim(value_bias, member * span, span, 0)
    layout = (pictures.shape[0], pictures.shape[1], HEADS // groups, HEAD)
    image_keys = project(pictures, key_weight).astype(jnp.bfloat16).reshape(layout)
    image_values = (
        (project(pictures, value_weight) + value_shift).astype(jnp.bfloat16).reshape(layout)
    )
    normed = layer_norm(residual, gain, shift).astype(jnp.bfloat16)
    query_rows = (project(normed, weight) + query_bias).astype(jnp.bfloat16)
    queries = rows_to_heads(query_rows.reshape(rows, length, 1, groups, span))
    queries = queries.reshape(rows * groups, length, HEADS // groups, HEAD)
    attended, log_total = cross_heads_forward(queries, image_keys, image_values, chosen)
    merged = heads_to_rows(attended.reshape(rows * groups, length, 1, 1, span)).reshape(
        rows, length, width
    )
    kept = (residual, normed, queries, image_keys, image_values, log_total, merged)
    return (residual + project(merged, out_weight) + out_bias, kept)


def cross_backward(
    adjoint, kept, pictures, chosen, gain, shift, weight, pair_matrix, out_weight, groups, member
):
    residual, normed, queries, image_keys, image_values, log_total, merged = kept
    rows, length, width = residual.shape
    span = width // groups
    key_weight = lax.dynamic_slice_in_dim(pair_matrix, member * span, span, 1)
    value_weight = lax.dynamic_slice_in_dim(pair_matrix, width + member * span, span, 1)
    branch = adjoint.astype(jnp.bfloat16)
    out_bias_adjoint = column_total(branch)
    merged_adjoint = project_back(branch, out_weight).astype(jnp.bfloat16)
    head_adjoint = adjoint_to_heads(merged_adjoint.reshape(rows, length, 1, groups, span))
    head_adjoint = head_adjoint.reshape(rows * groups, length, HEADS // groups, HEAD)
    query_adjoint, key_adjoint, value_adjoint = cross_heads_back(
        queries, image_keys, image_values, chosen, log_total, head_adjoint
    )
    query_rows = adjoint_to_rows(query_adjoint.reshape(rows * groups, length, 1, 1, span)).reshape(
        rows, length, width
    )
    query_bias_adjoint = column_total(query_rows)
    residual_adjoint, gain_adjoint, shift_adjoint = norm_back(
        residual, gain, shift, project_back(query_rows, weight)
    )
    layout = (pictures.shape[0], pictures.shape[1], span)
    key_adjoint = key_adjoint.reshape(layout)
    value_adjoint = value_adjoint.reshape(layout)
    value_bias_adjoint = lax.dynamic_update_slice_in_dim(
        jnp.zeros((width,), jnp.float32), column_total(value_adjoint), member * span, 0
    )
    picture_adjoint = project_back(key_adjoint, key_weight) + project_back(
        value_adjoint, value_weight
    )
    pairs = ((normed, query_rows), (merged, branch), (key_adjoint, value_adjoint))
    small = (gain_adjoint, shift_adjoint, query_bias_adjoint, value_bias_adjoint, out_bias_adjoint)
    return (adjoint + residual_adjoint, pairs, small, picture_adjoint)


def feed_forward(residual, gain, shift, up_matrix, up_shift, down_matrix, down_shift):
    normed = layer_norm(residual, gain, shift).astype(jnp.bfloat16)
    hidden = project(normed, up_matrix) + up_shift
    active = jax.nn.gelu(hidden, approximate=True).astype(jnp.bfloat16)
    return (
        residual + project(active, down_matrix) + down_shift,
        (residual, normed, hidden, active),
    )


def feed_backward(adjoint, kept, gain, shift, up_matrix, down_matrix):
    residual, normed, hidden, active = kept
    branch = adjoint.astype(jnp.bfloat16)
    down_shift_adjoint = column_total(branch)
    unused, pull = jax.vjp(partial(jax.nn.gelu, approximate=True), hidden)
    hidden_adjoint = pull(project_back(branch, down_matrix))[0].astype(jnp.bfloat16)
    up_shift_adjoint = column_total(hidden_adjoint)
    residual_adjoint, gain_adjoint, shift_adjoint = norm_back(
        residual, gain, shift, project_back(hidden_adjoint, up_matrix)
    )
    pairs = ((normed, hidden_adjoint), (active, branch))
    small = (gain_adjoint, shift_adjoint, up_shift_adjoint, down_shift_adjoint)
    return (adjoint + residual_adjoint, pairs, small)


def per_device(
    tokens,
    images,
    segment_labels,
    image_index,
    cotangent,
    norm_gain,
    vector_bias,
    up_bias,
    self_weight,
    self_out_weight,
    up_weight,
    down_weight,
    query_weight,
    pair_weight,
    cross_out_weight,
):
    groups = lax.axis_size("heads")
    member = lax.axis_index("heads")
    everyone = lax.axis_size(("dp", "heads"))
    length = segment_labels.shape[1]
    position = jnp.arange(length)
    allowed = (segment_labels[:, :, None] == segment_labels[:, None, :]) & (
        position[:, None] >= position[None, :]
    )[None]
    labels = jnp.arange(image_index.shape[1])
    caption_image = jnp.sum(
        jnp.where(segment_labels[:, :, None] == labels[None, None, :], image_index[:, None, :], 0),
        axis=-1,
        dtype=jnp.int32,
    )
    pictures = lax.all_gather(images, "heads", axis=0, tiled=True)
    chosen = caption_image[:, :, None] == jnp.arange(pictures.shape[0])[None, None, :]
    first = (
        lax.all_gather(self_weight[0], ("dp", "heads"), axis=0, tiled=True),
        lax.all_gather(self_out_weight[0], ("dp", "heads"), axis=0, tiled=True),
        lax.all_gather(up_weight[0], ("dp", "heads"), axis=0, tiled=True),
        lax.all_gather(down_weight[0], ("dp", "heads"), axis=0, tiled=True),
        lax.all_gather(norm_gain, ("dp", "heads"), axis=1, tiled=True),
        lax.all_gather(vector_bias, ("dp", "heads"), axis=1, tiled=True),
        lax.all_gather(up_bias, ("dp", "heads"), axis=1, tiled=True),
    )
    gains = first[4].astype(jnp.float32)
    biases = first[5].astype(jnp.float32)
    up_biases = first[6].astype(jnp.float32)
    residual = tokens.astype(jnp.float32)
    residual, kept_self_one = self_forward(
        residual,
        allowed,
        gains[0],
        biases[0],
        first[0],
        biases[5],
        biases[6],
        first[1],
        biases[7],
        groups,
    )
    residual, kept_feed_one = feed_forward(
        residual, gains[1], biases[1], first[2], up_biases[0], first[3], biases[8]
    )
    second = (
        lax.all_gather(self_weight[1], ("dp", "heads"), axis=0, tiled=True),
        lax.all_gather(self_out_weight[1], ("dp", "heads"), axis=0, tiled=True),
        lax.all_gather(up_weight[1], ("dp", "heads"), axis=0, tiled=True),
        lax.all_gather(down_weight[1], ("dp", "heads"), axis=0, tiled=True),
        lax.all_gather(query_weight, ("dp", "heads"), axis=0, tiled=True),
        lax.all_gather(pair_weight, ("dp", "heads"), axis=0, tiled=True),
        lax.all_gather(cross_out_weight, ("dp", "heads"), axis=0, tiled=True),
    )
    residual, kept_self_two = self_forward(
        residual,
        allowed,
        gains[2],
        biases[2],
        second[0],
        biases[9],
        biases[10],
        second[1],
        biases[11],
        groups,
    )
    residual, kept_cross = cross_forward(
        residual,
        pictures,
        chosen,
        gains[3],
        biases[3],
        second[4],
        biases[13],
        second[5],
        biases[14],
        second[6],
        biases[15],
        groups,
        member,
    )
    residual, kept_feed_two = feed_forward(
        residual, gains[4], biases[4], second[2], up_biases[1], second[3], biases[12]
    )
    second = (
        lax.all_gather(self_weight[1], ("dp", "heads"), axis=0, tiled=True),
        lax.all_gather(self_out_weight[1], ("dp", "heads"), axis=0, tiled=True),
        lax.all_gather(up_weight[1], ("dp", "heads"), axis=0, tiled=True),
        lax.all_gather(down_weight[1], ("dp", "heads"), axis=0, tiled=True),
        lax.all_gather(query_weight, ("dp", "heads"), axis=0, tiled=True),
        lax.all_gather(pair_weight, ("dp", "heads"), axis=0, tiled=True),
        lax.all_gather(cross_out_weight, ("dp", "heads"), axis=0, tiled=True),
    )
    adjoint = cotangent.astype(jnp.float32)
    adjoint, feed_two, feed_two_small = feed_backward(
        adjoint, kept_feed_two, gains[4], biases[4], second[2], second[3]
    )
    adjoint, cross_pairs, cross_small, picture_adjoint = cross_backward(
        adjoint,
        kept_cross,
        pictures,
        chosen,
        gains[3],
        biases[3],
        second[4],
        second[5],
        second[6],
        groups,
        member,
    )
    image_gradient = lax.psum_scatter(
        picture_adjoint.astype(jnp.bfloat16), "heads", scatter_dimension=0, tiled=True
    ).astype(jnp.float32)
    adjoint, self_two, self_two_small = self_backward(
        adjoint, kept_self_two, gains[2], biases[2], second[0], second[1], allowed, groups
    )
    first = (
        lax.all_gather(self_weight[0], ("dp", "heads"), axis=0, tiled=True),
        lax.all_gather(self_out_weight[0], ("dp", "heads"), axis=0, tiled=True),
        lax.all_gather(up_weight[0], ("dp", "heads"), axis=0, tiled=True),
        lax.all_gather(down_weight[0], ("dp", "heads"), axis=0, tiled=True),
        lax.all_gather(norm_gain, ("dp", "heads"), axis=1, tiled=True),
    )
    back_gains = first[4].astype(jnp.float32)
    adjoint, feed_one, feed_one_small = feed_backward(
        adjoint, kept_feed_one, back_gains[1], biases[1], first[2], first[3]
    )
    adjoint, self_one, self_one_small = self_backward(
        adjoint, kept_self_one, back_gains[0], biases[0], first[0], first[1], allowed, groups
    )
    width = tokens.shape[2]
    hidden_width = feed_one[0][1].shape[2]
    span = width // groups
    row_pairs = (
        self_one[0],
        self_one[1],
        feed_one[0],
        self_two[0],
        self_two[1],
        feed_two[0],
        cross_pairs[0],
    )
    key_adjoint, value_adjoint = cross_pairs[2]
    blocks = []
    for left, right in row_pairs:
        blocks.append(weight_adjoint(left, right))
    pair_block = jnp.zeros(
        (width // everyone * lax.axis_size(("dp", "heads")), 2 * width), jnp.float32
    )
    pair_block = lax.dynamic_update_slice_in_dim(
        pair_block, weight_adjoint(pictures, key_adjoint), member * span, 1
    )
    pair_block = lax.dynamic_update_slice_in_dim(
        pair_block, weight_adjoint(pictures, value_adjoint), width + member * span, 1
    )
    blocks.append(pair_block)
    left, right = cross_pairs[1]
    blocks.append(weight_adjoint(left, right))
    row_sums = lax.psum_scatter(
        jnp.concatenate(blocks, axis=1), ("dp", "heads"), scatter_dimension=0, tiled=True
    )
    blocks = []
    for left, right in (feed_one[1], feed_two[1]):
        blocks.append(weight_adjoint(left, right))
    down_sums = lax.psum_scatter(
        jnp.concatenate(blocks, axis=1), ("dp", "heads"), scatter_dimension=0, tiled=True
    )
    down_sums = jnp.transpose(down_sums.reshape(down_sums.shape[0], 2, width), (1, 0, 2))
    columns = (
        3 * width,
        width,
        hidden_width,
        3 * width,
        width,
        hidden_width,
        width,
        2 * width,
        width,
    )
    pieces = []
    offset = 0
    for span_width in columns:
        pieces.append(row_sums[:, offset : offset + span_width])
        offset = offset + span_width
    gain_rows = jnp.stack(
        [self_one_small[0], feed_one_small[0], self_two_small[0], cross_small[0], feed_two_small[0]]
    )
    bias_rows = jnp.stack(
        [
            self_one_small[1],
            feed_one_small[1],
            self_two_small[1],
            cross_small[1],
            feed_two_small[1],
            self_one_small[2],
            self_one_small[3],
            self_one_small[4],
            feed_one_small[3],
            self_two_small[2],
            self_two_small[3],
            self_two_small[4],
            feed_two_small[3],
            cross_small[2],
            cross_small[3],
            cross_small[4],
        ]
    )
    up_rows = jnp.stack([feed_one_small[2], feed_two_small[2]])
    small_sums = (
        lax.psum_scatter(gain_rows, ("dp", "heads"), scatter_dimension=1, tiled=True),
        lax.psum_scatter(bias_rows, ("dp", "heads"), scatter_dimension=1, tiled=True),
        lax.psum_scatter(up_rows, ("dp", "heads"), scatter_dimension=1, tiled=True),
    )
    return (
        residual,
        adjoint,
        image_gradient,
        small_sums[0],
        small_sums[1],
        small_sums[2],
        jnp.stack([pieces[0], pieces[3]]),
        jnp.stack([pieces[1], pieces[4]]),
        jnp.stack([pieces[2], pieces[5]]),
        down_sums,
        pieces[6],
        pieces[7],
        pieces[8],
    )


MESH = pl.DeviceIdType.MESH
CHIPS = 16
UNITS = 14
SMALL = UNITS
ROUTES = ("zxy", "zyx", "yxz", "zxy", "zyx", "zxy", "zyx", "yxz", "zxy", "zyx", "zxy", "yxz", "zyx", "zxy", "zxy")
ROUNDS = 6


class Place:
    def __init__(self):
        dp = lax.axis_index("dp")
        self.dp = dp
        self.h = lax.axis_index("heads")
        self.x = lax.rem(dp, 2)
        self.y = lax.rem(dp // 2, 2)
        self.z = dp // 4
        self.to_x = (dp + 1 - 2 * self.x, self.h)
        self.to_y = (dp + 2 - 4 * self.y, self.h)
        self.above = (dp + 4, self.h)
        self.below = (dp - 4, self.h)
        self.sibling = (dp, 1 - self.h)

    def barrier(self, sibling=False):
        bar = pltpu.get_barrier_semaphore()

        def greet(device):
            pl.semaphore_signal(bar, inc=1, device_id=device, device_id_type=MESH)

        greet(self.to_x)
        greet(self.to_y)
        if sibling:
            greet(self.sibling)
        pl.when(self.z < 3)(lambda: greet(self.above))
        pl.when(self.z > 0)(lambda: greet(self.below))
        peers = (3 if sibling else 2) + jnp.where(self.z < 3, 1, 0) + jnp.where(self.z > 0, 1, 0)
        pl.semaphore_wait(bar, peers)


def remote(source, target, send, recv, device):
    return pltpu.make_async_remote_copy(
        src_ref=source,
        dst_ref=target,
        send_sem=send,
        recv_sem=recv,
        device_id=device,
        device_id_type=MESH,
    )


class Gather:
    def __init__(self, at, views, send, recv):
        self.at, self.views, self.send, self.recv = at, views, send, recv

    def hop(self, u, slot, piece, device):
        return remote(piece, piece, self.send.at[u, slot], self.recv.at[u, slot], device)

    def line(self, u, step, piece_of, act):
        at = self.at
        z = at.z
        if act == "send":

            @pl.when((z < 3) & (z >= step - 1))
            def _():
                self.hop(u, step - 1, piece_of(z - (step - 1)), at.above).start()

            @pl.when((z > 0) & (z + step - 1 <= 3))
            def _():
                self.hop(u, step + 2, piece_of(z + (step - 1)), at.below).start()

        elif act == "recv":

            @pl.when(z >= step)
            def _():
                self.hop(u, step - 1, piece_of(z - step), at.below).wait_recv()

            @pl.when(z + step <= 3)
            def _():
                self.hop(u, step + 2, piece_of(z + step), at.above).wait_recv()

        else:

            @pl.when((z < 3) & (z >= step - 1))
            def _():
                self.hop(u, step - 1, piece_of(z - (step - 1)), at.above).wait_send()

            @pl.when((z > 0) & (z + step - 1 <= 3))
            def _():
                self.hop(u, step + 2, piece_of(z + (step - 1)), at.below).wait_send()

    def cross(self, u, axis, first, act):
        at, view = self.at, self.views(u)
        x, y, z = at.x, at.y, at.z
        route = ROUTES[u]
        if route[0] == "z":
            if axis == route[1]:
                mine, its = view.at[:, y, x], (view.at[:, y, 1 - x] if axis == "x" else view.at[:, 1 - y, x])
            elif axis == "x":
                mine, its = view.at[:, :, x], view.at[:, :, 1 - x]
            else:
                mine, its = view.at[:, y], view.at[:, 1 - y]
        elif axis == route[0]:
            mine, its = view.at[z, y, x], (view.at[z, y, 1 - x] if axis == "x" else view.at[z, 1 - y, x])
        elif axis == "x":
            mine, its = view.at[z, :, x], view.at[z, :, 1 - x]
        else:
            mine, its = view.at[z, y], view.at[z, 1 - y]
        slot, device = (6, at.to_x) if axis == "x" else (7, at.to_y)
        if act == "recv":
            self.hop(u, slot, its, device).wait_recv()
        elif act == "send":
            self.hop(u, slot, mine, device).start()
        else:
            self.hop(u, slot, mine, device).wait_send()

    def stages(self, u):
        at, view, route = self.at, self.views(u), ROUTES[u]
        if route[0] == "z":
            along = partial(self.line, u, piece_of=lambda k: view.at[k, at.y, at.x])
            lines = [partial(along, step) for step in (1, 2, 3)]
            return lines + [partial(self.cross, u, route[1], None), partial(self.cross, u, route[2], None)]
        along = partial(self.line, u, piece_of=lambda k: view.at[k])
        lines = [partial(along, step) for step in (1, 2, 3)]
        return [partial(self.cross, u, route[0], None), partial(self.cross, u, route[1], None)] + lines

    def round(self, u, k):
        stages = self.stages(u)
        if k > 0:
            stages[k - 1](act="recv")
        if k < 5:
            stages[k](act="send")

    def drain(self, u):
        for stage in self.stages(u):
            stage(act="sent")


def add_blocks(total, extra, count):
    @pl.loop(0, count)
    def _(i):
        left, right = total(i), extra(i)
        left[...] = (left[...].astype(jnp.float32) + right[...].astype(jnp.float32)).astype(left.dtype)


class Scatter:
    def __init__(self, at, views, spare, send, recv):
        self.at, self.views, self.spare, self.send, self.recv = at, views, spare, send, recv

    def hop(self, u, slot, source, target, device):
        return remote(source, target, self.send.at[u, slot], self.recv.at[u, slot], device)

    def line(self, u, step, act):
        at = self.at
        z = at.z
        wide = ROUTES[u][0] != "z"
        view, up, down = self.views(u), self.spare(u, "up"), self.spare(u, "down")

        def piece(k):
            return view.at[k] if wide else view.at[k, at.y, at.x]

        def send_up():
            return self.hop(u, step - 1, piece(z + 4 - step), up.at[step - 1], at.above)

        def send_down():
            return self.hop(u, step + 2, piece(z + step - 4), down.at[step - 1], at.below)

        if act == "send":
            pl.when((z < 3) & (z <= step - 1))(lambda: send_up().start())
            pl.when((z > 0) & (z >= 4 - step))(lambda: send_down().start())
        elif act == "sent":
            pl.when((z < 3) & (z <= step - 1))(lambda: send_up().wait_send())
            pl.when((z > 0) & (z >= 4 - step))(lambda: send_down().wait_send())
        else:
            shape = (2, 2) if wide else (1,)

            def take(k, slots):
                if wide:
                    for i in (0, 1):
                        add_blocks(lambda j: view.at[k, i, j], lambda j: slots.at[step - 1, i, j], 2)
                else:
                    add_blocks(lambda j: view.at[k, at.y, at.x], lambda j: slots.at[step - 1], 1)

            @pl.when((z >= 1) & (z <= step))
            def _():
                self.hop(u, step - 1, piece(z), up.at[step - 1], at.below).wait_recv()
                take(z + 3 - step, up)

            @pl.when((z < 3) & (z >= 3 - step))
            def _():
                self.hop(u, step + 2, piece(z), down.at[step - 1], at.above).wait_recv()
                take(z + step - 3, down)

    def cross(self, u, axis, act):
        at, view, spare = self.at, self.views(u), self.spare(u, axis)
        x, y, z = at.x, at.y, at.z
        route = ROUTES[u]
        slot, device = (6, at.to_x) if axis == "x" else (7, at.to_y)
        if route[0] == "z":
            if axis == route[2]:
                its = view.at[:, :, 1 - x] if axis == "x" else view.at[:, 1 - y]

                def add():
                    for j in (0, 1):
                        if axis == "x":
                            add_blocks(lambda i: view.at[i, j, x], lambda i: spare.at[i, j], 4)
                        else:
                            add_blocks(lambda i: view.at[i, y, j], lambda i: spare.at[i, j], 4)
            else:
                its = view.at[:, y, 1 - x] if axis == "x" else view.at[:, 1 - y, x]

                def add():
                    add_blocks(lambda i: view.at[i, y, x], lambda i: spare.at[i], 4)
        elif axis == route[1]:
            its = view.at[z, :, 1 - x] if axis == "x" else view.at[z, 1 - y]

            def add():
                if axis == "x":
                    add_blocks(lambda i: view.at[z, i, x], lambda i: spare.at[i], 2)
                else:
                    add_blocks(lambda i: view.at[z, y, i], lambda i: spare.at[i], 2)
        else:
            its = view.at[z, y, 1 - x] if axis == "x" else view.at[z, 1 - y, x]

            def add():
                add_blocks(lambda i: view.at[z, y, x], lambda i: spare, 1)

        hop = self.hop(u, slot, its, spare, device)
        if act == "send":
            hop.start()
        elif act == "sent":
            hop.wait_send()
        else:
            hop.wait_recv()
            add()

    def stages(self, u):
        route = ROUTES[u]
        lines = [partial(self.line, u, step) for step in (1, 2, 3)]
        if route[0] == "z":
            return [partial(self.cross, u, route[2]), partial(self.cross, u, route[1])] + lines
        return lines + [partial(self.cross, u, route[1]), partial(self.cross, u, route[0])]

    def round(self, u, k, end):
        stages = self.stages(u)
        if k > 0:
            stages[k - 1](act="recv")
        if k < 5:
            stages[k](act="send")
        else:
            end(u)

    def drain(self, u):
        for stage in self.stages(u):
            stage(act="sent")


def spare_shapes(rows, width, small):
    narrow = [u for u in range(UNITS) if ROUTES[u][0] == "z"]
    wide = [u for u in range(UNITS) if ROUTES[u][0] != "z"]

    def of(count, tail, kind):
        return [
            pltpu.VMEM((count, 4, 2) + tail, kind),
            pltpu.VMEM((count, 4) + tail, kind),
            pltpu.VMEM((count, 3) + tail, kind),
            pltpu.VMEM((count, 3) + tail, kind),
        ]

    shapes = of(len(narrow), (rows, width), jnp.bfloat16)
    tail = (rows, width)
    shapes += [
        pltpu.VMEM((len(wide), 2) + tail, jnp.bfloat16),
        pltpu.VMEM((len(wide),) + tail, jnp.bfloat16),
        pltpu.VMEM((len(wide), 3, 2, 2) + tail, jnp.bfloat16),
        pltpu.VMEM((len(wide), 3, 2, 2) + tail, jnp.bfloat16),
    ]
    shapes += of(1, (rows, small), jnp.float32)

    def pick(refs):
        def spare(u, what):
            route = ROUTES[u]
            if u == SMALL:
                base, index = 8, 0
            elif route[0] == "z":
                base, index = 0, narrow.index(u)
            else:
                base, index = 4, wide.index(u)
            if what in "xy":
                first = route[2] if route[0] == "z" else route[1]
                slot = 0 if what == first else 1
            else:
                slot = 2 if what == "up" else 3
            return refs[base + slot].at[index]

        return spare

    return shapes, pick


def gather_order():
    events = [((-1 if u == SMALL else u) + 2.5 * k, u, k) for u in range(UNITS + 1) for k in range(ROUNDS)]
    return [(u, k) for key, u, k in sorted(events)]


class ForwardRefs(NamedTuple):
    blocks: Any
    small: Any
    tokens: Any
    images: Any
    causal: Any
    choice: Any
    full: Any
    table: Any
    residuals: Any
    mixed: Any
    attended: Any
    queries: Any
    pair: Any
    hidden: Any
    out_rows: Any
    layer_out: Any
    g: Any
    g_small: Any
    tab: Any
    res: Any
    normed: Any
    mix: Any
    att: Any
    qc: Any
    pr: Any
    hid: Any
    act: Any
    acc: Any
    give: Any
    take: Any
    img: Any
    tok: Any
    rowsw: Any
    send: Any
    recv: Any
    local: Any
    swap_send: Any
    swap_recv: Any
    quarter_send: Any
    quarter_recv: Any
    keep: Any


class BackRefs(NamedTuple):
    full: Any
    table: Any
    residuals: Any
    mixed: Any
    attended: Any
    queries: Any
    pair: Any
    hidden: Any
    out_rows: Any
    cotangent: Any
    images: Any
    causal: Any
    choice: Any
    sums_out: Any
    small_out: Any
    token_out: Any
    image_out: Any
    g: Any
    tab: Any
    dx: Any
    branch: Any
    res: Any
    scale: Any
    normed: Any
    hid: Any
    dhid: Any
    act: Any
    mix: Any
    att: Any
    datt: Any
    qc: Any
    pr: Any
    rowsw: Any
    img: Any
    give: Any
    take: Any
    pic_give: Any
    pic_take: Any
    og: Any
    sums: Any
    small: Any
    send: Any
    recv: Any
    swap_send: Any
    swap_recv: Any
    quarter_send: Any
    quarter_recv: Any
    quarter_local: Any
    load: Any
    store: Any


def lowest(value):
    return value.astype(jnp.bfloat16)


def mm(left, right):
    return jnp.dot(left, right, preferred_element_type=jnp.float32)


def mm_back(left, right):
    return lax.dot_general(left, right, (((1,), (1,)), ((), ())), preferred_element_type=jnp.float32)


def mm_rows(left, right):
    return lax.dot_general(left, right, (((0,), (0,)), ((), ())), preferred_element_type=jnp.float32)


def first_lanes(value):
    return lax.broadcasted_iota(jnp.int32, value.shape, 1) < HEAD


def two_heads(value):
    lanes = first_lanes(value)
    zero = jnp.zeros_like(value)
    return jnp.concatenate([jnp.where(lanes, value, zero), jnp.where(lanes, zero, value)], axis=0)


def beside(value):
    half = value.shape[0] // 2
    return jnp.concatenate([value[:half], value[half:]], axis=1)


def softmax_of(scores):
    shares = jnp.exp(scores - jnp.max(scores, axis=1, keepdims=True))
    return shares / jnp.sum(shares, axis=1, keepdims=True)


SPAN = 128
ROWS_AT_ONCE = 256


def whole(ref):
    value = ref[...]
    return value.reshape(-1, value.shape[-1])


def picture_bias(choice):
    away = jnp.full_like(choice, masked_score)
    zero = jnp.zeros_like(choice)
    first = jnp.where(choice == 0.0, zero, away)
    second = jnp.where(choice == 1.0, zero, away)
    return jnp.concatenate([first, first, second, second], axis=1)


def norm_parts(value):
    center = value - jnp.mean(value, axis=1, keepdims=True)
    variance = jnp.mean(center * center, axis=1, keepdims=True)
    scale = lax.rsqrt(variance + 1e-05)
    return center * scale, scale


GELU_A = math.sqrt(2 / math.pi)
GELU_B = 0.044715


def gelu(value):
    return 0.5 * value * (1.0 + jnp.tanh(GELU_A * (value + GELU_B * (value * value * value))))


def merge_events(events, segments):
    done, order, rest = set(), [], list(segments)
    for u, k in events:
        order.append(("move", u, k))
        if k == ROUNDS - 1:
            done.add(u)
        if rest and rest[0][0] <= done:
            order.append(("work", rest.pop(0)[1]))
    return order + [("work", work) for needs, work in rest]


def forward_kernel(*refs):
    r = ForwardRefs(*refs)
    at = Place()
    h = at.h
    at.barrier(sibling=True)
    tokens = r.tok.shape[0]
    width = r.tok.shape[1]
    half = width // 2
    spans = [pl.ds(i, ROWS_AT_ONCE) for i in range(0, tokens, ROWS_AT_ONCE)]
    gather = Gather(at, lambda u: r.g_small if u == SMALL else r.g.at[u], r.send, r.recv)

    copies = [
        pltpu.make_async_copy(r.small, r.g_small.at[at.z, at.y, at.x], r.local.at[0]),
        pltpu.make_async_copy(r.blocks, r.g.at[:, at.z, at.y, at.x], r.local.at[1]),
        pltpu.make_async_copy(r.tokens, r.tok, r.local.at[2]),
        pltpu.make_async_copy(r.images, r.img, r.local.at[3]),
    ]
    for copy in copies:
        copy.start()

    keeps = []

    def keep(source, target):
        copy = pltpu.make_async_copy(source, target, r.keep.at[len(keeps)])
        keeps.append(copy)
        copy.start()

    def vector(n):
        return r.tab[pl.ds(n, 1), :]

    def own_vector(n):
        return r.tab[pl.ds(n, 1), pl.ds(pl.multiple_of(h * half, 128), half)]

    def start():
        for copy in copies[2:]:
            copy.wait()
        r.res[0] = r.tok[...].astype(jnp.float32)
        r.tab[...] = whole(r.g_small).astype(jnp.float32).T
        keep(r.tab, r.table)

    def norm(n):
        @pl.loop(0, tokens // 64)
        def _(i):
            rows = pl.ds(pl.multiple_of(i * 64, 64), 64)
            value, scale = norm_parts(r.res[n, rows, :])
            r.normed[rows, :] = lowest(value * vector(n) + vector(5 + n))

        keep(r.res.at[n], r.residuals.at[n])

    def quarter(l, u):
        away = (1 - h) * 2
        mine = pltpu.make_async_copy(
            r.g.at[u, pl.ds(h * 2, 2), :, :, :, pl.ds(half, half)],
            r.rowsw.at[l, :, :, :, :, pl.ds(pl.multiple_of(h * half, 128), half)],
            r.local.at[4 + l],
        )
        theirs = remote(
            r.g.at[u, pl.ds(away, 2), :, :, :, pl.ds(half, half)],
            r.rowsw.at[l, :, :, :, :, pl.ds(pl.multiple_of(h * half, 128), half)],
            r.quarter_send.at[l],
            r.quarter_recv.at[l],
            at.sibling,
        )
        return mine, theirs

    def start_quarter(l, u):
        mine, theirs = quarter(l, u)
        mine.start()
        theirs.start()

    def end_quarter(l, u):
        mine, theirs = quarter(l, u)
        mine.wait()
        theirs.wait()
        keep(r.rowsw.at[l], r.out_rows.at[l])

    def swap(e, i):
        rows = spans[i]
        return remote(
            r.give.at[e % 2, rows], r.take.at[e % 2, rows], r.swap_send.at[e, i], r.swap_recv.at[e, i], at.sibling
        )

    def offer(e, i, value):
        r.give[e % 2, spans[i], :] = lowest(value)
        swap(e, i).start()

    def join(e, i, n, bias):
        swap(e, i).wait()
        rows = spans[i]
        both = r.give[e % 2, rows, :].astype(jnp.float32) + r.take[e % 2, rows, :].astype(jnp.float32)
        r.res[n + 1, rows, :] = r.res[n, rows, :] + both + vector(5 + bias)

    def mix(l, u, query_bias, value_bias, i):
        rows = spans[i]
        value = r.normed[rows, :]
        both = mm(value, whole(r.g.at[u]))
        r.mix[l, rows, :half] = lowest(both[:, :half] + own_vector(5 + query_bias))
        r.mix[l, rows, half:width] = lowest(both[:, half:])
        r.mix[l, rows, width:] = lowest(
            mm(value, whole(r.g.at[u + 1, :, :, :, :, :half])) + own_vector(5 + value_bias)
        )

    def attend(l, blocks):
        @pl.loop(*blocks)
        def _(i):
            rows = pl.ds(pl.multiple_of(i * SPAN, SPAN), SPAN)
            bias = r.causal[i]
            bias = jnp.concatenate([bias, bias], axis=0)
            for j in range(half // 128):
                lanes = [pl.ds(part * half + j * 128, 128) for part in range(3)]
                queries, keys, values = [r.mix[l, rows, lane] for lane in lanes]
                scores = mm_back(two_heads(queries), keys) * HEAD ** (-0.5) + bias
                shares = lowest(softmax_of(scores))
                r.att[l, rows, pl.ds(j * 128, 128)] = lowest(mm(beside(shares), two_heads(values)))

    def project_out(l, e, a, i):
        value = r.att[a, spans[i], :]
        offer(e, i, mm(value, whole(r.rowsw.at[a])))

    def up(l, u, s, i):
        rows = spans[i]
        value = mm(r.normed[rows, :], whole(r.g.at[u])) + vector(21 + 2 * l + s)
        r.hid[l, rows, pl.ds(s * width, width)] = value
        r.act[rows, pl.ds(s * width, width)] = lowest(gelu(value))

    def down(u, s, i, e):
        rows = spans[i]
        value = mm(r.act[rows, pl.ds(s * width, width)], whole(r.g.at[u]))
        if s == 0:
            r.acc[rows, :] = value
        else:
            offer(e, i, r.acc[rows, :] + value)

    def picture_pair(i):
        rows = spans[i]
        value = mm(r.img[rows, :], whole(r.g.at[9]))
        r.pr[rows, :half] = lowest(value[:, :half])
        r.pr[rows, half:] = lowest(value[:, half:] + own_vector(5 + 14))

    def cross_queries(i):
        rows = spans[i]
        r.qc[rows, :] = lowest(mm(r.normed[rows, :], whole(r.g.at[8, :, :, :, :, :half])) + own_vector(5 + 13))

    def cross(blocks):
        @pl.loop(*blocks)
        def _(i):
            rows = pl.ds(pl.multiple_of(i * SPAN, SPAN), SPAN)
            bias = picture_bias(r.choice[rows, :])
            bias = jnp.concatenate([bias, bias], axis=0)
            for j in range(half // 128):
                keys = r.pr[:, pl.ds(j * 128, 128)]
                values = r.pr[:, pl.ds(half + j * 128, 128)]
                scores = mm_back(two_heads(r.qc[rows, pl.ds(j * 128, 128)]), keys) * HEAD ** (-0.5) + bias
                shares = lowest(softmax_of(scores))
                r.att[2, rows, pl.ds(j * 128, 128)] = lowest(mm(beside(shares), two_heads(values)))

    segments = []

    def add(needs, work, *args):
        segments.append((frozenset(needs), partial(work, *args)))

    def add_attention(l, n, u, e, biases, rest):
        add({SMALL, u, u + 1}, start_quarter, l, u + 1)
        add(rest, norm, n)
        for i in (0, 1):
            add(rest, mix, l, u, biases[0], biases[1], i)
        for i in (0, 1):
            add(rest, attend, l, (2 * i, 2 * i + 2))
        add(rest, end_quarter, l, u + 1)
        add(rest, keep, r.mix.at[l], r.mixed.at[l])
        for i in (0, 1):
            add(rest, project_out, l, e, l, i)
        add(rest, keep, r.att.at[l], r.attended.at[l])
        for i in (0, 1):
            add(rest, join, e, i, n, biases[2])

    def add_feed(l, n, u, e, bias):
        add((), norm, n)
        for s in (0, 1):
            for i in (0, 1):
                add({u + s}, up, l, u + s, s, i)
        add((), keep, r.hid.at[l], r.hidden.at[l])
        for s in (0, 1):
            for i in (0, 1):
                add({u + 2 + s}, down, u + 2 + s, s, i, e)
        if e < 4:
            for i in (0, 1):
                add((), join, e, i, n, bias)

    add({SMALL}, start)
    add_attention(0, 0, 0, 0, (5, 6, 7), ())
    add_feed(0, 1, 2, 1, 8)
    add_attention(1, 2, 6, 2, (9, 10, 11), ())
    add({9}, picture_pair, 0)
    add((), picture_pair, 1)
    add((), keep, r.pr, r.pair)
    add({8}, start_quarter, 2, 8)
    add((), norm, 3)
    for i in (0, 1):
        add((), cross_queries, i)
    add((), keep, r.qc, r.queries)
    for i in range(4):
        add((), cross, (i, i + 1))
    add((), end_quarter, 2, 8)
    for i in (0, 1):
        add((), project_out, 2, 3, 2, i)
    add((), keep, r.att.at[2], r.attended.at[2])
    for i in (0, 1):
        add((), join, 3, i, 3, 15)
    add_feed(1, 4, 10, 4, 12)

    for copy in copies[:2]:
        copy.wait()
    for step in merge_events(gather_order(), segments):
        if step[0] == "move":
            gather.round(step[1], step[2])
            if step[2] == ROUNDS - 1 and step[1] != SMALL:
                keep(r.g.at[step[1]], r.full.at[step[1]])
        else:
            step[1]()
    for i in (0, 1):
        swap(4, i).wait()
    mine = pl.ds(pl.multiple_of(h * ROWS_AT_ONCE, ROWS_AT_ONCE), ROWS_AT_ONCE)
    both = r.give[0, mine, :].astype(jnp.float32) + r.take[0, mine, :].astype(jnp.float32)
    r.layer_out[...] = r.res[4, mine, :] + both + vector(5 + 12)
    for u in range(UNITS + 1):
        gather.drain(u)
    for copy in keeps:
        copy.wait()


def forward(blocks, small, tokens, images, causal, choice):
    units, rows, width = blocks.shape
    count = tokens.shape[0]
    half = width // 2
    bf, fl = jnp.bfloat16, jnp.float32
    shape = jax.ShapeDtypeStruct
    dma = pltpu.SemaphoreType.DMA
    outs = (
        shape((units, 4, 2, 2, rows, width), bf),
        shape((128, width), fl),
        shape((5, count, width), fl),
        shape((2, count, width + half), bf),
        shape((3, count, half), bf),
        shape((count, half), bf),
        shape((count, width), bf),
        shape((2, count, 2 * width), fl),
        shape((3, 2, 2, 2, rows, width), bf),
        shape((count // 2, width), fl),
    )
    anywhere, here = pl.BlockSpec(memory_space=pl.ANY), pl.BlockSpec(memory_space=pltpu.VMEM)
    return pl.pallas_call(
        forward_kernel,
        out_shape=outs,
        in_specs=[anywhere] * 4 + [here] * 2,
        out_specs=[anywhere] * 9 + [here],
        scratch_shapes=[
            pltpu.VMEM((units, 4, 2, 2, rows, width), bf),
            pltpu.VMEM((4, 2, 2) + small.shape, bf),
            pltpu.VMEM((128, width), fl),
            pltpu.VMEM((5, count, width), fl),
            pltpu.VMEM((count, width), bf),
            pltpu.VMEM((2, count, width + half), bf),
            pltpu.VMEM((3, count, half), bf),
            pltpu.VMEM((count, half), bf),
            pltpu.VMEM((count, width), bf),
            pltpu.VMEM((2, count, 2 * width), fl),
            pltpu.VMEM((count, 2 * width), bf),
            pltpu.VMEM((count, width), fl),
            pltpu.VMEM((2, count, width), bf),
            pltpu.VMEM((2, count, width), bf),
            pltpu.VMEM((count, width), bf),
            pltpu.VMEM((count, width), bf),
            pltpu.VMEM((3, 2, 2, 2, rows, width), bf),
            dma((units + 1, 8)),
            dma((units + 1, 8)),
            dma((8,)),
            dma((5, 2)),
            dma((5, 2)),
            dma((3,)),
            dma((3,)),
            dma((40,)),
        ],
        compiler_params=pltpu.CompilerParams(collective_id=0, has_side_effects=True, vmem_limit_bytes=60 << 20),
    )(blocks, small, tokens, images, causal, choice)


BACK_UNITS = (12, 13, 10, 11, 9, 8, 6, 7, 4, 5, 2, 3, 0, 1, SMALL)
OUT_UNITS = (8, 7, 1)


def gelu_parts(value):
    square = value * value
    bent = jnp.tanh(value * (GELU_A + (GELU_A * GELU_B) * square))
    rise = 0.5 + 0.5 * bent
    slope = rise + (0.5 * value) * (1.0 - bent * bent) * (GELU_A + (3.0 * GELU_A * GELU_B) * square)
    return value * rise, slope


def merge_back(segments, lag):
    clock, events, ready = 0.0, [], {}
    for place, (cost, work, finished) in enumerate(segments):
        events.append((clock, 1, place, ("work", work)))
        clock += cost
        for u in finished:
            ready[u] = clock
    previous = 0.0
    for i, u in enumerate(BACK_UNITS):
        begin = ready[u] if u == SMALL else max(ready[u], previous)
        previous = begin + lag[0]
        for k in range(ROUNDS):
            events.append((begin + lag[1] * k, 0, i, ("move", u, k)))
    events.sort(key=lambda event: event[:3])
    return [event[3] for event in events]


BACK_LAG = (4.0, 20.0)


def backward_kernel(*refs, pick, spares):
    named = len(BackRefs._fields)
    r = BackRefs(*refs[:named])
    spare = pick(refs[named:])
    at = Place()
    h = at.h
    at.barrier(sibling=True)
    tokens, width = r.branch.shape
    half = width // 2
    spans = [pl.ds(i, ROWS_AT_ONCE) for i in range(0, tokens, ROWS_AT_ONCE)]
    mine = pl.ds(pl.multiple_of(h * ROWS_AT_ONCE, ROWS_AT_ONCE), ROWS_AT_ONCE)
    others = pl.ds(pl.multiple_of((1 - h) * ROWS_AT_ONCE, ROWS_AT_ONCE), ROWS_AT_ONCE)
    own_lanes = pl.ds(pl.multiple_of(h * half, 128), half)
    other_lanes = pl.ds(pl.multiple_of((1 - h) * half, 128), half)
    scatter = Scatter(at, lambda u: r.small if u == SMALL else r.g.at[u], spare, r.send, r.recv)

    loads = {}

    def fetch(name, source, target):
        copy = pltpu.make_async_copy(source, target, r.load.at[len(loads)])
        loads[name] = copy
        copy.start()

    def need(name):
        copy = loads[name]
        if copy is not None:
            copy.wait()
            loads[name] = None

    def fetch_unit(u):
        if u in OUT_UNITS:
            fetch(("g", u), r.full.at[u, :, :, :, :, pl.ds(0, half)], r.g.at[u, :, :, :, :, pl.ds(0, half)])
        else:
            fetch(("g", u), r.full.at[u], r.g.at[u])

    def fetch_residual(n, slot):
        fetch(("res", n), r.residuals.at[n], r.res.at[slot])

    def fetch_hidden(l):
        for s in (0, 1):
            fetch(("hid", l, s), r.hidden.at[l, :, pl.ds(s * width, width)], r.hid.at[s])

    def fetch_mixed(l):
        fetch(("mix", l), r.mixed.at[l], r.mix)

    fetch("table", r.table, r.tab)
    fetch("cotangent", r.cotangent, r.branch)
    fetch_unit(12)
    fetch_hidden(1)
    fetch_unit(13)
    fetch_residual(4, 0)
    fetch_unit(10)
    fetch_unit(11)
    fetch("rows", r.out_rows, r.rowsw)
    fetch("queries", r.queries, r.qc)
    fetch("pair", r.pair, r.pr)
    fetch_residual(3, 1)
    fetch("attended", r.attended, r.att)
    fetch("images", r.images, r.img)
    for u in (9, 8):
        fetch_unit(u)
    fetch_mixed(1)
    for u in (6, 7, 4, 5, 2, 3, 0, 1):
        fetch_unit(u)

    def vector(n):
        return r.tab[pl.ds(n, 1), :]

    def add_row(n, value):
        r.sums[pl.ds(n, 1), :] += jnp.sum(value, axis=0, keepdims=True)

    def add_own(n, value):
        r.sums[pl.ds(n, 1), own_lanes] += jnp.sum(value, axis=0, keepdims=True)

    def start():
        need("cotangent")
        r.sums[...] = jnp.zeros_like(r.sums)
        r.dx[...] = r.branch[...].astype(jnp.float32)

    def norm(n, slot):
        need(("res", n))
        need("table")

        @pl.loop(0, tokens // 64)
        def _(i):
            rows = pl.ds(pl.multiple_of(i * 64, 64), 64)
            value, scale = norm_parts(r.res[slot, rows, :])
            r.res[slot, rows, :] = value
            r.scale[rows, :] = scale
            r.normed[rows, :] = lowest(value * vector(n) + vector(5 + n))

    def begin_branch(bias):
        @pl.loop(0, tokens // 64, init_carry=jnp.zeros((1, width), jnp.float32))
        def total(i, carry):
            rows = pl.ds(pl.multiple_of(i * 64, 64), 64)
            value = lowest(r.dx[rows, :])
            r.branch[rows, :] = value
            return carry + jnp.sum(value.astype(jnp.float32), axis=0, keepdims=True)

        r.sums[pl.ds(5 + bias, 1), :] = total

    def swap(e, i):
        rows = spans[i]
        return remote(
            r.give.at[e % 2, rows], r.take.at[e % 2, rows], r.swap_send.at[e, i], r.swap_recv.at[e, i], at.sibling
        )

    def offer(e, i, value):
        r.give[e % 2, spans[i], :] = lowest(value)
        swap(e, i).start()

    def join(e, i, n, slot):
        swap(e, i).wait()
        base = i * ROWS_AT_ONCE
        gain = vector(n)
        zero = jnp.zeros((1, width), jnp.float32)

        @pl.loop(0, ROWS_AT_ONCE // 64, init_carry=(zero, zero))
        def totals(k, carry):
            rows = pl.ds(pl.multiple_of(base + k * 64, 64), 64)
            given = r.give[e % 2, rows, :].astype(jnp.float32) + r.take[e % 2, rows, :].astype(jnp.float32)
            value = r.res[slot, rows, :]
            product = given * value
            scaled = given * gain
            first = jnp.mean(scaled, axis=1, keepdims=True)
            second = jnp.mean(product * gain, axis=1, keepdims=True)
            r.dx[rows, :] += r.scale[rows, :] * (scaled - first - value * second)
            return (
                carry[0] + jnp.sum(product, axis=0, keepdims=True),
                carry[1] + jnp.sum(given, axis=0, keepdims=True),
            )

        r.sums[pl.ds(n, 1), :] += totals[0]
        r.sums[pl.ds(5 + n, 1), :] += totals[1]

    def store_rows(u, part, value, lanes=slice(None)):
        value = lowest(value)
        r.g[u, 2 * part : 2 * part + 2, :, :, :, lanes] = value.reshape((2, 2, 2, -1) + value.shape[1:])

    def feed_hidden(l, u, s, i):
        need(("g", u))
        need(("hid", l, s))
        rows, lanes = spans[i], pl.ds(s * width, width)
        back = mm_back(r.branch[rows, :], whole(r.g.at[u]))
        active, slope = gelu_parts(r.hid[s, rows, :])
        value = lowest(back * slope)
        r.act[rows, lanes] = lowest(active)
        r.dhid[rows, lanes] = value
        add_row(21 + 2 * l + s, value.astype(jnp.float32))

    def feed_down(u, s, part):
        lanes = pl.ds(s * width + part * half, half)
        store_rows(u, part, mm_rows(r.act[:, lanes], r.branch[...]))

    def feed_normed(u, i, e):
        need(("g", u))
        need(("g", u + 1))
        rows = spans[i]
        value = mm_back(r.dhid[rows, :width], whole(r.g.at[u]))
        offer(e, i, value + mm_back(r.dhid[rows, width:], whole(r.g.at[u + 1])))

    def feed_up(u, s, part):
        lanes = pl.ds(s * width, width)
        store_rows(u, part, mm_rows(r.normed[:, pl.ds(part * half, half)], r.dhid[:, lanes]))

    def attended_back(a, i):
        need("rows")
        r.datt[spans[i], :] = lowest(mm_back(r.branch[spans[i], :], whole(r.rowsw.at[a])))

    def near_copy(a, u):
        return pltpu.make_async_copy(
            r.og.at[:, :, :, :, own_lanes],
            r.g.at[u, pl.ds(2 * h, 2), :, :, :, pl.ds(half, half)],
            r.quarter_local.at[a],
        )

    def far_copy(a, u, rows_of):
        return remote(
            r.og.at[:, :, :, :, other_lanes],
            r.g.at[u, pl.ds(2 * rows_of, 2), :, :, :, pl.ds(half, half)],
            r.quarter_send.at[a],
            r.quarter_recv.at[a],
            at.sibling,
        )

    def out_gradient(a, u):
        need("attended")
        value = lowest(mm_rows(r.att[a], r.branch[...]))
        r.og[...] = value.reshape(r.og.shape)
        near_copy(a, u).start()
        far_copy(a, u, h).start()

    def end_quarter(a, u):
        near_copy(a, u).wait()
        far_copy(a, u, h).wait_send()
        far_copy(a, u, 1 - h).wait_recv()

    scaling = HEAD ** (-0.5)

    def attend_back(l, blocks):
        need(("mix", l))

        @pl.loop(*blocks)
        def _(b):
            rows = pl.ds(pl.multiple_of(b * SPAN, SPAN), SPAN)
            bias = r.causal[b]
            bias = jnp.concatenate([bias, bias], axis=0)
            for j in range(half // 128):
                lanes = [pl.ds(part * half + j * 128, 128) for part in range(3)]
                queries, keys, values = [r.mix[rows, lane] for lane in lanes]
                queries = two_heads(queries)
                given = two_heads(r.datt[rows, pl.ds(j * 128, 128)])
                shares = softmax_of(mm_back(queries, keys) * scaling + bias)
                share_adjoint = mm_back(given, values)
                score_adjoint = lowest(shares * (share_adjoint - jnp.sum(shares * share_adjoint, axis=1, keepdims=True)))
                r.dhid[rows, lanes[0]] = lowest(mm(beside(score_adjoint), two_heads(keys)) * scaling)
                r.dhid[rows, lanes[1]] = lowest(mm_rows(score_adjoint, queries) * scaling)
                r.dhid[rows, lanes[2]] = lowest(mm_rows(lowest(shares), given))

    def mixed_normed(u, e, i, biases):
        need(("g", u))
        need(("g", u + 1))
        rows = spans[i]
        value = mm_back(r.dhid[rows, :width], whole(r.g.at[u]))
        value += mm_back(r.dhid[rows, pl.ds(width, half)], whole(r.g.at[u + 1, :, :, :, :, pl.ds(0, half)]))
        offer(e, i, value)

    def mixed_sums(biases):
        add_own(5 + biases[0], r.dhid[:, :half].astype(jnp.float32))
        add_own(5 + biases[1], r.dhid[:, pl.ds(width, half)].astype(jnp.float32))

    def mixed_gradient(u, part):
        store_rows(u, part, mm_rows(r.normed[:, pl.ds(part * half, half)], r.dhid[:, :width]))

    def value_gradient(u, part):
        value = mm_rows(r.normed[:, pl.ds(part * half, half)], r.dhid[:, pl.ds(width, half)])
        store_rows(u, part, value, pl.ds(0, half))

    def cross_back(b):
        need("queries")
        need("pair")
        rows = pl.ds(b * SPAN, SPAN)
        bias = picture_bias(r.choice[rows, :])
        bias = jnp.concatenate([bias, bias], axis=0)
        for j in range(half // 128):
            lanes = pl.ds(j * 128, 128)
            value_lanes = pl.ds(half + j * 128, 128)
            keys, values = r.pr[:, lanes], r.pr[:, value_lanes]
            queries = two_heads(r.qc[rows, lanes])
            given = two_heads(r.datt[rows, lanes])
            shares = softmax_of(mm_back(queries, keys) * scaling + bias)
            share_adjoint = mm_back(given, values)
            score_adjoint = lowest(shares * (share_adjoint - jnp.sum(shares * share_adjoint, axis=1, keepdims=True)))
            r.act[rows, lanes] = lowest(mm(beside(score_adjoint), two_heads(keys)) * scaling)
            key_adjoint = mm_rows(score_adjoint, queries) * scaling
            value_adjoint = mm_rows(lowest(shares), given)
            if b == 0:
                r.hid[0, :, lanes] = key_adjoint
                r.hid[0, :, value_lanes] = value_adjoint
            else:
                r.hid[0, :, lanes] += key_adjoint
                r.hid[0, :, value_lanes] += value_adjoint

    def pair_adjoint():
        r.dhid[:, :width] = lowest(r.hid[0])
        add_own(5 + 13, r.act[:, :half].astype(jnp.float32))
        add_own(5 + 14, r.dhid[:, pl.ds(half, half)].astype(jnp.float32))

    def query_normed(e, i):
        need(("g", 8))
        offer(e, i, mm_back(r.act[spans[i], pl.ds(0, half)], whole(r.g.at[8, :, :, :, :, pl.ds(0, half)])))

    def query_gradient(part):
        value = mm_rows(r.normed[:, pl.ds(part * half, half)], r.act[:, pl.ds(0, half)])
        store_rows(8, part, value, pl.ds(0, half))

    def pic_swap():
        return remote(r.pic_give, r.pic_take, r.swap_send.at[5, 0], r.swap_recv.at[5, 0], at.sibling)

    def picture_back():
        need(("g", 9))
        r.pic_give[...] = lowest(mm_back(r.dhid[others, pl.ds(0, width)], whole(r.g.at[9])))
        pic_swap().start()

    def picture_own():
        r.hid[1, pl.ds(0, ROWS_AT_ONCE), :] = mm_back(r.dhid[mine, pl.ds(0, width)], whole(r.g.at[9]))

    def picture_copy():
        return pltpu.make_async_copy(r.hid.at[1, pl.ds(0, ROWS_AT_ONCE)], r.image_out, r.store.at[UNITS])

    def picture_join():
        pic_swap().wait()
        r.hid[1, pl.ds(0, ROWS_AT_ONCE), :] += r.pic_take[...].astype(jnp.float32)
        picture_copy().start()

    def pair_gradient(part):
        need("images")
        store_rows(9, part, mm_rows(r.img[:, pl.ds(part * half, half)], r.dhid[:, pl.ds(0, width)]))

    def picture_end():
        picture_copy().wait()
        fetch_hidden(0)

    def small_total():
        r.small[...] = r.sums[...].T.reshape(r.small.shape)

    def token_copy():
        return pltpu.make_async_copy(r.dx.at[mine], r.token_out, r.store.at[UNITS + 1])

    segments = []

    def add(cost, work, *args, finished=()):
        segments.append((cost, partial(work, *args), finished))

    def add_feed(l, n, slot, u, e, bias, after):
        add(1.0, begin_branch, bias)
        for s in (0, 1):
            for i in (0, 1):
                add(1.5, feed_hidden, l, u + 2 + s, s, i)
            for part in (0, 1):
                add(0.8, feed_down, u + 2 + s, s, part, finished=(u + 2 + s,) if part else ())
        for i in (0, 1):
            add(1.4, feed_normed, u, i, e)
        add(1.5, norm, n, slot)
        for s in (0, 1):
            for part in (0, 1):
                add(0.8, feed_up, u + s, s, part, finished=(u + s,) if part else ())
        for i in (0, 1):
            add(1.2, join, e, i, n, slot)
        for work in after:
            add(0.1, *work)

    def add_attention(l, n, slot, u, e, biases, after):
        add(1.0, begin_branch, biases[2])
        for i in (0, 1):
            add(0.4, attended_back, l, i)
        add(0.8, out_gradient, l, u + 1)
        add(4.0, attend_back, l, (0, 2))
        add(4.0, attend_back, l, (2, 4))
        for i in (0, 1):
            add(1.2, mixed_normed, u, e, i, biases)
        add(1.5, norm, n, slot)
        for part in (0, 1):
            add(0.8, mixed_gradient, u, part, finished=(u,) if part else ())
        for part in (0, 1):
            add(0.5, value_gradient, u + 1, part)
        add(0.2, end_quarter, l, u + 1, finished=(u + 1,))
        add(0.5, mixed_sums, biases)
        for i in (0, 1):
            add(1.2, join, e, i, n, slot)
        for work in after:
            add(0.1, *work)

    add(1.0, start)
    add_feed(1, 4, 0, 10, 0, 12, [(fetch_residual, 2, 0)])
    add(1.0, begin_branch, 15)
    for i in (0, 1):
        add(0.4, attended_back, 2, i)
    add(0.8, out_gradient, 2, 8)
    for b in range(tokens // SPAN):
        add(3.5, cross_back, b)
    add(1.0, pair_adjoint)
    for i in (0, 1):
        add(0.5, query_normed, 1, i)
    add(0.8, picture_back)
    add(0.8, picture_own)
    for part in (0, 1):
        add(0.8, pair_gradient, part, finished=(9,) if part else ())
    add(1.5, norm, 3, 1)
    for part in (0, 1):
        add(0.5, query_gradient, part)
    add(0.2, end_quarter, 2, 8, finished=(8,))
    for i in (0, 1):
        add(1.2, join, 1, i, 3, 1)
    add(0.3, picture_join)
    add(0.1, fetch_residual, 1, 1)
    add_attention(1, 2, 0, 6, 2, (9, 10, 11), [(picture_end,), (fetch_residual, 0, 0), (fetch_mixed, 0)])
    add_feed(0, 1, 1, 2, 3, 8, [])
    add_attention(0, 0, 0, 0, 4, (5, 6, 7), [])
    add(0.5, small_total, finished=(SMALL,))

    def end_unit(u):
        if u == SMALL:
            r.small_out[...] = r.small[at.z, at.y, at.x]
        else:
            pltpu.make_async_copy(r.g.at[u, at.z, at.y, at.x], r.sums_out.at[u], r.store.at[u]).start()

    last = len(segments) - 1
    for step in merge_back(segments, BACK_LAG):
        if step[0] == "move":
            scatter.round(step[1], step[2], end_unit)
        else:
            step[1]()
            if step[1] is segments[last][1]:
                token_copy().start()
    for u in BACK_UNITS:
        scatter.drain(u)
        if u != SMALL:
            pltpu.make_async_copy(r.g.at[u, at.z, at.y, at.x], r.sums_out.at[u], r.store.at[u]).wait()
    token_copy().wait()


def backward(full, table, residuals, mixed, attended, queries, pair, hidden, out_rows, cotangent, images, causal, choice):
    units, rows, width = full.shape[0], full.shape[4], full.shape[5]
    count = cotangent.shape[0]
    half = width // 2
    bf, fl = jnp.bfloat16, jnp.float32
    shape = jax.ShapeDtypeStruct
    dma = pltpu.SemaphoreType.DMA
    shapes, pick = spare_shapes(rows, width, 128)
    anywhere, here = pl.BlockSpec(memory_space=pl.ANY), pl.BlockSpec(memory_space=pltpu.VMEM)
    return pl.pallas_call(
        partial(backward_kernel, pick=pick, spares=len(shapes)),
        out_shape=(
            shape((units, rows, width), bf),
            shape((rows, 128), fl),
            shape((count // 2, width), fl),
            shape((count // 2, width), fl),
        ),
        in_specs=[anywhere] * 11 + [here] * 2,
        out_specs=[anywhere, here, anywhere, anywhere],
        scratch_shapes=[
            pltpu.VMEM(full.shape, bf),
            pltpu.VMEM((128, width), fl),
            pltpu.VMEM((count, width), fl),
            pltpu.VMEM((count, width), bf),
            pltpu.VMEM((2, count, width), fl),
            pltpu.VMEM((count, 1), fl),
            pltpu.VMEM((count, width), bf),
            pltpu.VMEM((2, count, width), fl),
            pltpu.VMEM((count, 2 * width), bf),
            pltpu.VMEM((count, 2 * width), bf),
            pltpu.VMEM((count, width + half), bf),
            pltpu.VMEM((3, count, half), bf),
            pltpu.VMEM((count, half), bf),
            pltpu.VMEM((count, half), bf),
            pltpu.VMEM((count, width), bf),
            pltpu.VMEM(out_rows.shape, bf),
            pltpu.VMEM((count, width), bf),
            pltpu.VMEM((2, count, width), bf),
            pltpu.VMEM((2, count, width), bf),
            pltpu.VMEM((count // 2, width), bf),
            pltpu.VMEM((count // 2, width), bf),
            pltpu.VMEM(out_rows.shape[1:], bf),
            pltpu.VMEM((128, width), fl),
            pltpu.VMEM((4, 2, 2, rows, 128), fl),
            dma((units + 1, 8)),
            dma((units + 1, 8)),
            dma((6, 2)),
            dma((6, 2)),
            dma((3,)),
            dma((3,)),
            dma((3,)),
            dma((40,)),
            dma((units + 2,)),
            *shapes,
        ],
        compiler_params=pltpu.CompilerParams(collective_id=1, has_side_effects=True, vmem_limit_bytes=63 << 20),
    )(full, table, residuals, mixed, attended, queries, pair, hidden, out_rows, cotangent, images, causal, choice)


def swap_cores(value):
    return lax.ppermute(value, "heads", [(0, 1), (1, 0)])


def both_cores(value, member):
    other = swap_cores(value)
    return jnp.stack([jnp.where(member == 0, value, other), jnp.where(member == 0, other, value)])


def to_units(member, self_weight, self_out_weight, up_weight, query_weight, pair_weight, cross_out_weight):
    width = self_weight.shape[1 + 1] // 3
    half = width // 2
    rows = self_weight.shape[1]
    own = slice(member * half, member * half + half)
    value = slice(width + member * half, width + member * half + half)
    units = []
    for layer in (0, 1):
        weight = self_weight[layer]
        units.append(jnp.concatenate([weight[:, own], weight[:, value]], axis=1))
        units.append(jnp.concatenate([weight[:, 2 * width + member * half : 2 * width + member * half + half], self_out_weight[layer][:, own]], axis=1))
        up = up_weight[layer].reshape(rows, CHIPS, 2, 2, -1)[:, :, member]
        units.append(up[:, :, 0].reshape(rows, width))
        units.append(up[:, :, 1].reshape(rows, width))
    units.append(jnp.concatenate([query_weight[:, own], cross_out_weight[:, own]], axis=1))
    units.append(jnp.concatenate([pair_weight[:, own], pair_weight[:, value]], axis=1))
    return jnp.stack(units)


UNIT_OF_PIECE = (0, 1, 2, 3, 6, 7, 10, 11, 8, 9)


def chip_blocks(member, pieces, down_weight):
    theirs, ours = (
        jnp.where(member == 0, pieces[1], pieces[0]),
        jnp.where(member == 0, pieces[0], pieces[1]),
    )
    rows = jnp.concatenate(list(both_rows(member, ours, swap_cores(theirs))), axis=1)
    down = down_weight.reshape(2, 2, rows.shape[1], rows.shape[2])
    order = {u: rows[i] for i, u in enumerate(UNIT_OF_PIECE)}
    order.update({4: down[0, 0], 5: down[0, 1], 12: down[1, 0], 13: down[1, 1]})
    return jnp.stack([order[u] for u in range(UNITS)])


def both_rows(member, ours, other):
    return jnp.where(member == 0, ours, other), jnp.where(member == 0, other, ours)


def chip_program(
    tokens,
    images,
    segment_labels,
    image_index,
    cotangent,
    norm_gain,
    vector_bias,
    up_bias,
    self_weight,
    self_out_weight,
    up_weight,
    down_weight,
    query_weight,
    pair_weight,
    cross_out_weight,
):
    member = lax.axis_index("heads")
    rows, length, width = tokens.shape
    half = width // 2
    slim = self_weight.shape[1]
    matrices = (self_weight, self_out_weight, up_weight, query_weight, pair_weight, cross_out_weight)
    blocks = chip_blocks(member, [to_units(m, *matrices) for m in (0, 1)], down_weight)
    vectors = jnp.concatenate([norm_gain, vector_bias], axis=0)
    vectors = jnp.concatenate(list(both_cores(vectors, member)), axis=1)
    vectors = jnp.concatenate([vectors, up_bias.reshape(4, 2 * slim)], axis=0)
    small = jnp.pad(vectors, ((0, 128 - vectors.shape[0]), (0, 0))).T
    carried = both_cores(jnp.stack([tokens.reshape(-1, width), images.reshape(-1, width), cotangent.reshape(-1, width)]), member)
    carried = carried.transpose(1, 0, 2, 3).reshape(3, -1, width)
    pictures = carried[1]
    chip_rows = segment_labels.shape[0]
    labels = jnp.arange(image_index.shape[1])
    caption_image = jnp.sum(
        jnp.where(segment_labels[:, :, None] == labels[None, None, :], image_index[:, None, :], 0), axis=-1, dtype=jnp.int32
    )
    count = chip_rows * length
    span_rows = SPAN // length
    row_of = jnp.arange(SPAN) // length
    same = row_of[:, None] == row_of[None, :]
    span_labels = segment_labels.reshape(-1, SPAN)
    causal = (span_labels[:, :, None] == span_labels[:, None, :]) & (same & (jnp.arange(SPAN)[:, None] >= jnp.arange(SPAN)[None, :]))[None]
    causal = jnp.where(causal, 0.0, masked_score).astype(jnp.float32)
    choice = jnp.broadcast_to(caption_image.reshape(count, 1).astype(jnp.float32), (count, 128))
    full, table, residuals, mixed, attended, queries, pair, hidden, out_rows, layer_out = forward(
        blocks, small, carried[0], carried[1], causal, choice
    )
    sums, small_sums, token_gradient, image_gradient = backward(
        full, table, residuals, mixed, attended, queries, pair, hidden, out_rows, carried[2], carried[1], causal, choice
    )
    outs = finish(member, sums.astype(jnp.float32), small_sums, slim, width)
    mine = (layer_out.reshape(rows, length, width), token_gradient.reshape(rows, length, width), image_gradient[None])
    return mine + outs


def finish(member, sums, small_sums, slim, width):
    half = width // 2
    pieces = jnp.stack([sums[u] for u in UNIT_OF_PIECE]).reshape(len(UNIT_OF_PIECE), 2, slim, width)
    ours, theirs = pieces[:, member], pieces[:, 1 - member]
    both = jnp.stack(list(both_rows(member, ours, swap_cores(theirs))))

    def halves(piece, side):
        return jnp.concatenate([both[0, piece][:, side * half : (side + 1) * half], both[1, piece][:, side * half : (side + 1) * half]], axis=1)

    def up(piece):
        parts = [both[:, piece + s].reshape(2, slim, CHIPS, 2 * slim) for s in (0, 1)]
        return jnp.stack(parts, axis=0).transpose(2, 3, 1, 0, 4).reshape(slim, 4 * width)

    self_weight = jnp.stack([jnp.concatenate([halves(p, 0), halves(p, 1), halves(p + 1, 0)], axis=1) for p in (0, 4)])
    self_out = jnp.stack([halves(p, 1) for p in (1, 5)])
    up_gradient = jnp.stack([up(2), up(6)])
    down = jnp.stack([jnp.concatenate([sums[u], sums[u + 1]]) for u in (4, 12)])
    pair = jnp.concatenate([halves(9, 0), halves(9, 1)], axis=1)
    table = small_sums.T
    shared = table[:21]
    other = swap_cores(shared)
    split = jnp.zeros((21, 1), bool).at[jnp.array([5 + n for n in (5, 6, 9, 10, 13, 14)])].set(True)
    shared = jnp.where(split, shared + other, shared)
    shared = lax.dynamic_slice_in_dim(shared, member * slim, slim, 1)
    up_bias = table[21:25].reshape(2, 4 * slim)
    return (shared[:5], shared[5:], up_bias, self_weight, self_out, up_gradient, down, halves(8, 0), pair, halves(8, 1))


def solution(mesh):
    in_specs = (
        P(("dp", "heads"), None, None),
        P(("dp", "heads"), None, None),
        P("dp", None),
        P("dp", None),
        P(("dp", "heads"), None, None),
        P(None, ("dp", "heads")),
        P(None, ("dp", "heads")),
        P(None, ("dp", "heads")),
        P(None, ("dp", "heads"), None),
        P(None, ("dp", "heads"), None),
        P(None, ("dp", "heads"), None),
        P(None, ("dp", "heads"), None),
        P(("dp", "heads"), None),
        P(("dp", "heads"), None),
        P(("dp", "heads"), None),
    )
    out_specs = (
        P(("dp", "heads"), None, None),
        P(("dp", "heads"), None, None),
        P(("dp", "heads"), None, None),
        P(None, ("dp", "heads")),
        P(None, ("dp", "heads")),
        P(None, ("dp", "heads")),
        P(None, ("dp", "heads"), None),
        P(None, ("dp", "heads"), None),
        P(None, ("dp", "heads"), None),
        P(None, ("dp", "heads"), None),
        P(("dp", "heads"), None),
        P(("dp", "heads"), None),
        P(("dp", "heads"), None),
    )
    dp, cores = mesh.shape["dp"], mesh.shape["heads"]
    program = chip_program if (dp, cores) == (CHIPS, 2) else per_device
    return jax.shard_map(
        program, mesh=mesh, in_specs=in_specs, out_specs=out_specs, check_vma=False
    )
```

```python
from functools import partial
import math
from typing import Any, NamedTuple

import jax
import jax.numpy as jnp
from jax import lax
from jax.experimental import pallas as pl
from jax.experimental.pallas import tpu as pltpu
from jax.sharding import PartitionSpec as P

HEADS = 12
HEAD = 64


masked_score = -1e30


def layer_norm(residual, gain, shift):
    center = residual - jnp.mean(residual, axis=-1, keepdims=True)
    variance = jnp.mean(center * center, axis=-1, keepdims=True)
    return center * lax.rsqrt(variance + 1e-05) * gain + shift


def project(left, weight):
    return jnp.einsum("rld,de->rle", left, weight, preferred_element_type=jnp.float32)


def weight_adjoint(left, adjoint):
    return jnp.einsum("rld,rle->de", left, adjoint, preferred_element_type=jnp.float32)


def project_back(adjoint, weight):
    return jnp.einsum("rle,de->rld", adjoint, weight, preferred_element_type=jnp.float32)


def column_total(adjoint):
    return jnp.sum(adjoint, axis=(0, 1), dtype=jnp.float32)


def norm_back(residual, gain, shift, adjoint):
    unused, pull = jax.vjp(layer_norm, residual, gain, shift)
    return pull(adjoint)


def rows_to_heads(pieces):
    return lax.all_to_all(pieces, "heads", split_axis=3, concat_axis=0, tiled=True)


def heads_to_rows(pieces):
    return lax.all_to_all(pieces, "heads", split_axis=0, concat_axis=3, tiled=True)


def adjoint_to_heads(pieces):
    return lax.all_to_all(pieces, "heads", split_axis=3, concat_axis=0, tiled=True)


def adjoint_to_rows(pieces):
    return lax.all_to_all(pieces, "heads", split_axis=0, concat_axis=3, tiled=True)


def softmax_parts(scores):
    peak = jnp.max(scores, axis=-1, keepdims=True)
    log_total = peak + jnp.log(jnp.sum(jnp.exp(scores - peak), axis=-1, keepdims=True))
    return (jnp.exp(scores - log_total), log_total)


def softmax_back(shares, adjoint):
    return (shares * (adjoint - jnp.sum(shares * adjoint, axis=-1, keepdims=True))).astype(
        jnp.bfloat16
    )


def self_scores(queries, keys, allowed):
    scores = jnp.einsum(
        "rqhd,rkhd->rhqk", queries, keys, preferred_element_type=jnp.float32
    ) * HEAD ** (-0.5)
    return jnp.where(allowed[:, None], scores, masked_score)


def self_heads_forward(queries, keys, values, allowed):
    shares, log_total = softmax_parts(self_scores(queries, keys, allowed))
    attended = jnp.einsum(
        "rhqk,rkhd->rqhd", shares.astype(jnp.bfloat16), values, preferred_element_type=jnp.float32
    )
    return (attended.astype(jnp.bfloat16), log_total)


def self_heads_back(queries, keys, values, allowed, log_total, adjoint):
    shares = jnp.exp(self_scores(queries, keys, allowed) - log_total)
    value_adjoint = jnp.einsum(
        "rhqk,rqhd->rkhd", shares.astype(jnp.bfloat16), adjoint, preferred_element_type=jnp.float32
    )
    share_adjoint = jnp.einsum(
        "rqhd,rkhd->rhqk", adjoint, values, preferred_element_type=jnp.float32
    )
    score_adjoint = softmax_back(shares, share_adjoint)
    scale = HEAD ** (-0.5)
    query_adjoint = (
        jnp.einsum("rhqk,rkhd->rqhd", score_adjoint, keys, preferred_element_type=jnp.float32)
        * scale
    )
    key_adjoint = (
        jnp.einsum("rhqk,rqhd->rkhd", score_adjoint, queries, preferred_element_type=jnp.float32)
        * scale
    )
    return (
        query_adjoint.astype(jnp.bfloat16),
        key_adjoint.astype(jnp.bfloat16),
        value_adjoint.astype(jnp.bfloat16),
    )


def cross_scores(queries, image_keys, chosen):
    rows, length, heads, head_size = queries.shape
    scores = jnp.einsum(
        "rqhd,gkhd->rhqgk", queries, image_keys, preferred_element_type=jnp.float32
    ) * HEAD ** (-0.5)
    scores = jnp.where(chosen[:, None, :, :, None], scores, masked_score)
    return scores.reshape(rows, heads, length, -1)


def block_rows(rows, length):
    return math.gcd(rows, max(1, 512 // length))


def cross_heads_forward(queries, image_keys, image_values, chosen):
    rows, length, heads, head_size = queries.shape
    block = block_rows(rows, length)
    flat_values = image_values.reshape(-1, heads, head_size)

    def one_block(inputs):
        block_queries, block_chosen = inputs
        shares, log_total = softmax_parts(cross_scores(block_queries, image_keys, block_chosen))
        attended = jnp.einsum(
            "rhqc,chd->rqhd",
            shares.astype(jnp.bfloat16),
            flat_values,
            preferred_element_type=jnp.float32,
        )
        return (attended.astype(jnp.bfloat16), log_total)

    blocked = (
        queries.reshape(rows // block, block, length, heads, head_size),
        chosen.reshape(rows // block, block, length, -1),
    )
    attended, log_total = lax.map(one_block, blocked)
    return (attended.reshape(queries.shape), log_total)


def cross_heads_back(queries, image_keys, image_values, chosen, log_total, adjoint):
    rows, length, heads, head_size = queries.shape
    block = block_rows(rows, length)
    flat_keys = image_keys.reshape(-1, heads, head_size)
    flat_values = image_values.reshape(-1, heads, head_size)
    scale = HEAD ** (-0.5)

    def one_block(carry, inputs):
        key_total, value_total = carry
        block_queries, block_chosen, block_log, block_adjoint = inputs
        shares = jnp.exp(cross_scores(block_queries, image_keys, block_chosen) - block_log)
        value_total = value_total + jnp.einsum(
            "rhqc,rqhd->chd",
            shares.astype(jnp.bfloat16),
            block_adjoint,
            preferred_element_type=jnp.float32,
        )
        share_adjoint = jnp.einsum(
            "rqhd,chd->rhqc", block_adjoint, flat_values, preferred_element_type=jnp.float32
        )
        score_adjoint = softmax_back(shares, share_adjoint)
        key_total = (
            key_total
            + jnp.einsum(
                "rhqc,rqhd->chd", score_adjoint, block_queries, preferred_element_type=jnp.float32
            )
            * scale
        )
        query_adjoint = (
            jnp.einsum(
                "rhqc,chd->rqhd", score_adjoint, flat_keys, preferred_element_type=jnp.float32
            )
            * scale
        )
        return ((key_total, value_total), query_adjoint.astype(jnp.bfloat16))

    start = jnp.zeros(flat_keys.shape, jnp.float32)
    blocked = (
        queries.reshape(rows // block, block, length, heads, head_size),
        chosen.reshape(rows // block, block, length, -1),
        log_total,
        adjoint.reshape(rows // block, block, length, heads, head_size),
    )
    (key_total, value_total), query_adjoint = lax.scan(one_block, (start, start), blocked)
    return (
        query_adjoint.reshape(queries.shape),
        key_total.astype(jnp.bfloat16),
        value_total.astype(jnp.bfloat16),
    )


def self_forward(
    residual, allowed, gain, shift, weight, query_bias, value_bias, out_weight, out_bias, groups
):
    rows, length, width = residual.shape
    span = width // groups
    normed = layer_norm(residual, gain, shift).astype(jnp.bfloat16)
    offset = jnp.concatenate([query_bias, jnp.zeros_like(query_bias), value_bias])
    mixed = (project(normed, weight) + offset).astype(jnp.bfloat16)
    gathered = rows_to_heads(mixed.reshape(rows, length, 3, groups, span))
    gathered = gathered.reshape(rows * groups, length, 3, HEADS // groups, HEAD)
    queries, keys, values = (gathered[:, :, 0], gathered[:, :, 1], gathered[:, :, 2])
    attended, log_total = self_heads_forward(queries, keys, values, allowed)
    merged = heads_to_rows(attended.reshape(rows * groups, length, 1, 1, span)).reshape(
        rows, length, width
    )
    kept = (residual, normed, queries, keys, values, log_total, merged)
    return (residual + project(merged, out_weight) + out_bias, kept)


def self_backward(adjoint, kept, gain, shift, weight, out_weight, allowed, groups):
    residual, normed, queries, keys, values, log_total, merged = kept
    rows, length, width = residual.shape
    span = width // groups
    branch = adjoint.astype(jnp.bfloat16)
    out_bias_adjoint = column_total(branch)
    merged_adjoint = project_back(branch, out_weight).astype(jnp.bfloat16)
    head_adjoint = adjoint_to_heads(merged_adjoint.reshape(rows, length, 1, groups, span))
    head_adjoint = head_adjoint.reshape(rows * groups, length, HEADS // groups, HEAD)
    query_adjoint, key_adjoint, value_adjoint = self_heads_back(
        queries, keys, values, allowed, log_total, head_adjoint
    )
    stacked = jnp.stack([query_adjoint, key_adjoint, value_adjoint], axis=2).reshape(
        rows * groups, length, 3, 1, span
    )
    mixed_adjoint = adjoint_to_rows(stacked).reshape(rows, length, 3 * width)
    offset_adjoint = column_total(mixed_adjoint)
    residual_adjoint, gain_adjoint, shift_adjoint = norm_back(
        residual, gain, shift, project_back(mixed_adjoint, weight)
    )
    pairs = ((normed, mixed_adjoint), (merged, branch))
    small = (
        gain_adjoint,
        shift_adjoint,
        offset_adjoint[:width],
        offset_adjoint[2 * width :],
        out_bias_adjoint,
    )
    return (adjoint + residual_adjoint, pairs, small)


def cross_forward(
    residual,
    pictures,
    chosen,
    gain,
    shift,
    weight,
    query_bias,
    pair_matrix,
    value_bias,
    out_weight,
    out_bias,
    groups,
    member,
):
    rows, length, width = residual.shape
    span = width // groups
    key_weight = lax.dynamic_slice_in_dim(pair_matrix, member * span, span, 1)
    value_weight = lax.dynamic_slice_in_dim(pair_matrix, width + member * span, span, 1)
    value_shift = lax.dynamic_slice_in_dim(value_bias, member * span, span, 0)
    layout = (pictures.shape[0], pictures.shape[1], HEADS // groups, HEAD)
    image_keys = project(pictures, key_weight).astype(jnp.bfloat16).reshape(layout)
    image_values = (
        (project(pictures, value_weight) + value_shift).astype(jnp.bfloat16).reshape(layout)
    )
    normed = layer_norm(residual, gain, shift).astype(jnp.bfloat16)
    query_rows = (project(normed, weight) + query_bias).astype(jnp.bfloat16)
    queries = rows_to_heads(query_rows.reshape(rows, length, 1, groups, span))
    queries = queries.reshape(rows * groups, length, HEADS // groups, HEAD)
    attended, log_total = cross_heads_forward(queries, image_keys, image_values, chosen)
    merged = heads_to_rows(attended.reshape(rows * groups, length, 1, 1, span)).reshape(
        rows, length, width
    )
    kept = (residual, normed, queries, image_keys, image_values, log_total, merged)
    return (residual + project(merged, out_weight) + out_bias, kept)


def cross_backward(
    adjoint, kept, pictures, chosen, gain, shift, weight, pair_matrix, out_weight, groups, member
):
    residual, normed, queries, image_keys, image_values, log_total, merged = kept
    rows, length, width = residual.shape
    span = width // groups
    key_weight = lax.dynamic_slice_in_dim(pair_matrix, member * span, span, 1)
    value_weight = lax.dynamic_slice_in_dim(pair_matrix, width + member * span, span, 1)
    branch = adjoint.astype(jnp.bfloat16)
    out_bias_adjoint = column_total(branch)
    merged_adjoint = project_back(branch, out_weight).astype(jnp.bfloat16)
    head_adjoint = adjoint_to_heads(merged_adjoint.reshape(rows, length, 1, groups, span))
    head_adjoint = head_adjoint.reshape(rows * groups, length, HEADS // groups, HEAD)
    query_adjoint, key_adjoint, value_adjoint = cross_heads_back(
        queries, image_keys, image_values, chosen, log_total, head_adjoint
    )
    query_rows = adjoint_to_rows(query_adjoint.reshape(rows * groups, length, 1, 1, span)).reshape(
        rows, length, width
    )
    query_bias_adjoint = column_total(query_rows)
    residual_adjoint, gain_adjoint, shift_adjoint = norm_back(
        residual, gain, shift, project_back(query_rows, weight)
    )
    layout = (pictures.shape[0], pictures.shape[1], span)
    key_adjoint = key_adjoint.reshape(layout)
    value_adjoint = value_adjoint.reshape(layout)
    value_bias_adjoint = lax.dynamic_update_slice_in_dim(
        jnp.zeros((width,), jnp.float32), column_total(value_adjoint), member * span, 0
    )
    picture_adjoint = project_back(key_adjoint, key_weight) + project_back(
        value_adjoint, value_weight
    )
    pairs = ((normed, query_rows), (merged, branch), (key_adjoint, value_adjoint))
    small = (gain_adjoint, shift_adjoint, query_bias_adjoint, value_bias_adjoint, out_bias_adjoint)
    return (adjoint + residual_adjoint, pairs, small, picture_adjoint)


def feed_forward(residual, gain, shift, up_matrix, up_shift, down_matrix, down_shift):
    normed = layer_norm(residual, gain, shift).astype(jnp.bfloat16)
    hidden = project(normed, up_matrix) + up_shift
    active = jax.nn.gelu(hidden, approximate=True).astype(jnp.bfloat16)
    return (
        residual + project(active, down_matrix) + down_shift,
        (residual, normed, hidden, active),
    )


def feed_backward(adjoint, kept, gain, shift, up_matrix, down_matrix):
    residual, normed, hidden, active = kept
    branch = adjoint.astype(jnp.bfloat16)
    down_shift_adjoint = column_total(branch)
    unused, pull = jax.vjp(partial(jax.nn.gelu, approximate=True), hidden)
    hidden_adjoint = pull(project_back(branch, down_matrix))[0].astype(jnp.bfloat16)
    up_shift_adjoint = column_total(hidden_adjoint)
    residual_adjoint, gain_adjoint, shift_adjoint = norm_back(
        residual, gain, shift, project_back(hidden_adjoint, up_matrix)
    )
    pairs = ((normed, hidden_adjoint), (active, branch))
    small = (gain_adjoint, shift_adjoint, up_shift_adjoint, down_shift_adjoint)
    return (adjoint + residual_adjoint, pairs, small)


def per_device(
    tokens,
    images,
    segment_labels,
    image_index,
    cotangent,
    norm_gain,
    vector_bias,
    up_bias,
    self_weight,
    self_out_weight,
    up_weight,
    down_weight,
    query_weight,
    pair_weight,
    cross_out_weight,
):
    groups = lax.axis_size("heads")
    member = lax.axis_index("heads")
    everyone = lax.axis_size(("dp", "heads"))
    length = segment_labels.shape[1]
    position = jnp.arange(length)
    allowed = (segment_labels[:, :, None] == segment_labels[:, None, :]) & (
        position[:, None] >= position[None, :]
    )[None]
    labels = jnp.arange(image_index.shape[1])
    caption_image = jnp.sum(
        jnp.where(segment_labels[:, :, None] == labels[None, None, :], image_index[:, None, :], 0),
        axis=-1,
        dtype=jnp.int32,
    )
    pictures = lax.all_gather(images, "heads", axis=0, tiled=True)
    chosen = caption_image[:, :, None] == jnp.arange(pictures.shape[0])[None, None, :]
    first = (
        lax.all_gather(self_weight[0], ("dp", "heads"), axis=0, tiled=True),
        lax.all_gather(self_out_weight[0], ("dp", "heads"), axis=0, tiled=True),
        lax.all_gather(up_weight[0], ("dp", "heads"), axis=0, tiled=True),
        lax.all_gather(down_weight[0], ("dp", "heads"), axis=0, tiled=True),
        lax.all_gather(norm_gain, ("dp", "heads"), axis=1, tiled=True),
        lax.all_gather(vector_bias, ("dp", "heads"), axis=1, tiled=True),
        lax.all_gather(up_bias, ("dp", "heads"), axis=1, tiled=True),
    )
    gains = first[4].astype(jnp.float32)
    biases = first[5].astype(jnp.float32)
    up_biases = first[6].astype(jnp.float32)
    residual = tokens.astype(jnp.float32)
    residual, kept_self_one = self_forward(
        residual,
        allowed,
        gains[0],
        biases[0],
        first[0],
        biases[5],
        biases[6],
        first[1],
        biases[7],
        groups,
    )
    residual, kept_feed_one = feed_forward(
        residual, gains[1], biases[1], first[2], up_biases[0], first[3], biases[8]
    )
    second = (
        lax.all_gather(self_weight[1], ("dp", "heads"), axis=0, tiled=True),
        lax.all_gather(self_out_weight[1], ("dp", "heads"), axis=0, tiled=True),
        lax.all_gather(up_weight[1], ("dp", "heads"), axis=0, tiled=True),
        lax.all_gather(down_weight[1], ("dp", "heads"), axis=0, tiled=True),
        lax.all_gather(query_weight, ("dp", "heads"), axis=0, tiled=True),
        lax.all_gather(pair_weight, ("dp", "heads"), axis=0, tiled=True),
        lax.all_gather(cross_out_weight, ("dp", "heads"), axis=0, tiled=True),
    )
    residual, kept_self_two = self_forward(
        residual,
        allowed,
        gains[2],
        biases[2],
        second[0],
        biases[9],
        biases[10],
        second[1],
        biases[11],
        groups,
    )
    residual, kept_cross = cross_forward(
        residual,
        pictures,
        chosen,
        gains[3],
        biases[3],
        second[4],
        biases[13],
        second[5],
        biases[14],
        second[6],
        biases[15],
        groups,
        member,
    )
    residual, kept_feed_two = feed_forward(
        residual, gains[4], biases[4], second[2], up_biases[1], second[3], biases[12]
    )
    second = (
        lax.all_gather(self_weight[1], ("dp", "heads"), axis=0, tiled=True),
        lax.all_gather(self_out_weight[1], ("dp", "heads"), axis=0, tiled=True),
        lax.all_gather(up_weight[1], ("dp", "heads"), axis=0, tiled=True),
        lax.all_gather(down_weight[1], ("dp", "heads"), axis=0, tiled=True),
        lax.all_gather(query_weight, ("dp", "heads"), axis=0, tiled=True),
        lax.all_gather(pair_weight, ("dp", "heads"), axis=0, tiled=True),
        lax.all_gather(cross_out_weight, ("dp", "heads"), axis=0, tiled=True),
    )
    adjoint = cotangent.astype(jnp.float32)
    adjoint, feed_two, feed_two_small = feed_backward(
        adjoint, kept_feed_two, gains[4], biases[4], second[2], second[3]
    )
    adjoint, cross_pairs, cross_small, picture_adjoint = cross_backward(
        adjoint,
        kept_cross,
        pictures,
        chosen,
        gains[3],
        biases[3],
        second[4],
        second[5],
        second[6],
        groups,
        member,
    )
    image_gradient = lax.psum_scatter(
        picture_adjoint.astype(jnp.bfloat16), "heads", scatter_dimension=0, tiled=True
    ).astype(jnp.float32)
    adjoint, self_two, self_two_small = self_backward(
        adjoint, kept_self_two, gains[2], biases[2], second[0], second[1], allowed, groups
    )
    first = (
        lax.all_gather(self_weight[0], ("dp", "heads"), axis=0, tiled=True),
        lax.all_gather(self_out_weight[0], ("dp", "heads"), axis=0, tiled=True),
        lax.all_gather(up_weight[0], ("dp", "heads"), axis=0, tiled=True),
        lax.all_gather(down_weight[0], ("dp", "heads"), axis=0, tiled=True),
        lax.all_gather(norm_gain, ("dp", "heads"), axis=1, tiled=True),
    )
    back_gains = first[4].astype(jnp.float32)
    adjoint, feed_one, feed_one_small = feed_backward(
        adjoint, kept_feed_one, back_gains[1], biases[1], first[2], first[3]
    )
    adjoint, self_one, self_one_small = self_backward(
        adjoint, kept_self_one, back_gains[0], biases[0], first[0], first[1], allowed, groups
    )
    width = tokens.shape[2]
    hidden_width = feed_one[0][1].shape[2]
    span = width // groups
    row_pairs = (
        self_one[0],
        self_one[1],
        feed_one[0],
        self_two[0],
        self_two[1],
        feed_two[0],
        cross_pairs[0],
    )
    key_adjoint, value_adjoint = cross_pairs[2]
    blocks = []
    for left, right in row_pairs:
        blocks.append(weight_adjoint(left, right))
    pair_block = jnp.zeros(
        (width // everyone * lax.axis_size(("dp", "heads")), 2 * width), jnp.float32
    )
    pair_block = lax.dynamic_update_slice_in_dim(
        pair_block, weight_adjoint(pictures, key_adjoint), member * span, 1
    )
    pair_block = lax.dynamic_update_slice_in_dim(
        pair_block, weight_adjoint(pictures, value_adjoint), width + member * span, 1
    )
    blocks.append(pair_block)
    left, right = cross_pairs[1]
    blocks.append(weight_adjoint(left, right))
    row_sums = lax.psum_scatter(
        jnp.concatenate(blocks, axis=1), ("dp", "heads"), scatter_dimension=0, tiled=True
    )
    blocks = []
    for left, right in (feed_one[1], feed_two[1]):
        blocks.append(weight_adjoint(left, right))
    down_sums = lax.psum_scatter(
        jnp.concatenate(blocks, axis=1), ("dp", "heads"), scatter_dimension=0, tiled=True
    )
    down_sums = jnp.transpose(down_sums.reshape(down_sums.shape[0], 2, width), (1, 0, 2))
    columns = (
        3 * width,
        width,
        hidden_width,
        3 * width,
        width,
        hidden_width,
        width,
        2 * width,
        width,
    )
    pieces = []
    offset = 0
    for span_width in columns:
        pieces.append(row_sums[:, offset : offset + span_width])
        offset = offset + span_width
    gain_rows = jnp.stack(
        [self_one_small[0], feed_one_small[0], self_two_small[0], cross_small[0], feed_two_small[0]]
    )
    bias_rows = jnp.stack(
        [
            self_one_small[1],
            feed_one_small[1],
            self_two_small[1],
            cross_small[1],
            feed_two_small[1],
            self_one_small[2],
            self_one_small[3],
            self_one_small[4],
            feed_one_small[3],
            self_two_small[2],
            self_two_small[3],
            self_two_small[4],
            feed_two_small[3],
            cross_small[2],
            cross_small[3],
            cross_small[4],
        ]
    )
    up_rows = jnp.stack([feed_one_small[2], feed_two_small[2]])
    small_sums = (
        lax.psum_scatter(gain_rows, ("dp", "heads"), scatter_dimension=1, tiled=True),
        lax.psum_scatter(bias_rows, ("dp", "heads"), scatter_dimension=1, tiled=True),
        lax.psum_scatter(up_rows, ("dp", "heads"), scatter_dimension=1, tiled=True),
    )
    return (
        residual,
        adjoint,
        image_gradient,
        small_sums[0],
        small_sums[1],
        small_sums[2],
        jnp.stack([pieces[0], pieces[3]]),
        jnp.stack([pieces[1], pieces[4]]),
        jnp.stack([pieces[2], pieces[5]]),
        down_sums,
        pieces[6],
        pieces[7],
        pieces[8],
    )


MESH = pl.DeviceIdType.MESH
CHIPS = 16
UNITS = 14
SMALL = UNITS
GATHER_ROUTES = ("zyx", "zxy", "yxz", "zxy", "zyx", "zxy", "zyx", "xyz", "zyx", "zxy", "zyx", "xyz", "zxy", "yxz", "zxy")
SCATTER_ROUTES = ("zyx", "zyx", "zxy", "zxy", "yxz", "zyx", "zxy", "zyx", "xyz", "zyx", "zxy", "xyz", "zxy", "zyx", "zxy")
ROUNDS = 6


class Place:
    def __init__(self):
        dp = lax.axis_index("dp")
        self.dp = dp
        self.h = lax.axis_index("heads")
        self.x = lax.rem(dp, 2)
        self.y = lax.rem(dp // 2, 2)
        self.z = dp // 4
        self.to_x = (dp + 1 - 2 * self.x, self.h)
        self.to_y = (dp + 2 - 4 * self.y, self.h)
        self.above = (dp + 4, self.h)
        self.below = (dp - 4, self.h)
        self.sibling = (dp, 1 - self.h)

    def barrier(self, sibling=False):
        bar = pltpu.get_barrier_semaphore()

        def greet(device):
            pl.semaphore_signal(bar, inc=1, device_id=device, device_id_type=MESH)

        greet(self.to_x)
        greet(self.to_y)
        if sibling:
            greet(self.sibling)
        pl.when(self.z < 3)(lambda: greet(self.above))
        pl.when(self.z > 0)(lambda: greet(self.below))
        peers = (3 if sibling else 2) + jnp.where(self.z < 3, 1, 0) + jnp.where(self.z > 0, 1, 0)
        pl.semaphore_wait(bar, peers)


def remote(source, target, send, recv, device):
    return pltpu.make_async_remote_copy(
        src_ref=source,
        dst_ref=target,
        send_sem=send,
        recv_sem=recv,
        device_id=device,
        device_id_type=MESH,
    )


class Gather:
    def __init__(self, at, views, send, recv):
        self.at, self.views, self.send, self.recv = at, views, send, recv

    def hop(self, u, slot, piece, device):
        return remote(piece, piece, self.send.at[u, slot], self.recv.at[u, slot], device)

    def line(self, u, step, piece_of, act):
        at = self.at
        z = at.z
        if act == "send":

            @pl.when((z < 3) & (z >= step - 1))
            def _():
                self.hop(u, step - 1, piece_of(z - (step - 1)), at.above).start()

            @pl.when((z > 0) & (z + step - 1 <= 3))
            def _():
                self.hop(u, step + 2, piece_of(z + (step - 1)), at.below).start()

        elif act == "recv":

            @pl.when(z >= step)
            def _():
                self.hop(u, step - 1, piece_of(z - step), at.below).wait_recv()

            @pl.when(z + step <= 3)
            def _():
                self.hop(u, step + 2, piece_of(z + step), at.above).wait_recv()

        else:

            @pl.when((z < 3) & (z >= step - 1))
            def _():
                self.hop(u, step - 1, piece_of(z - (step - 1)), at.above).wait_send()

            @pl.when((z > 0) & (z + step - 1 <= 3))
            def _():
                self.hop(u, step + 2, piece_of(z + (step - 1)), at.below).wait_send()

    def cross(self, u, axis, first, act):
        at, view = self.at, self.views(u)
        x, y, z = at.x, at.y, at.z
        route = GATHER_ROUTES[u]
        if route[0] == "z":
            if axis == route[1]:
                mine, its = view.at[:, y, x], (view.at[:, y, 1 - x] if axis == "x" else view.at[:, 1 - y, x])
            elif axis == "x":
                mine, its = view.at[:, :, x], view.at[:, :, 1 - x]
            else:
                mine, its = view.at[:, y], view.at[:, 1 - y]
        elif axis == route[0]:
            mine, its = view.at[z, y, x], (view.at[z, y, 1 - x] if axis == "x" else view.at[z, 1 - y, x])
        elif axis == "x":
            mine, its = view.at[z, :, x], view.at[z, :, 1 - x]
        else:
            mine, its = view.at[z, y], view.at[z, 1 - y]
        slot, device = (6, at.to_x) if axis == "x" else (7, at.to_y)
        if act == "recv":
            self.hop(u, slot, its, device).wait_recv()
        elif act == "send":
            self.hop(u, slot, mine, device).start()
        else:
            self.hop(u, slot, mine, device).wait_send()

    def stages(self, u):
        at, view, route = self.at, self.views(u), GATHER_ROUTES[u]
        if route[0] == "z":
            along = partial(self.line, u, piece_of=lambda k: view.at[k, at.y, at.x])
            lines = [partial(along, step) for step in (1, 2, 3)]
            return lines + [partial(self.cross, u, route[1], None), partial(self.cross, u, route[2], None)]
        along = partial(self.line, u, piece_of=lambda k: view.at[k])
        lines = [partial(along, step) for step in (1, 2, 3)]
        return [partial(self.cross, u, route[0], None), partial(self.cross, u, route[1], None)] + lines

    def round(self, u, k):
        stages = self.stages(u)
        if k > 0:
            stages[k - 1](act="recv")
        if k < 5:
            stages[k](act="send")

    def drain(self, u):
        for stage in self.stages(u):
            stage(act="sent")


def add_blocks(total, extra, count):
    @pl.loop(0, count)
    def _(i):
        left, right = total(i), extra(i)
        left[...] = (left[...].astype(jnp.float32) + right[...].astype(jnp.float32)).astype(left.dtype)


class Scatter:
    def __init__(self, at, views, spare, send, recv):
        self.at, self.views, self.spare, self.send, self.recv = at, views, spare, send, recv

    def hop(self, u, slot, source, target, device):
        return remote(source, target, self.send.at[u, slot], self.recv.at[u, slot], device)

    def line(self, u, step, act):
        at = self.at
        z = at.z
        wide = SCATTER_ROUTES[u][0] != "z"
        view, up, down = self.views(u), self.spare(u, "up"), self.spare(u, "down")

        def piece(k):
            return view.at[k] if wide else view.at[k, at.y, at.x]

        def send_up():
            return self.hop(u, step - 1, piece(z + 4 - step), up.at[step - 1], at.above)

        def send_down():
            return self.hop(u, step + 2, piece(z + step - 4), down.at[step - 1], at.below)

        if act == "send":
            pl.when((z < 3) & (z <= step - 1))(lambda: send_up().start())
            pl.when((z > 0) & (z >= 4 - step))(lambda: send_down().start())
        elif act == "sent":
            pl.when((z < 3) & (z <= step - 1))(lambda: send_up().wait_send())
            pl.when((z > 0) & (z >= 4 - step))(lambda: send_down().wait_send())
        else:
            shape = (2, 2) if wide else (1,)

            def take(k, slots):
                if wide:
                    for i in (0, 1):
                        add_blocks(lambda j: view.at[k, i, j], lambda j: slots.at[step - 1, i, j], 2)
                else:
                    add_blocks(lambda j: view.at[k, at.y, at.x], lambda j: slots.at[step - 1], 1)

            @pl.when((z >= 1) & (z <= step))
            def _():
                self.hop(u, step - 1, piece(z), up.at[step - 1], at.below).wait_recv()
                take(z + 3 - step, up)

            @pl.when((z < 3) & (z >= 3 - step))
            def _():
                self.hop(u, step + 2, piece(z), down.at[step - 1], at.above).wait_recv()
                take(z + step - 3, down)

    def cross(self, u, axis, act):
        at, view, spare = self.at, self.views(u), self.spare(u, axis)
        x, y, z = at.x, at.y, at.z
        route = SCATTER_ROUTES[u]
        slot, device = (6, at.to_x) if axis == "x" else (7, at.to_y)
        if route[0] == "z":
            if axis == route[2]:
                its = view.at[:, :, 1 - x] if axis == "x" else view.at[:, 1 - y]

                def add():
                    for j in (0, 1):
                        if axis == "x":
                            add_blocks(lambda i: view.at[i, j, x], lambda i: spare.at[i, j], 4)
                        else:
                            add_blocks(lambda i: view.at[i, y, j], lambda i: spare.at[i, j], 4)
            else:
                its = view.at[:, y, 1 - x] if axis == "x" else view.at[:, 1 - y, x]

                def add():
                    add_blocks(lambda i: view.at[i, y, x], lambda i: spare.at[i], 4)
        elif axis == route[1]:
            its = view.at[z, :, 1 - x] if axis == "x" else view.at[z, 1 - y]

            def add():
                if axis == "x":
                    add_blocks(lambda i: view.at[z, i, x], lambda i: spare.at[i], 2)
                else:
                    add_blocks(lambda i: view.at[z, y, i], lambda i: spare.at[i], 2)
        else:
            its = view.at[z, y, 1 - x] if axis == "x" else view.at[z, 1 - y, x]

            def add():
                add_blocks(lambda i: view.at[z, y, x], lambda i: spare, 1)

        hop = self.hop(u, slot, its, spare, device)
        if act == "send":
            hop.start()
        elif act == "sent":
            hop.wait_send()
        else:
            hop.wait_recv()
            add()

    def stages(self, u):
        route = SCATTER_ROUTES[u]
        lines = [partial(self.line, u, step) for step in (1, 2, 3)]
        if route[0] == "z":
            return [partial(self.cross, u, route[2]), partial(self.cross, u, route[1])] + lines
        return lines + [partial(self.cross, u, route[1]), partial(self.cross, u, route[0])]

    def round(self, u, k, end):
        stages = self.stages(u)
        if k > 0:
            stages[k - 1](act="recv")
        if k < 5:
            stages[k](act="send")
        else:
            end(u)

    def drain(self, u):
        for stage in self.stages(u):
            stage(act="sent")


def spare_shapes(rows, width, small):
    narrow = [u for u in range(UNITS) if SCATTER_ROUTES[u][0] == "z"]
    wide = [u for u in range(UNITS) if SCATTER_ROUTES[u][0] != "z"]

    def of(count, tail, kind):
        return [
            pltpu.VMEM((count, 4, 2) + tail, kind),
            pltpu.VMEM((count, 4) + tail, kind),
            pltpu.VMEM((count, 3) + tail, kind),
            pltpu.VMEM((count, 3) + tail, kind),
        ]

    shapes = of(len(narrow), (rows, width), jnp.bfloat16)
    tail = (rows, width)
    shapes += [
        pltpu.VMEM((len(wide), 2) + tail, jnp.bfloat16),
        pltpu.VMEM((len(wide),) + tail, jnp.bfloat16),
        pltpu.VMEM((len(wide), 3, 2, 2) + tail, jnp.bfloat16),
        pltpu.VMEM((len(wide), 3, 2, 2) + tail, jnp.bfloat16),
    ]
    shapes += of(1, (rows, small), jnp.float32)

    def pick(refs):
        def spare(u, what):
            route = SCATTER_ROUTES[u]
            if u == SMALL:
                base, index = 8, 0
            elif route[0] == "z":
                base, index = 0, narrow.index(u)
            else:
                base, index = 4, wide.index(u)
            if what in "xy":
                first = route[2] if route[0] == "z" else route[1]
                slot = 0 if what == first else 1
            else:
                slot = 2 if what == "up" else 3
            return refs[base + slot].at[index]

        return spare

    return shapes, pick


class ForwardRefs(NamedTuple):
    blocks: Any
    small: Any
    tokens: Any
    images: Any
    causal: Any
    choice: Any
    full: Any
    table: Any
    residuals: Any
    mixed: Any
    attended: Any
    queries: Any
    pair: Any
    hidden: Any
    out_rows: Any
    layer_out: Any
    g: Any
    g_small: Any
    tab: Any
    res: Any
    normed: Any
    mix: Any
    att: Any
    qc: Any
    pr: Any
    hid: Any
    act: Any
    acc: Any
    give: Any
    take: Any
    img: Any
    tok: Any
    rowsw: Any
    send: Any
    recv: Any
    local: Any
    swap_send: Any
    swap_recv: Any
    quarter_send: Any
    quarter_recv: Any
    keep: Any


class BackRefs(NamedTuple):
    full: Any
    table: Any
    residuals: Any
    mixed: Any
    attended: Any
    queries: Any
    pair: Any
    hidden: Any
    out_rows: Any
    cotangent: Any
    images: Any
    causal: Any
    choice: Any
    sums_out: Any
    small_out: Any
    token_out: Any
    image_out: Any
    g: Any
    tab: Any
    dx: Any
    branch: Any
    res: Any
    scale: Any
    normed: Any
    hid: Any
    dhid: Any
    act: Any
    mix: Any
    att: Any
    datt: Any
    qc: Any
    pr: Any
    rowsw: Any
    img: Any
    give: Any
    take: Any
    pic_give: Any
    pic_take: Any
    og: Any
    sums: Any
    small: Any
    send: Any
    recv: Any
    swap_send: Any
    swap_recv: Any
    quarter_send: Any
    quarter_recv: Any
    quarter_local: Any
    load: Any
    store: Any


def lowest(value):
    return value.astype(jnp.bfloat16)


def mm(left, right):
    return jnp.dot(left, right, preferred_element_type=jnp.float32)


def mm_back(left, right):
    return lax.dot_general(left, right, (((1,), (1,)), ((), ())), preferred_element_type=jnp.float32)


def mm_rows(left, right):
    return lax.dot_general(left, right, (((0,), (0,)), ((), ())), preferred_element_type=jnp.float32)


def first_lanes(value):
    return lax.broadcasted_iota(jnp.int32, value.shape, 1) < HEAD


def two_heads(value):
    lanes = first_lanes(value)
    zero = jnp.zeros_like(value)
    return jnp.concatenate([jnp.where(lanes, value, zero), jnp.where(lanes, zero, value)], axis=0)


def beside(value):
    half = value.shape[0] // 2
    return jnp.concatenate([value[:half], value[half:]], axis=1)


def below(value):
    half = value.shape[1] // 2
    return jnp.concatenate([value[:, :half], value[:, half:]], axis=0)


def softmax_of(scores, axis):
    shares = jnp.exp(scores - jnp.max(scores, axis=axis, keepdims=True))
    return shares * (1.0 / jnp.sum(shares, axis=axis, keepdims=True))


SPAN = 128
SCALING = HEAD ** (-0.5)
ROWS_AT_ONCE = 256


def whole(ref):
    value = ref[...]
    return value.reshape(-1, value.shape[-1])


def picture_bias(choice):
    away = jnp.full_like(choice, masked_score)
    zero = jnp.zeros_like(choice)
    first = jnp.where(choice == 0.0, zero, away)
    second = jnp.where(choice == 1.0, zero, away)
    return jnp.concatenate([first, first, second, second], axis=1)


def norm_parts(value):
    center = value - jnp.mean(value, axis=1, keepdims=True)
    variance = jnp.mean(center * center, axis=1, keepdims=True)
    scale = lax.rsqrt(variance + 1e-05)
    return center * scale, scale


GELU_A = math.sqrt(2 / math.pi)
GELU_B = 0.044715


def gelu(value):
    return 0.5 * value * (1.0 + jnp.tanh(GELU_A * (value + GELU_B * (value * value * value))))


GATHER_ORDER = (
    84, 18, 0, 12, 85, 42, 19, 6, 1, 30, 86, 24, 13, 20, 36, 43, 7, 2, 87, 66, 31, 21, 48, 25, 3, 54, 37, 8, 78, 32, 60,
    67, 49, 26, 9, 72, 88, 55, 38, 33, 22, 27, 79, 4, 61, 50, 39, 73, 56, 14, 51, 44, 10, 62, 57, 89, -1, 34, 15, 74,
    23, 28, 45, 63, 5, 40, 75, 16, 68, 52, 46, 11, -1, -1, -1, -1, -1, -1, 58, -1, -1, -1, -1, -1, -1, -1, 17, -1, -1,
    -1, -1, -1, -1, 35, 69, 47, 29, -1, -1, -1, -1, 80, -1, -1, 64, 41, -1, -1, -1, -1, -1, -1, 76, -1, -1, -1, -1, -1,
    -1, -1, 81, 70, 53, 59, -1, -1, -1, -1, -1, -1, -1, -1, -1, -1, -1, -1, -1, -1, -1, -1, -1, -1, -1, 71, 82, 65, -1,
    -1, -1, -1, -1, 77, -1, -1, 83, -1, -1,
)
SCATTER_ORDER = (
    -1, -1, -1, -1, -1, -1, 72, -1, -1, -1, -1, 78, -1, -1, -1, -1, -1, -1, -1, 66, -1, -1, -1, -1, -1, -1, -1, -1, 60,
    -1, 67, -1, 73, -1, -1, -1, -1, -1, -1, 79, -1, 68, -1, -1, 54, -1, -1, -1, -1, -1, -1, 48, -1, -1, -1, -1, -1, -1,
    -1, 61, -1, 49, -1, -1, -1, -1, 36, -1, -1, -1, -1, -1, 50, -1, 42, 55, -1, -1, -1, -1, -1, -1, -1, -1, -1, 74, -1,
    24, -1, -1, 30, -1, 80, -1, -1, -1, -1, 12, -1, 25, -1, -1, 37, -1, -1, -1, -1, 43, -1, -1, 26, 62, -1, -1, 75, -1,
    -1, -1, -1, 31, -1, 81, -1, -1, -1, -1, 56, -1, 6, -1, -1, 13, 84, 76, 63, 82, 38, 44, 57, 7, 64, 32, 58, 14, 39,
    45, 0, 18, 33, 40, 8, 46, 15, 34, 1, 16, 19, 77, 85, 9, 83, 69, 10, 65, 2, 51, 59, 20, 86, 70, 41, 3, 47, 27, 21,
    35, 87, 52, 4, 17, 22, 11, 28, 71, 88, 53, 5, 23, 89, 29,
)


def play(order, steps, move):
    moved, left = set(), list(steps)
    for code in order:
        if code < 0:
            work, needs = left.pop(0)
            assert needs <= moved
            work()
        else:
            u, k = divmod(code, ROUNDS)
            move(u, k)
            if k == ROUNDS - 1:
                moved.add(u)
    assert not left


def forward_kernel(*refs):
    r = ForwardRefs(*refs)
    at = Place()
    h = at.h
    at.barrier(sibling=True)
    tokens = r.tok.shape[0]
    width = r.tok.shape[1]
    half = width // 2
    spans = [pl.ds(i, ROWS_AT_ONCE) for i in range(0, tokens, ROWS_AT_ONCE)]
    gather = Gather(at, lambda u: r.g_small if u == SMALL else r.g.at[u], r.send, r.recv)

    copies = [
        pltpu.make_async_copy(r.small, r.g_small.at[at.z, at.y, at.x], r.local.at[0]),
        pltpu.make_async_copy(r.blocks, r.g.at[:, at.z, at.y, at.x], r.local.at[1]),
        pltpu.make_async_copy(r.tokens, r.tok, r.local.at[2]),
        pltpu.make_async_copy(r.images, r.img, r.local.at[3]),
    ]
    for copy in copies:
        copy.start()

    keeps = []

    def keep(source, target):
        copy = pltpu.make_async_copy(source, target, r.keep.at[len(keeps)])
        keeps.append(copy)
        copy.start()

    def vector(n):
        return r.tab[pl.ds(n, 1), :]

    def own_vector(n):
        return r.tab[pl.ds(n, 1), pl.ds(pl.multiple_of(h * half, 128), half)]

    def start():
        for copy in copies[2:]:
            copy.wait()
        r.res[0] = r.tok[...].astype(jnp.float32)
        r.tab[...] = whole(r.g_small).astype(jnp.float32).T
        keep(r.tab, r.table)

    def norm(n):
        @pl.loop(0, tokens // 64, unroll=True)
        def _(i):
            rows = pl.ds(pl.multiple_of(i * 64, 64), 64)
            value, scale = norm_parts(r.res[n, rows, :])
            r.normed[rows, :] = lowest(value * vector(n) + vector(5 + n))

        keep(r.res.at[n], r.residuals.at[n])

    def quarter(l, u):
        away = (1 - h) * 2
        mine = pltpu.make_async_copy(
            r.g.at[u, pl.ds(h * 2, 2), :, :, :, pl.ds(half, half)],
            r.rowsw.at[l, :, :, :, :, pl.ds(pl.multiple_of(h * half, 128), half)],
            r.local.at[4 + l],
        )
        theirs = remote(
            r.g.at[u, pl.ds(away, 2), :, :, :, pl.ds(half, half)],
            r.rowsw.at[l, :, :, :, :, pl.ds(pl.multiple_of(h * half, 128), half)],
            r.quarter_send.at[l],
            r.quarter_recv.at[l],
            at.sibling,
        )
        return mine, theirs

    def start_quarter(l, u):
        mine, theirs = quarter(l, u)
        mine.start()
        theirs.start()

    def end_quarter(l, u):
        mine, theirs = quarter(l, u)
        mine.wait()
        theirs.wait()
        keep(r.rowsw.at[l], r.out_rows.at[l])

    def swap(e, i):
        rows = spans[i]
        return remote(
            r.give.at[e % 2, rows], r.take.at[e % 2, rows], r.swap_send.at[e, i], r.swap_recv.at[e, i], at.sibling
        )

    def offer(e, i, value):
        r.give[e % 2, spans[i], :] = lowest(value)
        swap(e, i).start()

    def join(e, i, n, bias):
        swap(e, i).wait()
        rows = spans[i]
        both = r.give[e % 2, rows, :].astype(jnp.float32) + r.take[e % 2, rows, :].astype(jnp.float32)
        r.res[n + 1, rows, :] = r.res[n, rows, :] + both + vector(5 + bias)

    def mix(l, u, query_bias, value_bias, i):
        rows = spans[i]
        value = r.normed[rows, :]
        both = mm(value, whole(r.g.at[u]))
        r.mix[l, rows, :half] = lowest(both[:, :half] + own_vector(5 + query_bias))
        r.mix[l, rows, half:width] = lowest(both[:, half:])
        r.mix[l, rows, width:] = lowest(
            mm(value, whole(r.g.at[u + 1, :, :, :, :, :half])) + own_vector(5 + value_bias)
        )

    def attend(l, blocks):
        @pl.loop(*blocks, unroll=True)
        def _(i):
            rows = pl.ds(pl.multiple_of(i * SPAN, SPAN), SPAN)
            bias = r.causal[i]
            bias = jnp.concatenate([bias, bias], axis=0)
            for j in range(half // 128):
                lanes = [pl.ds(part * half + j * 128, 128) for part in range(3)]
                queries, keys, values = [r.mix[l, rows, lane] for lane in lanes]
                scores = mm_back(two_heads(queries * SCALING), keys) + bias
                shares = lowest(softmax_of(scores, 1))
                r.att[l, rows, pl.ds(j * 128, 128)] = lowest(mm(beside(shares), two_heads(values)))

    def project_out(l, e, a, i):
        value = r.att[a, spans[i], :]
        offer(e, i, mm(value, whole(r.rowsw.at[a])))

    def up(l, u, s, i):
        rows = spans[i]
        value = mm(r.normed[rows, :], whole(r.g.at[u])) + vector(21 + 2 * l + s)
        r.hid[l, rows, pl.ds(s * width, width)] = value
        r.act[rows, pl.ds(s * width, width)] = lowest(gelu(value))

    def down(u, s, i, e):
        rows = spans[i]
        value = mm(r.act[rows, pl.ds(s * width, width)], whole(r.g.at[u]))
        if s == 0:
            r.acc[rows, :] = value
        else:
            offer(e, i, r.acc[rows, :] + value)

    def picture_pair(i):
        rows = spans[i]
        value = mm(r.img[rows, :], whole(r.g.at[9]))
        r.pr[rows, :half] = lowest(value[:, :half])
        r.pr[rows, half:] = lowest(value[:, half:] + own_vector(5 + 14))

    def cross_queries(i):
        rows = spans[i]
        r.qc[rows, :] = lowest(mm(r.normed[rows, :], whole(r.g.at[8, :, :, :, :, :half])) + own_vector(5 + 13))

    def cross(blocks):
        @pl.loop(*blocks, unroll=True)
        def _(i):
            rows = pl.ds(pl.multiple_of(i * SPAN, SPAN), SPAN)
            bias = picture_bias(r.choice[rows, :])
            bias = jnp.concatenate([bias, bias], axis=0)
            for j in range(half // 128):
                keys = r.pr[:, pl.ds(j * 128, 128)]
                values = r.pr[:, pl.ds(half + j * 128, 128)]
                scores = mm_back(two_heads(r.qc[rows, pl.ds(j * 128, 128)] * SCALING), keys) + bias
                shares = lowest(softmax_of(scores, 1))
                r.att[2, rows, pl.ds(j * 128, 128)] = lowest(mm(beside(shares), two_heads(values)))

    segments = []

    def add(needs, work, *args):
        segments.append((partial(work, *args), frozenset(needs)))

    def add_attention(l, n, u, e, biases, rest):
        add({SMALL, u, u + 1}, start_quarter, l, u + 1)
        add(rest, norm, n)
        for i in (0, 1):
            add(rest, mix, l, u, biases[0], biases[1], i)
        for i in (0, 1):
            add(rest, attend, l, (2 * i, 2 * i + 2))
        add(rest, end_quarter, l, u + 1)
        add(rest, keep, r.mix.at[l], r.mixed.at[l])
        for i in (0, 1):
            add(rest, project_out, l, e, l, i)
        add(rest, keep, r.att.at[l], r.attended.at[l])
        for i in (0, 1):
            add(rest, join, e, i, n, biases[2])

    def add_feed(l, n, u, e, bias):
        add((), norm, n)
        for s in (0, 1):
            for i in (0, 1):
                add({u + s}, up, l, u + s, s, i)
        add((), keep, r.hid.at[l], r.hidden.at[l])
        for s in (0, 1):
            for i in (0, 1):
                add({u + 2 + s}, down, u + 2 + s, s, i, e)
        if e < 4:
            for i in (0, 1):
                add((), join, e, i, n, bias)

    add({SMALL}, start)
    add_attention(0, 0, 0, 0, (5, 6, 7), ())
    add_feed(0, 1, 2, 1, 8)
    add_attention(1, 2, 6, 2, (9, 10, 11), ())
    add({9}, picture_pair, 0)
    add((), picture_pair, 1)
    add((), keep, r.pr, r.pair)
    add({8}, start_quarter, 2, 8)
    add((), norm, 3)
    for i in (0, 1):
        add((), cross_queries, i)
    add((), keep, r.qc, r.queries)
    for i in range(4):
        add((), cross, (i, i + 1))
    add((), end_quarter, 2, 8)
    for i in (0, 1):
        add((), project_out, 2, 3, 2, i)
    add((), keep, r.att.at[2], r.attended.at[2])
    for i in (0, 1):
        add((), join, 3, i, 3, 15)
    add_feed(1, 4, 10, 4, 12)

    for copy in copies[:2]:
        copy.wait()

    def move(u, k):
        gather.round(u, k)
        if k == ROUNDS - 1 and u != SMALL:
            keep(r.g.at[u], r.full.at[u])

    play(GATHER_ORDER, segments, move)
    for i in (0, 1):
        swap(4, i).wait()
    mine = pl.ds(pl.multiple_of(h * ROWS_AT_ONCE, ROWS_AT_ONCE), ROWS_AT_ONCE)
    both = r.give[0, mine, :].astype(jnp.float32) + r.take[0, mine, :].astype(jnp.float32)
    r.layer_out[...] = r.res[4, mine, :] + both + vector(5 + 12)
    for u in range(UNITS + 1):
        gather.drain(u)
    for copy in keeps:
        copy.wait()


def forward(blocks, small, tokens, images, causal, choice):
    units, rows, width = blocks.shape
    count = tokens.shape[0]
    half = width // 2
    bf, fl = jnp.bfloat16, jnp.float32
    shape = jax.ShapeDtypeStruct
    dma = pltpu.SemaphoreType.DMA
    outs = (
        shape((units, 4, 2, 2, rows, width), bf),
        shape((128, width), fl),
        shape((5, count, width), fl),
        shape((2, count, width + half), bf),
        shape((3, count, half), bf),
        shape((count, half), bf),
        shape((count, width), bf),
        shape((2, count, 2 * width), fl),
        shape((3, 2, 2, 2, rows, width), bf),
        shape((count // 2, width), fl),
    )
    anywhere, here = pl.BlockSpec(memory_space=pl.ANY), pl.BlockSpec(memory_space=pltpu.VMEM)
    return pl.pallas_call(
        forward_kernel,
        out_shape=outs,
        in_specs=[anywhere] * 4 + [here] * 2,
        out_specs=[anywhere] * 9 + [here],
        scratch_shapes=[
            pltpu.VMEM((units, 4, 2, 2, rows, width), bf),
            pltpu.VMEM((4, 2, 2) + small.shape, bf),
            pltpu.VMEM((128, width), fl),
            pltpu.VMEM((5, count, width), fl),
            pltpu.VMEM((count, width), bf),
            pltpu.VMEM((2, count, width + half), bf),
            pltpu.VMEM((3, count, half), bf),
            pltpu.VMEM((count, half), bf),
            pltpu.VMEM((count, width), bf),
            pltpu.VMEM((2, count, 2 * width), fl),
            pltpu.VMEM((count, 2 * width), bf),
            pltpu.VMEM((count, width), fl),
            pltpu.VMEM((2, count, width), bf),
            pltpu.VMEM((2, count, width), bf),
            pltpu.VMEM((count, width), bf),
            pltpu.VMEM((count, width), bf),
            pltpu.VMEM((3, 2, 2, 2, rows, width), bf),
            dma((units + 1, 8)),
            dma((units + 1, 8)),
            dma((8,)),
            dma((5, 2)),
            dma((5, 2)),
            dma((3,)),
            dma((3,)),
            dma((40,)),
        ],
        compiler_params=pltpu.CompilerParams(collective_id=0, has_side_effects=True, vmem_limit_bytes=60 << 20),
    )(blocks, small, tokens, images, causal, choice)


BACK_UNITS = (12, 13, 10, 11, 9, 8, 6, 7, 4, 5, 2, 3, 0, 1, SMALL)
OUT_UNITS = (8, 7, 1)


def gelu_parts(value):
    square = value * value
    bent = jnp.tanh(value * (GELU_A + (GELU_A * GELU_B) * square))
    rise = 0.5 + 0.5 * bent
    slope = rise + (0.5 * value) * (1.0 - bent * bent) * (GELU_A + (3.0 * GELU_A * GELU_B) * square)
    return value * rise, slope


def backward_kernel(*refs, pick, spares):
    named = len(BackRefs._fields)
    r = BackRefs(*refs[:named])
    spare = pick(refs[named:])
    at = Place()
    h = at.h
    at.barrier(sibling=True)
    tokens, width = r.branch.shape
    half = width // 2
    spans = [pl.ds(i, ROWS_AT_ONCE) for i in range(0, tokens, ROWS_AT_ONCE)]
    mine = pl.ds(pl.multiple_of(h * ROWS_AT_ONCE, ROWS_AT_ONCE), ROWS_AT_ONCE)
    others = pl.ds(pl.multiple_of((1 - h) * ROWS_AT_ONCE, ROWS_AT_ONCE), ROWS_AT_ONCE)
    own_lanes = pl.ds(pl.multiple_of(h * half, 128), half)
    other_lanes = pl.ds(pl.multiple_of((1 - h) * half, 128), half)
    scatter = Scatter(at, lambda u: r.small if u == SMALL else r.g.at[u], spare, r.send, r.recv)

    loads = {}

    def fetch(name, source, target):
        copy = pltpu.make_async_copy(source, target, r.load.at[len(loads)])
        loads[name] = copy
        copy.start()

    def need(name):
        copy = loads[name]
        if copy is not None:
            copy.wait()
            loads[name] = None

    def fetch_unit(u):
        if u in OUT_UNITS:
            fetch(("g", u), r.full.at[u, :, :, :, :, pl.ds(0, half)], r.g.at[u, :, :, :, :, pl.ds(0, half)])
        else:
            fetch(("g", u), r.full.at[u], r.g.at[u])

    def fetch_residual(n, slot):
        fetch(("res", n), r.residuals.at[n], r.res.at[slot])

    def fetch_hidden(l):
        for s in (0, 1):
            fetch(("hid", l, s), r.hidden.at[l, :, pl.ds(s * width, width)], r.hid.at[s])

    def fetch_mixed(l):
        fetch(("mix", l), r.mixed.at[l], r.mix)

    fetch("table", r.table, r.tab)
    fetch("cotangent", r.cotangent, r.branch)
    fetch_unit(12)
    fetch_hidden(1)
    fetch_unit(13)
    fetch_residual(4, 0)
    fetch_unit(10)
    fetch_unit(11)
    fetch("rows", r.out_rows, r.rowsw)
    fetch("queries", r.queries, r.qc)
    fetch("pair", r.pair, r.pr)
    fetch_residual(3, 1)
    fetch("attended", r.attended, r.att)
    fetch("images", r.images, r.img)
    for u in (9, 8):
        fetch_unit(u)
    fetch_mixed(1)
    for u in (6, 7, 4, 5, 2, 3, 0, 1):
        fetch_unit(u)

    def vector(n):
        return r.tab[pl.ds(n, 1), :]

    def add_row(n, value):
        r.sums[pl.ds(n, 1), :] += jnp.sum(value, axis=0, keepdims=True)

    def add_own(n, value):
        r.sums[pl.ds(n, 1), own_lanes] += jnp.sum(value, axis=0, keepdims=True)

    def start():
        need("cotangent")
        r.sums[...] = jnp.zeros_like(r.sums)
        r.dx[...] = r.branch[...].astype(jnp.float32)

    def norm(n, slot):
        need(("res", n))
        need("table")

        @pl.loop(0, tokens // 64, unroll=True)
        def _(i):
            rows = pl.ds(pl.multiple_of(i * 64, 64), 64)
            value, scale = norm_parts(r.res[slot, rows, :])
            r.res[slot, rows, :] = value
            r.scale[rows, :] = scale
            r.normed[rows, :] = lowest(value * vector(n) + vector(5 + n))

    def begin_branch(bias):
        @pl.loop(0, tokens // 64, init_carry=jnp.zeros((1, width), jnp.float32), unroll=True)
        def total(i, carry):
            rows = pl.ds(pl.multiple_of(i * 64, 64), 64)
            value = lowest(r.dx[rows, :])
            r.branch[rows, :] = value
            return carry + jnp.sum(value.astype(jnp.float32), axis=0, keepdims=True)

        r.sums[pl.ds(5 + bias, 1), :] = total

    def swap(e, i):
        rows = spans[i]
        return remote(
            r.give.at[e % 2, rows], r.take.at[e % 2, rows], r.swap_send.at[e, i], r.swap_recv.at[e, i], at.sibling
        )

    def offer(e, i, value):
        r.give[e % 2, spans[i], :] = lowest(value)
        swap(e, i).start()

    def join(e, i, n, slot):
        swap(e, i).wait()
        base = i * ROWS_AT_ONCE
        gain = vector(n)
        zero = jnp.zeros((1, width), jnp.float32)

        @pl.loop(0, ROWS_AT_ONCE // 64, init_carry=(zero, zero), unroll=True)
        def totals(k, carry):
            rows = pl.ds(pl.multiple_of(base + k * 64, 64), 64)
            given = r.give[e % 2, rows, :].astype(jnp.float32) + r.take[e % 2, rows, :].astype(jnp.float32)
            value = r.res[slot, rows, :]
            product = given * value
            scaled = given * gain
            first = jnp.mean(scaled, axis=1, keepdims=True)
            second = jnp.mean(product * gain, axis=1, keepdims=True)
            r.dx[rows, :] += r.scale[rows, :] * (scaled - first - value * second)
            return (
                carry[0] + jnp.sum(product, axis=0, keepdims=True),
                carry[1] + jnp.sum(given, axis=0, keepdims=True),
            )

        r.sums[pl.ds(n, 1), :] += totals[0]
        r.sums[pl.ds(5 + n, 1), :] += totals[1]

    def store_rows(u, part, value, lanes=slice(None)):
        value = lowest(value)
        r.g[u, 2 * part : 2 * part + 2, :, :, :, lanes] = value.reshape((2, 2, 2, -1) + value.shape[1:])

    def feed_hidden(l, u, s, i):
        need(("g", u))
        need(("hid", l, s))
        rows, lanes = spans[i], pl.ds(s * width, width)
        back = mm_back(r.branch[rows, :], whole(r.g.at[u]))
        active, slope = gelu_parts(r.hid[s, rows, :])
        value = lowest(back * slope)
        r.act[rows, lanes] = lowest(active)
        r.dhid[rows, lanes] = value
        add_row(21 + 2 * l + s, value.astype(jnp.float32))

    def feed_down(u, s, part):
        lanes = pl.ds(s * width + part * half, half)
        store_rows(u, part, mm_rows(r.act[:, lanes], r.branch[...]))

    def feed_normed(u, i, e):
        need(("g", u))
        need(("g", u + 1))
        rows = spans[i]
        value = mm_back(r.dhid[rows, :width], whole(r.g.at[u]))
        offer(e, i, value + mm_back(r.dhid[rows, width:], whole(r.g.at[u + 1])))

    def feed_up(u, s, part):
        lanes = pl.ds(s * width, width)
        store_rows(u, part, mm_rows(r.normed[:, pl.ds(part * half, half)], r.dhid[:, lanes]))

    def attended_back(a, i):
        need("rows")
        r.datt[spans[i], :] = lowest(mm_back(r.branch[spans[i], :], whole(r.rowsw.at[a])))

    def near_copy(a, u):
        return pltpu.make_async_copy(
            r.og.at[:, :, :, :, own_lanes],
            r.g.at[u, pl.ds(2 * h, 2), :, :, :, pl.ds(half, half)],
            r.quarter_local.at[a],
        )

    def far_copy(a, u, rows_of):
        return remote(
            r.og.at[:, :, :, :, other_lanes],
            r.g.at[u, pl.ds(2 * rows_of, 2), :, :, :, pl.ds(half, half)],
            r.quarter_send.at[a],
            r.quarter_recv.at[a],
            at.sibling,
        )

    def out_gradient(a, u):
        need("attended")
        value = lowest(mm_rows(r.att[a], r.branch[...]))
        r.og[...] = value.reshape(r.og.shape)
        near_copy(a, u).start()
        far_copy(a, u, h).start()

    def end_quarter(a, u):
        near_copy(a, u).wait()
        far_copy(a, u, h).wait_send()
        far_copy(a, u, 1 - h).wait_recv()


    def attend_back(l, blocks):
        need(("mix", l))

        @pl.loop(*blocks, unroll=True)
        def _(b):
            rows = pl.ds(pl.multiple_of(b * SPAN, SPAN), SPAN)
            bias = r.causal[b].T
            bias = jnp.concatenate([bias, bias], axis=1)
            for j in range(half // 128):
                lanes = [pl.ds(part * half + j * 128, 128) for part in range(3)]
                queries, keys, values = [r.mix[rows, lane] for lane in lanes]
                queries = two_heads(queries * SCALING)
                given = two_heads(r.datt[rows, pl.ds(j * 128, 128)])
                shares = softmax_of(mm_back(keys, queries) + bias, 0)
                share_adjoint = mm_back(values, given)
                score_adjoint = lowest(shares * (share_adjoint - jnp.sum(shares * share_adjoint, axis=0, keepdims=True)))
                r.dhid[rows, lanes[0]] = lowest(mm_rows(below(score_adjoint), two_heads(keys * SCALING)))
                r.dhid[rows, lanes[1]] = lowest(mm(score_adjoint, queries))
                r.dhid[rows, lanes[2]] = lowest(mm(lowest(shares), given))

    def mixed_normed(u, e, i, biases):
        need(("g", u))
        need(("g", u + 1))
        rows = spans[i]
        value = mm_back(r.dhid[rows, :width], whole(r.g.at[u]))
        value += mm_back(r.dhid[rows, pl.ds(width, half)], whole(r.g.at[u + 1, :, :, :, :, pl.ds(0, half)]))
        offer(e, i, value)

    def mixed_sums(biases):
        add_own(5 + biases[0], r.dhid[:, :half].astype(jnp.float32))
        add_own(5 + biases[1], r.dhid[:, pl.ds(width, half)].astype(jnp.float32))

    def mixed_gradient(u, part):
        store_rows(u, part, mm_rows(r.normed[:, pl.ds(part * half, half)], r.dhid[:, :width]))

    def value_gradient(u, part):
        value = mm_rows(r.normed[:, pl.ds(part * half, half)], r.dhid[:, pl.ds(width, half)])
        store_rows(u, part, value, pl.ds(0, half))

    def cross_back(b):
        need("queries")
        need("pair")
        rows = pl.ds(b * SPAN, SPAN)
        bias = picture_bias(r.choice[rows, :]).T
        bias = jnp.concatenate([bias, bias], axis=1)
        for j in range(half // 128):
            lanes = pl.ds(j * 128, 128)
            value_lanes = pl.ds(half + j * 128, 128)
            keys, values = r.pr[:, lanes], r.pr[:, value_lanes]
            queries = two_heads(r.qc[rows, lanes] * SCALING)
            given = two_heads(r.datt[rows, lanes])
            shares = softmax_of(mm_back(keys, queries) + bias, 0)
            share_adjoint = mm_back(values, given)
            score_adjoint = lowest(shares * (share_adjoint - jnp.sum(shares * share_adjoint, axis=0, keepdims=True)))
            r.act[rows, lanes] = lowest(mm_rows(below(score_adjoint), two_heads(keys * SCALING)))
            key_adjoint = mm(score_adjoint, queries)
            value_adjoint = mm(lowest(shares), given)
            if b == 0:
                r.hid[0, :, lanes] = key_adjoint
                r.hid[0, :, value_lanes] = value_adjoint
            else:
                r.hid[0, :, lanes] += key_adjoint
                r.hid[0, :, value_lanes] += value_adjoint

    def pair_adjoint():
        r.dhid[:, :width] = lowest(r.hid[0])
        add_own(5 + 13, r.act[:, :half].astype(jnp.float32))
        add_own(5 + 14, r.dhid[:, pl.ds(half, half)].astype(jnp.float32))

    def query_normed(e, i):
        need(("g", 8))
        offer(e, i, mm_back(r.act[spans[i], pl.ds(0, half)], whole(r.g.at[8, :, :, :, :, pl.ds(0, half)])))

    def query_gradient(part):
        value = mm_rows(r.normed[:, pl.ds(part * half, half)], r.act[:, pl.ds(0, half)])
        store_rows(8, part, value, pl.ds(0, half))

    def pic_swap():
        return remote(r.pic_give, r.pic_take, r.swap_send.at[5, 0], r.swap_recv.at[5, 0], at.sibling)

    def picture_back():
        need(("g", 9))
        r.pic_give[...] = lowest(mm_back(r.dhid[others, pl.ds(0, width)], whole(r.g.at[9])))
        pic_swap().start()

    def picture_own():
        r.hid[1, pl.ds(0, ROWS_AT_ONCE), :] = mm_back(r.dhid[mine, pl.ds(0, width)], whole(r.g.at[9]))

    def picture_copy():
        return pltpu.make_async_copy(r.hid.at[1, pl.ds(0, ROWS_AT_ONCE)], r.image_out, r.store.at[UNITS])

    def picture_join():
        pic_swap().wait()
        r.hid[1, pl.ds(0, ROWS_AT_ONCE), :] += r.pic_take[...].astype(jnp.float32)
        picture_copy().start()

    def pair_gradient(part):
        need("images")
        store_rows(9, part, mm_rows(r.img[:, pl.ds(part * half, half)], r.dhid[:, pl.ds(0, width)]))

    def picture_end():
        picture_copy().wait()
        fetch_hidden(0)

    def small_total():
        r.small[...] = r.sums[...].T.reshape(r.small.shape)

    def token_copy():
        return pltpu.make_async_copy(r.dx.at[mine], r.token_out, r.store.at[UNITS + 1])

    segments, ready = [], set()

    def add(work, *args, finished=()):
        def step():
            work(*args)
            ready.update(finished)

        segments.append((step, frozenset()))

    def add_feed(l, n, slot, u, e, bias, after):
        add(begin_branch, bias)
        for s in (0, 1):
            for i in (0, 1):
                add(feed_hidden, l, u + 2 + s, s, i)
            for part in (0, 1):
                add(feed_down, u + 2 + s, s, part, finished=(u + 2 + s,) if part else ())
        for i in (0, 1):
            add(feed_normed, u, i, e)
        add(norm, n, slot)
        for s in (0, 1):
            for part in (0, 1):
                add(feed_up, u + s, s, part, finished=(u + s,) if part else ())
        for i in (0, 1):
            add(join, e, i, n, slot)
        for work in after:
            add(*work)

    def add_attention(l, n, slot, u, e, biases, after):
        add(begin_branch, biases[2])
        for i in (0, 1):
            add(attended_back, l, i)
        add(out_gradient, l, u + 1)
        add(attend_back, l, (0, 2))
        add(attend_back, l, (2, 4))
        for i in (0, 1):
            add(mixed_normed, u, e, i, biases)
        add(norm, n, slot)
        for part in (0, 1):
            add(mixed_gradient, u, part, finished=(u,) if part else ())
        for part in (0, 1):
            add(value_gradient, u + 1, part)
        add(end_quarter, l, u + 1, finished=(u + 1,))
        add(mixed_sums, biases)
        for i in (0, 1):
            add(join, e, i, n, slot)
        for work in after:
            add(*work)

    add(start)
    add_feed(1, 4, 0, 10, 0, 12, [(fetch_residual, 2, 0)])
    add(begin_branch, 15)
    for i in (0, 1):
        add(attended_back, 2, i)
    add(out_gradient, 2, 8)
    for b in range(tokens // SPAN):
        add(cross_back, b)
    add(pair_adjoint)
    for i in (0, 1):
        add(query_normed, 1, i)
    add(picture_back)
    add(picture_own)
    for part in (0, 1):
        add(pair_gradient, part, finished=(9,) if part else ())
    add(norm, 3, 1)
    for part in (0, 1):
        add(query_gradient, part)
    add(end_quarter, 2, 8, finished=(8,))
    for i in (0, 1):
        add(join, 1, i, 3, 1)
    add(picture_join)
    add(fetch_residual, 1, 1)
    add_attention(1, 2, 0, 6, 2, (9, 10, 11), [(picture_end,), (fetch_residual, 0, 0), (fetch_mixed, 0)])
    add_feed(0, 1, 1, 2, 3, 8, [])
    add_attention(0, 0, 0, 0, 4, (5, 6, 7), [])
    add(small_total, finished=(SMALL,))
    add(lambda: token_copy().start())

    def end_unit(u):
        if u == SMALL:
            r.small_out[...] = r.small[at.z, at.y, at.x]
        else:
            pltpu.make_async_copy(r.g.at[u, at.z, at.y, at.x], r.sums_out.at[u], r.store.at[u]).start()

    def move(u, k):
        assert u in ready
        scatter.round(u, k, end_unit)

    play(SCATTER_ORDER, segments, move)
    for u in BACK_UNITS:
        scatter.drain(u)
        if u != SMALL:
            pltpu.make_async_copy(r.g.at[u, at.z, at.y, at.x], r.sums_out.at[u], r.store.at[u]).wait()
    token_copy().wait()


def backward(full, table, residuals, mixed, attended, queries, pair, hidden, out_rows, cotangent, images, causal, choice):
    units, rows, width = full.shape[0], full.shape[4], full.shape[5]
    count = cotangent.shape[0]
    half = width // 2
    bf, fl = jnp.bfloat16, jnp.float32
    shape = jax.ShapeDtypeStruct
    dma = pltpu.SemaphoreType.DMA
    shapes, pick = spare_shapes(rows, width, 128)
    anywhere, here = pl.BlockSpec(memory_space=pl.ANY), pl.BlockSpec(memory_space=pltpu.VMEM)
    return pl.pallas_call(
        partial(backward_kernel, pick=pick, spares=len(shapes)),
        out_shape=(
            shape((units, rows, width), bf),
            shape((rows, 128), fl),
            shape((count // 2, width), fl),
            shape((count // 2, width), fl),
        ),
        in_specs=[anywhere] * 11 + [here] * 2,
        out_specs=[anywhere, here, anywhere, anywhere],
        scratch_shapes=[
            pltpu.VMEM(full.shape, bf),
            pltpu.VMEM((128, width), fl),
            pltpu.VMEM((count, width), fl),
            pltpu.VMEM((count, width), bf),
            pltpu.VMEM((2, count, width), fl),
            pltpu.VMEM((count, 1), fl),
            pltpu.VMEM((count, width), bf),
            pltpu.VMEM((2, count, width), fl),
            pltpu.VMEM((count, 2 * width), bf),
            pltpu.VMEM((count, 2 * width), bf),
            pltpu.VMEM((count, width + half), bf),
            pltpu.VMEM((3, count, half), bf),
            pltpu.VMEM((count, half), bf),
            pltpu.VMEM((count, half), bf),
            pltpu.VMEM((count, width), bf),
            pltpu.VMEM(out_rows.shape, bf),
            pltpu.VMEM((count, width), bf),
            pltpu.VMEM((2, count, width), bf),
            pltpu.VMEM((2, count, width), bf),
            pltpu.VMEM((count // 2, width), bf),
            pltpu.VMEM((count // 2, width), bf),
            pltpu.VMEM(out_rows.shape[1:], bf),
            pltpu.VMEM((128, width), fl),
            pltpu.VMEM((4, 2, 2, rows, 128), fl),
            dma((units + 1, 8)),
            dma((units + 1, 8)),
            dma((6, 2)),
            dma((6, 2)),
            dma((3,)),
            dma((3,)),
            dma((3,)),
            dma((40,)),
            dma((units + 2,)),
            *shapes,
        ],
        compiler_params=pltpu.CompilerParams(collective_id=1, has_side_effects=True, vmem_limit_bytes=63 << 20),
    )(full, table, residuals, mixed, attended, queries, pair, hidden, out_rows, cotangent, images, causal, choice)


def swap_cores(value):
    return lax.ppermute(value, "heads", [(0, 1), (1, 0)])


def both_cores(value, member):
    other = swap_cores(value)
    return jnp.stack([jnp.where(member == 0, value, other), jnp.where(member == 0, other, value)])


def to_units(member, self_weight, self_out_weight, up_weight, query_weight, pair_weight, cross_out_weight):
    width = self_weight.shape[1 + 1] // 3
    half = width // 2
    rows = self_weight.shape[1]
    own = slice(member * half, member * half + half)
    value = slice(width + member * half, width + member * half + half)
    units = []
    for layer in (0, 1):
        weight = self_weight[layer]
        units.append(jnp.concatenate([weight[:, own], weight[:, value]], axis=1))
        units.append(jnp.concatenate([weight[:, 2 * width + member * half : 2 * width + member * half + half], self_out_weight[layer][:, own]], axis=1))
        up = up_weight[layer].reshape(rows, CHIPS, 2, 2, -1)[:, :, member]
        units.append(up[:, :, 0].reshape(rows, width))
        units.append(up[:, :, 1].reshape(rows, width))
    units.append(jnp.concatenate([query_weight[:, own], cross_out_weight[:, own]], axis=1))
    units.append(jnp.concatenate([pair_weight[:, own], pair_weight[:, value]], axis=1))
    return jnp.stack(units)


UNIT_OF_PIECE = (0, 1, 2, 3, 6, 7, 10, 11, 8, 9)


def chip_blocks(member, pieces, down_weight):
    theirs, ours = (
        jnp.where(member == 0, pieces[1], pieces[0]),
        jnp.where(member == 0, pieces[0], pieces[1]),
    )
    rows = jnp.concatenate(list(both_rows(member, ours, swap_cores(theirs))), axis=1)
    down = down_weight.reshape(2, 2, rows.shape[1], rows.shape[2])
    order = {u: rows[i] for i, u in enumerate(UNIT_OF_PIECE)}
    order.update({4: down[0, 0], 5: down[0, 1], 12: down[1, 0], 13: down[1, 1]})
    return jnp.stack([order[u] for u in range(UNITS)])


def both_rows(member, ours, other):
    return jnp.where(member == 0, ours, other), jnp.where(member == 0, other, ours)


def chip_program(
    tokens,
    images,
    segment_labels,
    image_index,
    cotangent,
    norm_gain,
    vector_bias,
    up_bias,
    self_weight,
    self_out_weight,
    up_weight,
    down_weight,
    query_weight,
    pair_weight,
    cross_out_weight,
):
    member = lax.axis_index("heads")
    rows, length, width = tokens.shape
    half = width // 2
    slim = self_weight.shape[1]
    matrices = (self_weight, self_out_weight, up_weight, query_weight, pair_weight, cross_out_weight)
    blocks = chip_blocks(member, [to_units(m, *matrices) for m in (0, 1)], down_weight)
    vectors = jnp.concatenate([norm_gain, vector_bias], axis=0)
    vectors = jnp.concatenate(list(both_cores(vectors, member)), axis=1)
    vectors = jnp.concatenate([vectors, up_bias.reshape(4, 2 * slim)], axis=0)
    small = jnp.pad(vectors, ((0, 128 - vectors.shape[0]), (0, 0))).T
    carried = both_cores(jnp.stack([tokens.reshape(-1, width), images.reshape(-1, width), cotangent.reshape(-1, width)]), member)
    carried = carried.transpose(1, 0, 2, 3).reshape(3, -1, width)
    pictures = carried[1]
    chip_rows = segment_labels.shape[0]
    labels = jnp.arange(image_index.shape[1])
    caption_image = jnp.sum(
        jnp.where(segment_labels[:, :, None] == labels[None, None, :], image_index[:, None, :], 0), axis=-1, dtype=jnp.int32
    )
    count = chip_rows * length
    span_rows = SPAN // length
    row_of = jnp.arange(SPAN) // length
    same = row_of[:, None] == row_of[None, :]
    span_labels = segment_labels.reshape(-1, SPAN)
    causal = (span_labels[:, :, None] == span_labels[:, None, :]) & (same & (jnp.arange(SPAN)[:, None] >= jnp.arange(SPAN)[None, :]))[None]
    causal = jnp.where(causal, 0.0, masked_score).astype(jnp.float32)
    choice = jnp.broadcast_to(caption_image.reshape(count, 1).astype(jnp.float32), (count, 128))
    full, table, residuals, mixed, attended, queries, pair, hidden, out_rows, layer_out = forward(
        blocks, small, carried[0], carried[1], causal, choice
    )
    sums, small_sums, token_gradient, image_gradient = backward(
        full, table, residuals, mixed, attended, queries, pair, hidden, out_rows, carried[2], carried[1], causal, choice
    )
    outs = finish(member, sums.astype(jnp.float32), small_sums, slim, width)
    mine = (layer_out.reshape(rows, length, width), token_gradient.reshape(rows, length, width), image_gradient[None])
    return mine + outs


def finish(member, sums, small_sums, slim, width):
    half = width // 2
    pieces = jnp.stack([sums[u] for u in UNIT_OF_PIECE]).reshape(len(UNIT_OF_PIECE), 2, slim, width)
    ours, theirs = pieces[:, member], pieces[:, 1 - member]
    both = jnp.stack(list(both_rows(member, ours, swap_cores(theirs))))

    def halves(piece, side):
        return jnp.concatenate([both[0, piece][:, side * half : (side + 1) * half], both[1, piece][:, side * half : (side + 1) * half]], axis=1)

    def up(piece):
        parts = [both[:, piece + s].reshape(2, slim, CHIPS, 2 * slim) for s in (0, 1)]
        return jnp.stack(parts, axis=0).transpose(2, 3, 1, 0, 4).reshape(slim, 4 * width)

    self_weight = jnp.stack([jnp.concatenate([halves(p, 0), halves(p, 1), halves(p + 1, 0)], axis=1) for p in (0, 4)])
    self_out = jnp.stack([halves(p, 1) for p in (1, 5)])
    up_gradient = jnp.stack([up(2), up(6)])
    down = jnp.stack([jnp.concatenate([sums[u], sums[u + 1]]) for u in (4, 12)])
    pair = jnp.concatenate([halves(9, 0), halves(9, 1)], axis=1)
    table = small_sums.T
    shared = table[:21]
    other = swap_cores(shared)
    split = jnp.zeros((21, 1), bool).at[jnp.array([5 + n for n in (5, 6, 9, 10, 13, 14)])].set(True)
    shared = jnp.where(split, shared + other, shared)
    shared = lax.dynamic_slice_in_dim(shared, member * slim, slim, 1)
    up_bias = table[21:25].reshape(2, 4 * slim)
    return (shared[:5], shared[5:], up_bias, self_weight, self_out, up_gradient, down, halves(8, 0), pair, halves(8, 1))


def solution(mesh):
    in_specs = (
        P(("dp", "heads"), None, None),
        P(("dp", "heads"), None, None),
        P("dp", None),
        P("dp", None),
        P(("dp", "heads"), None, None),
        P(None, ("dp", "heads")),
        P(None, ("dp", "heads")),
        P(None, ("dp", "heads")),
        P(None, ("dp", "heads"), None),
        P(None, ("dp", "heads"), None),
        P(None, ("dp", "heads"), None),
        P(None, ("dp", "heads"), None),
        P(("dp", "heads"), None),
        P(("dp", "heads"), None),
        P(("dp", "heads"), None),
    )
    out_specs = (
        P(("dp", "heads"), None, None),
        P(("dp", "heads"), None, None),
        P(("dp", "heads"), None, None),
        P(None, ("dp", "heads")),
        P(None, ("dp", "heads")),
        P(None, ("dp", "heads")),
        P(None, ("dp", "heads"), None),
        P(None, ("dp", "heads"), None),
        P(None, ("dp", "heads"), None),
        P(None, ("dp", "heads"), None),
        P(("dp", "heads"), None),
        P(("dp", "heads"), None),
        P(("dp", "heads"), None),
    )
    dp, cores = mesh.shape["dp"], mesh.shape["heads"]
    program = chip_program if (dp, cores) == (CHIPS, 2) else per_device
    return jax.shard_map(
        program, mesh=mesh, in_specs=in_specs, out_specs=out_specs, check_vma=False
    )
```

```python
from functools import partial
import math
from typing import Any, NamedTuple

import jax
import jax.numpy as jnp
from jax import lax
from jax.experimental import pallas as pl
from jax.experimental.pallas import tpu as pltpu
from jax.sharding import PartitionSpec as P

HEADS = 12
HEAD = 64


masked_score = -1e30


def layer_norm(residual, gain, shift):
    center = residual - jnp.mean(residual, axis=-1, keepdims=True)
    variance = jnp.mean(center * center, axis=-1, keepdims=True)
    return center * lax.rsqrt(variance + 1e-05) * gain + shift


def project(left, weight):
    return jnp.einsum("rld,de->rle", left, weight, preferred_element_type=jnp.float32)


def weight_adjoint(left, adjoint):
    return jnp.einsum("rld,rle->de", left, adjoint, preferred_element_type=jnp.float32)


def project_back(adjoint, weight):
    return jnp.einsum("rle,de->rld", adjoint, weight, preferred_element_type=jnp.float32)


def column_total(adjoint):
    return jnp.sum(adjoint, axis=(0, 1), dtype=jnp.float32)


def norm_back(residual, gain, shift, adjoint):
    unused, pull = jax.vjp(layer_norm, residual, gain, shift)
    return pull(adjoint)


def rows_to_heads(pieces):
    return lax.all_to_all(pieces, "heads", split_axis=3, concat_axis=0, tiled=True)


def heads_to_rows(pieces):
    return lax.all_to_all(pieces, "heads", split_axis=0, concat_axis=3, tiled=True)


def adjoint_to_heads(pieces):
    return lax.all_to_all(pieces, "heads", split_axis=3, concat_axis=0, tiled=True)


def adjoint_to_rows(pieces):
    return lax.all_to_all(pieces, "heads", split_axis=0, concat_axis=3, tiled=True)


def softmax_parts(scores):
    peak = jnp.max(scores, axis=-1, keepdims=True)
    log_total = peak + jnp.log(jnp.sum(jnp.exp(scores - peak), axis=-1, keepdims=True))
    return (jnp.exp(scores - log_total), log_total)


def softmax_back(shares, adjoint):
    return (shares * (adjoint - jnp.sum(shares * adjoint, axis=-1, keepdims=True))).astype(
        jnp.bfloat16
    )


def self_scores(queries, keys, allowed):
    scores = jnp.einsum(
        "rqhd,rkhd->rhqk", queries, keys, preferred_element_type=jnp.float32
    ) * HEAD ** (-0.5)
    return jnp.where(allowed[:, None], scores, masked_score)


def self_heads_forward(queries, keys, values, allowed):
    shares, log_total = softmax_parts(self_scores(queries, keys, allowed))
    attended = jnp.einsum(
        "rhqk,rkhd->rqhd", shares.astype(jnp.bfloat16), values, preferred_element_type=jnp.float32
    )
    return (attended.astype(jnp.bfloat16), log_total)


def self_heads_back(queries, keys, values, allowed, log_total, adjoint):
    shares = jnp.exp(self_scores(queries, keys, allowed) - log_total)
    value_adjoint = jnp.einsum(
        "rhqk,rqhd->rkhd", shares.astype(jnp.bfloat16), adjoint, preferred_element_type=jnp.float32
    )
    share_adjoint = jnp.einsum(
        "rqhd,rkhd->rhqk", adjoint, values, preferred_element_type=jnp.float32
    )
    score_adjoint = softmax_back(shares, share_adjoint)
    scale = HEAD ** (-0.5)
    query_adjoint = (
        jnp.einsum("rhqk,rkhd->rqhd", score_adjoint, keys, preferred_element_type=jnp.float32)
        * scale
    )
    key_adjoint = (
        jnp.einsum("rhqk,rqhd->rkhd", score_adjoint, queries, preferred_element_type=jnp.float32)
        * scale
    )
    return (
        query_adjoint.astype(jnp.bfloat16),
        key_adjoint.astype(jnp.bfloat16),
        value_adjoint.astype(jnp.bfloat16),
    )


def cross_scores(queries, image_keys, chosen):
    rows, length, heads, head_size = queries.shape
    scores = jnp.einsum(
        "rqhd,gkhd->rhqgk", queries, image_keys, preferred_element_type=jnp.float32
    ) * HEAD ** (-0.5)
    scores = jnp.where(chosen[:, None, :, :, None], scores, masked_score)
    return scores.reshape(rows, heads, length, -1)


def block_rows(rows, length):
    return math.gcd(rows, max(1, 512 // length))


def cross_heads_forward(queries, image_keys, image_values, chosen):
    rows, length, heads, head_size = queries.shape
    block = block_rows(rows, length)
    flat_values = image_values.reshape(-1, heads, head_size)

    def one_block(inputs):
        block_queries, block_chosen = inputs
        shares, log_total = softmax_parts(cross_scores(block_queries, image_keys, block_chosen))
        attended = jnp.einsum(
            "rhqc,chd->rqhd",
            shares.astype(jnp.bfloat16),
            flat_values,
            preferred_element_type=jnp.float32,
        )
        return (attended.astype(jnp.bfloat16), log_total)

    blocked = (
        queries.reshape(rows // block, block, length, heads, head_size),
        chosen.reshape(rows // block, block, length, -1),
    )
    attended, log_total = lax.map(one_block, blocked)
    return (attended.reshape(queries.shape), log_total)


def cross_heads_back(queries, image_keys, image_values, chosen, log_total, adjoint):
    rows, length, heads, head_size = queries.shape
    block = block_rows(rows, length)
    flat_keys = image_keys.reshape(-1, heads, head_size)
    flat_values = image_values.reshape(-1, heads, head_size)
    scale = HEAD ** (-0.5)

    def one_block(carry, inputs):
        key_total, value_total = carry
        block_queries, block_chosen, block_log, block_adjoint = inputs
        shares = jnp.exp(cross_scores(block_queries, image_keys, block_chosen) - block_log)
        value_total = value_total + jnp.einsum(
            "rhqc,rqhd->chd",
            shares.astype(jnp.bfloat16),
            block_adjoint,
            preferred_element_type=jnp.float32,
        )
        share_adjoint = jnp.einsum(
            "rqhd,chd->rhqc", block_adjoint, flat_values, preferred_element_type=jnp.float32
        )
        score_adjoint = softmax_back(shares, share_adjoint)
        key_total = (
            key_total
            + jnp.einsum(
                "rhqc,rqhd->chd", score_adjoint, block_queries, preferred_element_type=jnp.float32
            )
            * scale
        )
        query_adjoint = (
            jnp.einsum(
                "rhqc,chd->rqhd", score_adjoint, flat_keys, preferred_element_type=jnp.float32
            )
            * scale
        )
        return ((key_total, value_total), query_adjoint.astype(jnp.bfloat16))

    start = jnp.zeros(flat_keys.shape, jnp.float32)
    blocked = (
        queries.reshape(rows // block, block, length, heads, head_size),
        chosen.reshape(rows // block, block, length, -1),
        log_total,
        adjoint.reshape(rows // block, block, length, heads, head_size),
    )
    (key_total, value_total), query_adjoint = lax.scan(one_block, (start, start), blocked)
    return (
        query_adjoint.reshape(queries.shape),
        key_total.astype(jnp.bfloat16),
        value_total.astype(jnp.bfloat16),
    )


def self_forward(
    residual, allowed, gain, shift, weight, query_bias, value_bias, out_weight, out_bias, groups
):
    rows, length, width = residual.shape
    span = width // groups
    normed = layer_norm(residual, gain, shift).astype(jnp.bfloat16)
    offset = jnp.concatenate([query_bias, jnp.zeros_like(query_bias), value_bias])
    mixed = (project(normed, weight) + offset).astype(jnp.bfloat16)
    gathered = rows_to_heads(mixed.reshape(rows, length, 3, groups, span))
    gathered = gathered.reshape(rows * groups, length, 3, HEADS // groups, HEAD)
    queries, keys, values = (gathered[:, :, 0], gathered[:, :, 1], gathered[:, :, 2])
    attended, log_total = self_heads_forward(queries, keys, values, allowed)
    merged = heads_to_rows(attended.reshape(rows * groups, length, 1, 1, span)).reshape(
        rows, length, width
    )
    kept = (residual, normed, queries, keys, values, log_total, merged)
    return (residual + project(merged, out_weight) + out_bias, kept)


def self_backward(adjoint, kept, gain, shift, weight, out_weight, allowed, groups):
    residual, normed, queries, keys, values, log_total, merged = kept
    rows, length, width = residual.shape
    span = width // groups
    branch = adjoint.astype(jnp.bfloat16)
    out_bias_adjoint = column_total(branch)
    merged_adjoint = project_back(branch, out_weight).astype(jnp.bfloat16)
    head_adjoint = adjoint_to_heads(merged_adjoint.reshape(rows, length, 1, groups, span))
    head_adjoint = head_adjoint.reshape(rows * groups, length, HEADS // groups, HEAD)
    query_adjoint, key_adjoint, value_adjoint = self_heads_back(
        queries, keys, values, allowed, log_total, head_adjoint
    )
    stacked = jnp.stack([query_adjoint, key_adjoint, value_adjoint], axis=2).reshape(
        rows * groups, length, 3, 1, span
    )
    mixed_adjoint = adjoint_to_rows(stacked).reshape(rows, length, 3 * width)
    offset_adjoint = column_total(mixed_adjoint)
    residual_adjoint, gain_adjoint, shift_adjoint = norm_back(
        residual, gain, shift, project_back(mixed_adjoint, weight)
    )
    pairs = ((normed, mixed_adjoint), (merged, branch))
    small = (
        gain_adjoint,
        shift_adjoint,
        offset_adjoint[:width],
        offset_adjoint[2 * width :],
        out_bias_adjoint,
    )
    return (adjoint + residual_adjoint, pairs, small)


def cross_forward(
    residual,
    pictures,
    chosen,
    gain,
    shift,
    weight,
    query_bias,
    pair_matrix,
    value_bias,
    out_weight,
    out_bias,
    groups,
    member,
):
    rows, length, width = residual.shape
    span = width // groups
    key_weight = lax.dynamic_slice_in_dim(pair_matrix, member * span, span, 1)
    value_weight = lax.dynamic_slice_in_dim(pair_matrix, width + member * span, span, 1)
    value_shift = lax.dynamic_slice_in_dim(value_bias, member * span, span, 0)
    layout = (pictures.shape[0], pictures.shape[1], HEADS // groups, HEAD)
    image_keys = project(pictures, key_weight).astype(jnp.bfloat16).reshape(layout)
    image_values = (
        (project(pictures, value_weight) + value_shift).astype(jnp.bfloat16).reshape(layout)
    )
    normed = layer_norm(residual, gain, shift).astype(jnp.bfloat16)
    query_rows = (project(normed, weight) + query_bias).astype(jnp.bfloat16)
    queries = rows_to_heads(query_rows.reshape(rows, length, 1, groups, span))
    queries = queries.reshape(rows * groups, length, HEADS // groups, HEAD)
    attended, log_total = cross_heads_forward(queries, image_keys, image_values, chosen)
    merged = heads_to_rows(attended.reshape(rows * groups, length, 1, 1, span)).reshape(
        rows, length, width
    )
    kept = (residual, normed, queries, image_keys, image_values, log_total, merged)
    return (residual + project(merged, out_weight) + out_bias, kept)


def cross_backward(
    adjoint, kept, pictures, chosen, gain, shift, weight, pair_matrix, out_weight, groups, member
):
    residual, normed, queries, image_keys, image_values, log_total, merged = kept
    rows, length, width = residual.shape
    span = width // groups
    key_weight = lax.dynamic_slice_in_dim(pair_matrix, member * span, span, 1)
    value_weight = lax.dynamic_slice_in_dim(pair_matrix, width + member * span, span, 1)
    branch = adjoint.astype(jnp.bfloat16)
    out_bias_adjoint = column_total(branch)
    merged_adjoint = project_back(branch, out_weight).astype(jnp.bfloat16)
    head_adjoint = adjoint_to_heads(merged_adjoint.reshape(rows, length, 1, groups, span))
    head_adjoint = head_adjoint.reshape(rows * groups, length, HEADS // groups, HEAD)
    query_adjoint, key_adjoint, value_adjoint = cross_heads_back(
        queries, image_keys, image_values, chosen, log_total, head_adjoint
    )
    query_rows = adjoint_to_rows(query_adjoint.reshape(rows * groups, length, 1, 1, span)).reshape(
        rows, length, width
    )
    query_bias_adjoint = column_total(query_rows)
    residual_adjoint, gain_adjoint, shift_adjoint = norm_back(
        residual, gain, shift, project_back(query_rows, weight)
    )
    layout = (pictures.shape[0], pictures.shape[1], span)
    key_adjoint = key_adjoint.reshape(layout)
    value_adjoint = value_adjoint.reshape(layout)
    value_bias_adjoint = lax.dynamic_update_slice_in_dim(
        jnp.zeros((width,), jnp.float32), column_total(value_adjoint), member * span, 0
    )
    picture_adjoint = project_back(key_adjoint, key_weight) + project_back(
        value_adjoint, value_weight
    )
    pairs = ((normed, query_rows), (merged, branch), (key_adjoint, value_adjoint))
    small = (gain_adjoint, shift_adjoint, query_bias_adjoint, value_bias_adjoint, out_bias_adjoint)
    return (adjoint + residual_adjoint, pairs, small, picture_adjoint)


def feed_forward(residual, gain, shift, up_matrix, up_shift, down_matrix, down_shift):
    normed = layer_norm(residual, gain, shift).astype(jnp.bfloat16)
    hidden = project(normed, up_matrix) + up_shift
    active = jax.nn.gelu(hidden, approximate=True).astype(jnp.bfloat16)
    return (
        residual + project(active, down_matrix) + down_shift,
        (residual, normed, hidden, active),
    )


def feed_backward(adjoint, kept, gain, shift, up_matrix, down_matrix):
    residual, normed, hidden, active = kept
    branch = adjoint.astype(jnp.bfloat16)
    down_shift_adjoint = column_total(branch)
    unused, pull = jax.vjp(partial(jax.nn.gelu, approximate=True), hidden)
    hidden_adjoint = pull(project_back(branch, down_matrix))[0].astype(jnp.bfloat16)
    up_shift_adjoint = column_total(hidden_adjoint)
    residual_adjoint, gain_adjoint, shift_adjoint = norm_back(
        residual, gain, shift, project_back(hidden_adjoint, up_matrix)
    )
    pairs = ((normed, hidden_adjoint), (active, branch))
    small = (gain_adjoint, shift_adjoint, up_shift_adjoint, down_shift_adjoint)
    return (adjoint + residual_adjoint, pairs, small)


def per_device(
    tokens,
    images,
    segment_labels,
    image_index,
    cotangent,
    norm_gain,
    vector_bias,
    up_bias,
    self_weight,
    self_out_weight,
    up_weight,
    down_weight,
    query_weight,
    pair_weight,
    cross_out_weight,
):
    groups = lax.axis_size("heads")
    member = lax.axis_index("heads")
    everyone = lax.axis_size(("dp", "heads"))
    length = segment_labels.shape[1]
    position = jnp.arange(length)
    allowed = (segment_labels[:, :, None] == segment_labels[:, None, :]) & (
        position[:, None] >= position[None, :]
    )[None]
    labels = jnp.arange(image_index.shape[1])
    caption_image = jnp.sum(
        jnp.where(segment_labels[:, :, None] == labels[None, None, :], image_index[:, None, :], 0),
        axis=-1,
        dtype=jnp.int32,
    )
    pictures = lax.all_gather(images, "heads", axis=0, tiled=True)
    chosen = caption_image[:, :, None] == jnp.arange(pictures.shape[0])[None, None, :]
    first = (
        lax.all_gather(self_weight[0], ("dp", "heads"), axis=0, tiled=True),
        lax.all_gather(self_out_weight[0], ("dp", "heads"), axis=0, tiled=True),
        lax.all_gather(up_weight[0], ("dp", "heads"), axis=0, tiled=True),
        lax.all_gather(down_weight[0], ("dp", "heads"), axis=0, tiled=True),
        lax.all_gather(norm_gain, ("dp", "heads"), axis=1, tiled=True),
        lax.all_gather(vector_bias, ("dp", "heads"), axis=1, tiled=True),
        lax.all_gather(up_bias, ("dp", "heads"), axis=1, tiled=True),
    )
    gains = first[4].astype(jnp.float32)
    biases = first[5].astype(jnp.float32)
    up_biases = first[6].astype(jnp.float32)
    residual = tokens.astype(jnp.float32)
    residual, kept_self_one = self_forward(
        residual,
        allowed,
        gains[0],
        biases[0],
        first[0],
        biases[5],
        biases[6],
        first[1],
        biases[7],
        groups,
    )
    residual, kept_feed_one = feed_forward(
        residual, gains[1], biases[1], first[2], up_biases[0], first[3], biases[8]
    )
    second = (
        lax.all_gather(self_weight[1], ("dp", "heads"), axis=0, tiled=True),
        lax.all_gather(self_out_weight[1], ("dp", "heads"), axis=0, tiled=True),
        lax.all_gather(up_weight[1], ("dp", "heads"), axis=0, tiled=True),
        lax.all_gather(down_weight[1], ("dp", "heads"), axis=0, tiled=True),
        lax.all_gather(query_weight, ("dp", "heads"), axis=0, tiled=True),
        lax.all_gather(pair_weight, ("dp", "heads"), axis=0, tiled=True),
        lax.all_gather(cross_out_weight, ("dp", "heads"), axis=0, tiled=True),
    )
    residual, kept_self_two = self_forward(
        residual,
        allowed,
        gains[2],
        biases[2],
        second[0],
        biases[9],
        biases[10],
        second[1],
        biases[11],
        groups,
    )
    residual, kept_cross = cross_forward(
        residual,
        pictures,
        chosen,
        gains[3],
        biases[3],
        second[4],
        biases[13],
        second[5],
        biases[14],
        second[6],
        biases[15],
        groups,
        member,
    )
    residual, kept_feed_two = feed_forward(
        residual, gains[4], biases[4], second[2], up_biases[1], second[3], biases[12]
    )
    second = (
        lax.all_gather(self_weight[1], ("dp", "heads"), axis=0, tiled=True),
        lax.all_gather(self_out_weight[1], ("dp", "heads"), axis=0, tiled=True),
        lax.all_gather(up_weight[1], ("dp", "heads"), axis=0, tiled=True),
        lax.all_gather(down_weight[1], ("dp", "heads"), axis=0, tiled=True),
        lax.all_gather(query_weight, ("dp", "heads"), axis=0, tiled=True),
        lax.all_gather(pair_weight, ("dp", "heads"), axis=0, tiled=True),
        lax.all_gather(cross_out_weight, ("dp", "heads"), axis=0, tiled=True),
    )
    adjoint = cotangent.astype(jnp.float32)
    adjoint, feed_two, feed_two_small = feed_backward(
        adjoint, kept_feed_two, gains[4], biases[4], second[2], second[3]
    )
    adjoint, cross_pairs, cross_small, picture_adjoint = cross_backward(
        adjoint,
        kept_cross,
        pictures,
        chosen,
        gains[3],
        biases[3],
        second[4],
        second[5],
        second[6],
        groups,
        member,
    )
    image_gradient = lax.psum_scatter(
        picture_adjoint.astype(jnp.bfloat16), "heads", scatter_dimension=0, tiled=True
    ).astype(jnp.float32)
    adjoint, self_two, self_two_small = self_backward(
        adjoint, kept_self_two, gains[2], biases[2], second[0], second[1], allowed, groups
    )
    first = (
        lax.all_gather(self_weight[0], ("dp", "heads"), axis=0, tiled=True),
        lax.all_gather(self_out_weight[0], ("dp", "heads"), axis=0, tiled=True),
        lax.all_gather(up_weight[0], ("dp", "heads"), axis=0, tiled=True),
        lax.all_gather(down_weight[0], ("dp", "heads"), axis=0, tiled=True),
        lax.all_gather(norm_gain, ("dp", "heads"), axis=1, tiled=True),
    )
    back_gains = first[4].astype(jnp.float32)
    adjoint, feed_one, feed_one_small = feed_backward(
        adjoint, kept_feed_one, back_gains[1], biases[1], first[2], first[3]
    )
    adjoint, self_one, self_one_small = self_backward(
        adjoint, kept_self_one, back_gains[0], biases[0], first[0], first[1], allowed, groups
    )
    width = tokens.shape[2]
    hidden_width = feed_one[0][1].shape[2]
    span = width // groups
    row_pairs = (
        self_one[0],
        self_one[1],
        feed_one[0],
        self_two[0],
        self_two[1],
        feed_two[0],
        cross_pairs[0],
    )
    key_adjoint, value_adjoint = cross_pairs[2]
    blocks = []
    for left, right in row_pairs:
        blocks.append(weight_adjoint(left, right))
    pair_block = jnp.zeros(
        (width // everyone * lax.axis_size(("dp", "heads")), 2 * width), jnp.float32
    )
    pair_block = lax.dynamic_update_slice_in_dim(
        pair_block, weight_adjoint(pictures, key_adjoint), member * span, 1
    )
    pair_block = lax.dynamic_update_slice_in_dim(
        pair_block, weight_adjoint(pictures, value_adjoint), width + member * span, 1
    )
    blocks.append(pair_block)
    left, right = cross_pairs[1]
    blocks.append(weight_adjoint(left, right))
    row_sums = lax.psum_scatter(
        jnp.concatenate(blocks, axis=1), ("dp", "heads"), scatter_dimension=0, tiled=True
    )
    blocks = []
    for left, right in (feed_one[1], feed_two[1]):
        blocks.append(weight_adjoint(left, right))
    down_sums = lax.psum_scatter(
        jnp.concatenate(blocks, axis=1), ("dp", "heads"), scatter_dimension=0, tiled=True
    )
    down_sums = jnp.transpose(down_sums.reshape(down_sums.shape[0], 2, width), (1, 0, 2))
    columns = (
        3 * width,
        width,
        hidden_width,
        3 * width,
        width,
        hidden_width,
        width,
        2 * width,
        width,
    )
    pieces = []
    offset = 0
    for span_width in columns:
        pieces.append(row_sums[:, offset : offset + span_width])
        offset = offset + span_width
    gain_rows = jnp.stack(
        [self_one_small[0], feed_one_small[0], self_two_small[0], cross_small[0], feed_two_small[0]]
    )
    bias_rows = jnp.stack(
        [
            self_one_small[1],
            feed_one_small[1],
            self_two_small[1],
            cross_small[1],
            feed_two_small[1],
            self_one_small[2],
            self_one_small[3],
            self_one_small[4],
            feed_one_small[3],
            self_two_small[2],
            self_two_small[3],
            self_two_small[4],
            feed_two_small[3],
            cross_small[2],
            cross_small[3],
            cross_small[4],
        ]
    )
    up_rows = jnp.stack([feed_one_small[2], feed_two_small[2]])
    small_sums = (
        lax.psum_scatter(gain_rows, ("dp", "heads"), scatter_dimension=1, tiled=True),
        lax.psum_scatter(bias_rows, ("dp", "heads"), scatter_dimension=1, tiled=True),
        lax.psum_scatter(up_rows, ("dp", "heads"), scatter_dimension=1, tiled=True),
    )
    return (
        residual,
        adjoint,
        image_gradient,
        small_sums[0],
        small_sums[1],
        small_sums[2],
        jnp.stack([pieces[0], pieces[3]]),
        jnp.stack([pieces[1], pieces[4]]),
        jnp.stack([pieces[2], pieces[5]]),
        down_sums,
        pieces[6],
        pieces[7],
        pieces[8],
    )


MESH = pl.DeviceIdType.MESH
CHIPS = 16
UNITS = 14
SMALL = UNITS
GATHER_ROUTES = ("zyx", "zxy", "yxz", "zxy", "zyx", "zxy", "zyx", "xyz", "zyx", "zxy", "zyx", "xyz", "zxy", "yxz", "zxy")
SCATTER_ROUTES = ("zyx", "zyx", "zxy", "zxy", "yxz", "zyx", "zxy", "zyx", "xyz", "zyx", "zxy", "xyz", "zxy", "zyx", "zxy")
ROUNDS = 6


class Place:
    def __init__(self):
        dp = lax.axis_index("dp")
        self.dp = dp
        self.h = lax.axis_index("heads")
        self.x = lax.rem(dp, 2)
        self.y = lax.rem(dp // 2, 2)
        self.z = dp // 4
        self.to_x = (dp + 1 - 2 * self.x, self.h)
        self.to_y = (dp + 2 - 4 * self.y, self.h)
        self.above = (dp + 4, self.h)
        self.below = (dp - 4, self.h)
        self.sibling = (dp, 1 - self.h)

    def barrier(self, sibling=False):
        bar = pltpu.get_barrier_semaphore()

        def greet(device):
            pl.semaphore_signal(bar, inc=1, device_id=device, device_id_type=MESH)

        greet(self.to_x)
        greet(self.to_y)
        if sibling:
            greet(self.sibling)
        pl.when(self.z < 3)(lambda: greet(self.above))
        pl.when(self.z > 0)(lambda: greet(self.below))
        peers = (3 if sibling else 2) + jnp.where(self.z < 3, 1, 0) + jnp.where(self.z > 0, 1, 0)
        pl.semaphore_wait(bar, peers)


def remote(source, target, send, recv, device):
    return pltpu.make_async_remote_copy(
        src_ref=source,
        dst_ref=target,
        send_sem=send,
        recv_sem=recv,
        device_id=device,
        device_id_type=MESH,
    )


class Gather:
    def __init__(self, at, views, send, recv):
        self.at, self.views, self.send, self.recv = at, views, send, recv

    def hop(self, u, slot, piece, device):
        return remote(piece, piece, self.send.at[u, slot], self.recv.at[u, slot], device)

    def line(self, u, step, piece_of, act):
        at = self.at
        z = at.z
        if act == "send":

            @pl.when((z < 3) & (z >= step - 1))
            def _():
                self.hop(u, step - 1, piece_of(z - (step - 1)), at.above).start()

            @pl.when((z > 0) & (z + step - 1 <= 3))
            def _():
                self.hop(u, step + 2, piece_of(z + (step - 1)), at.below).start()

        elif act == "recv":

            @pl.when(z >= step)
            def _():
                self.hop(u, step - 1, piece_of(z - step), at.below).wait_recv()

            @pl.when(z + step <= 3)
            def _():
                self.hop(u, step + 2, piece_of(z + step), at.above).wait_recv()

        else:

            @pl.when((z < 3) & (z >= step - 1))
            def _():
                self.hop(u, step - 1, piece_of(z - (step - 1)), at.above).wait_send()

            @pl.when((z > 0) & (z + step - 1 <= 3))
            def _():
                self.hop(u, step + 2, piece_of(z + (step - 1)), at.below).wait_send()

    def cross(self, u, axis, first, act):
        at, view = self.at, self.views(u)
        x, y, z = at.x, at.y, at.z
        route = GATHER_ROUTES[u]
        if route[0] == "z":
            if axis == route[1]:
                mine, its = view.at[:, y, x], (view.at[:, y, 1 - x] if axis == "x" else view.at[:, 1 - y, x])
            elif axis == "x":
                mine, its = view.at[:, :, x], view.at[:, :, 1 - x]
            else:
                mine, its = view.at[:, y], view.at[:, 1 - y]
        elif axis == route[0]:
            mine, its = view.at[z, y, x], (view.at[z, y, 1 - x] if axis == "x" else view.at[z, 1 - y, x])
        elif axis == "x":
            mine, its = view.at[z, :, x], view.at[z, :, 1 - x]
        else:
            mine, its = view.at[z, y], view.at[z, 1 - y]
        slot, device = (6, at.to_x) if axis == "x" else (7, at.to_y)
        if act == "recv":
            self.hop(u, slot, its, device).wait_recv()
        elif act == "send":
            self.hop(u, slot, mine, device).start()
        else:
            self.hop(u, slot, mine, device).wait_send()

    def stages(self, u):
        at, view, route = self.at, self.views(u), GATHER_ROUTES[u]
        if route[0] == "z":
            along = partial(self.line, u, piece_of=lambda k: view.at[k, at.y, at.x])
            lines = [partial(along, step) for step in (1, 2, 3)]
            return lines + [partial(self.cross, u, route[1], None), partial(self.cross, u, route[2], None)]
        along = partial(self.line, u, piece_of=lambda k: view.at[k])
        lines = [partial(along, step) for step in (1, 2, 3)]
        return [partial(self.cross, u, route[0], None), partial(self.cross, u, route[1], None)] + lines

    def round(self, u, k):
        stages = self.stages(u)
        if k > 0:
            stages[k - 1](act="recv")
        if k < 5:
            stages[k](act="send")

    def drain(self, u):
        for stage in self.stages(u):
            stage(act="sent")


def add_blocks(total, extra, count):
    @pl.loop(0, count)
    def _(i):
        left, right = total(i), extra(i)
        left[...] = (left[...].astype(jnp.float32) + right[...].astype(jnp.float32)).astype(left.dtype)


class Scatter:
    def __init__(self, at, views, spare, send, recv):
        self.at, self.views, self.spare, self.send, self.recv = at, views, spare, send, recv

    def hop(self, u, slot, source, target, device):
        return remote(source, target, self.send.at[u, slot], self.recv.at[u, slot], device)

    def line(self, u, step, act):
        at = self.at
        z = at.z
        wide = SCATTER_ROUTES[u][0] != "z"
        view, up, down = self.views(u), self.spare(u, "up"), self.spare(u, "down")

        def piece(k):
            return view.at[k] if wide else view.at[k, at.y, at.x]

        def send_up():
            return self.hop(u, step - 1, piece(z + 4 - step), up.at[step - 1], at.above)

        def send_down():
            return self.hop(u, step + 2, piece(z + step - 4), down.at[step - 1], at.below)

        if act == "send":
            pl.when((z < 3) & (z <= step - 1))(lambda: send_up().start())
            pl.when((z > 0) & (z >= 4 - step))(lambda: send_down().start())
        elif act == "sent":
            pl.when((z < 3) & (z <= step - 1))(lambda: send_up().wait_send())
            pl.when((z > 0) & (z >= 4 - step))(lambda: send_down().wait_send())
        else:
            shape = (2, 2) if wide else (1,)

            def take(k, slots):
                if wide:
                    for i in (0, 1):
                        add_blocks(lambda j: view.at[k, i, j], lambda j: slots.at[step - 1, i, j], 2)
                else:
                    add_blocks(lambda j: view.at[k, at.y, at.x], lambda j: slots.at[step - 1], 1)

            @pl.when((z >= 1) & (z <= step))
            def _():
                self.hop(u, step - 1, piece(z), up.at[step - 1], at.below).wait_recv()
                take(z + 3 - step, up)

            @pl.when((z < 3) & (z >= 3 - step))
            def _():
                self.hop(u, step + 2, piece(z), down.at[step - 1], at.above).wait_recv()
                take(z + step - 3, down)

    def cross(self, u, axis, act):
        at, view, spare = self.at, self.views(u), self.spare(u, axis)
        x, y, z = at.x, at.y, at.z
        route = SCATTER_ROUTES[u]
        slot, device = (6, at.to_x) if axis == "x" else (7, at.to_y)
        if route[0] == "z":
            if axis == route[2]:
                its = view.at[:, :, 1 - x] if axis == "x" else view.at[:, 1 - y]

                def add():
                    for j in (0, 1):
                        if axis == "x":
                            add_blocks(lambda i: view.at[i, j, x], lambda i: spare.at[i, j], 4)
                        else:
                            add_blocks(lambda i: view.at[i, y, j], lambda i: spare.at[i, j], 4)
            else:
                its = view.at[:, y, 1 - x] if axis == "x" else view.at[:, 1 - y, x]

                def add():
                    add_blocks(lambda i: view.at[i, y, x], lambda i: spare.at[i], 4)
        elif axis == route[1]:
            its = view.at[z, :, 1 - x] if axis == "x" else view.at[z, 1 - y]

            def add():
                if axis == "x":
                    add_blocks(lambda i: view.at[z, i, x], lambda i: spare.at[i], 2)
                else:
                    add_blocks(lambda i: view.at[z, y, i], lambda i: spare.at[i], 2)
        else:
            its = view.at[z, y, 1 - x] if axis == "x" else view.at[z, 1 - y, x]

            def add():
                add_blocks(lambda i: view.at[z, y, x], lambda i: spare, 1)

        hop = self.hop(u, slot, its, spare, device)
        if act == "send":
            hop.start()
        elif act == "sent":
            hop.wait_send()
        else:
            hop.wait_recv()
            add()

    def stages(self, u):
        route = SCATTER_ROUTES[u]
        lines = [partial(self.line, u, step) for step in (1, 2, 3)]
        if route[0] == "z":
            return [partial(self.cross, u, route[2]), partial(self.cross, u, route[1])] + lines
        return lines + [partial(self.cross, u, route[1]), partial(self.cross, u, route[0])]

    def round(self, u, k, end):
        stages = self.stages(u)
        if k > 0:
            stages[k - 1](act="recv")
        if k < 5:
            stages[k](act="send")
        else:
            end(u)

    def drain(self, u):
        for stage in self.stages(u):
            stage(act="sent")


def spare_shapes(rows, width, small):
    narrow = [u for u in range(UNITS) if SCATTER_ROUTES[u][0] == "z"]
    wide = [u for u in range(UNITS) if SCATTER_ROUTES[u][0] != "z"]

    def of(count, tail, kind):
        return [
            pltpu.VMEM((count, 4, 2) + tail, kind),
            pltpu.VMEM((count, 4) + tail, kind),
            pltpu.VMEM((count, 3) + tail, kind),
            pltpu.VMEM((count, 3) + tail, kind),
        ]

    shapes = of(len(narrow), (rows, width), jnp.bfloat16)
    tail = (rows, width)
    shapes += [
        pltpu.VMEM((len(wide), 2) + tail, jnp.bfloat16),
        pltpu.VMEM((len(wide),) + tail, jnp.bfloat16),
        pltpu.VMEM((len(wide), 3, 2, 2) + tail, jnp.bfloat16),
        pltpu.VMEM((len(wide), 3, 2, 2) + tail, jnp.bfloat16),
    ]
    shapes += of(1, (rows, small), jnp.float32)

    def pick(refs):
        def spare(u, what):
            route = SCATTER_ROUTES[u]
            if u == SMALL:
                base, index = 8, 0
            elif route[0] == "z":
                base, index = 0, narrow.index(u)
            else:
                base, index = 4, wide.index(u)
            if what in "xy":
                first = route[2] if route[0] == "z" else route[1]
                slot = 0 if what == first else 1
            else:
                slot = 2 if what == "up" else 3
            return refs[base + slot].at[index]

        return spare

    return shapes, pick


class ForwardRefs(NamedTuple):
    blocks: Any
    small: Any
    tokens: Any
    images: Any
    causal: Any
    choice: Any
    full: Any
    table: Any
    residuals: Any
    mixed: Any
    attended: Any
    queries: Any
    pair: Any
    hidden: Any
    out_rows: Any
    layer_out: Any
    g: Any
    g_small: Any
    tab: Any
    res: Any
    normed: Any
    mix: Any
    att: Any
    qc: Any
    pr: Any
    hid: Any
    act: Any
    acc: Any
    give: Any
    take: Any
    img: Any
    tok: Any
    rowsw: Any
    send: Any
    recv: Any
    local: Any
    swap_send: Any
    swap_recv: Any
    quarter_send: Any
    quarter_recv: Any
    keep: Any
    share_send: Any
    share_recv: Any


class BackRefs(NamedTuple):
    full: Any
    table: Any
    residuals: Any
    mixed: Any
    attended: Any
    queries: Any
    pair: Any
    hidden: Any
    out_rows: Any
    cotangent: Any
    images: Any
    causal: Any
    choice: Any
    sums_out: Any
    small_out: Any
    token_out: Any
    image_out: Any
    g: Any
    tab: Any
    dx: Any
    branch: Any
    res: Any
    scale: Any
    normed: Any
    hid: Any
    dhid: Any
    act: Any
    mix: Any
    att: Any
    datt: Any
    qc: Any
    pr: Any
    rowsw: Any
    img: Any
    give: Any
    take: Any
    pic_give: Any
    pic_take: Any
    og: Any
    sums: Any
    small: Any
    send: Any
    recv: Any
    swap_send: Any
    swap_recv: Any
    quarter_send: Any
    quarter_recv: Any
    quarter_local: Any
    load: Any
    store: Any
    share_send: Any
    share_recv: Any


def lowest(value):
    return value.astype(jnp.bfloat16)


def mm(left, right):
    return jnp.dot(left, right, preferred_element_type=jnp.float32)


def mm_back(left, right):
    return lax.dot_general(left, right, (((1,), (1,)), ((), ())), preferred_element_type=jnp.float32)


def mm_rows(left, right):
    return lax.dot_general(left, right, (((0,), (0,)), ((), ())), preferred_element_type=jnp.float32)


def first_lanes(value):
    return lax.broadcasted_iota(jnp.int32, value.shape, 1) < HEAD


def two_heads(value):
    lanes = first_lanes(value)
    zero = jnp.zeros_like(value)
    return jnp.concatenate([jnp.where(lanes, value, zero), jnp.where(lanes, zero, value)], axis=0)


def beside(value):
    half = value.shape[0] // 2
    return jnp.concatenate([value[:half], value[half:]], axis=1)


def below(value):
    half = value.shape[1] // 2
    return jnp.concatenate([value[:, :half], value[:, half:]], axis=0)


def softmax_of(scores, axis):
    shares = jnp.exp(scores - jnp.max(scores, axis=axis, keepdims=True))
    return shares * (1.0 / jnp.sum(shares, axis=axis, keepdims=True))


SPAN = 128
SCALING = HEAD ** (-0.5)
ROWS_AT_ONCE = 256


def whole(ref):
    value = ref[...]
    return value.reshape(-1, value.shape[-1])


def picture_bias(choice):
    away = jnp.full_like(choice, masked_score)
    zero = jnp.zeros_like(choice)
    first = jnp.where(choice == 0.0, zero, away)
    second = jnp.where(choice == 1.0, zero, away)
    return jnp.concatenate([first, first, second, second], axis=1)


def norm_parts(value):
    center = value - jnp.mean(value, axis=1, keepdims=True)
    variance = jnp.mean(center * center, axis=1, keepdims=True)
    scale = lax.rsqrt(variance + 1e-05)
    return center * scale, scale


GELU_A = math.sqrt(2 / math.pi)
GELU_B = 0.044715


def gelu(value):
    return 0.5 * value * (1.0 + jnp.tanh(GELU_A * (value + GELU_B * (value * value * value))))


GATHER_ORDER = (
    84, 18, 0, 12, 85, 42, 19, 6, 1, 30, 86, 24, 13, 20, 36, 43, 7, 2, 87, 66, 31, 21, 48, 25, 3, 54, 37, 8, 78, 32, 60,
    67, 49, 26, 9, 72, 88, 55, 38, 33, 22, 27, 79, 4, 61, 50, 39, 73, 56, 14, 51, 44, 10, 62, 57, 89, -1, 34, 15, 74,
    23, 28, 45, 63, 5, 40, 75, 16, 68, 52, 46, 11, -1, -1, -1, -1, -1, -1, 58, -1, -1, -1, -1, -1, -1, -1, 17, -1, -1,
    -1, -1, -1, -1, 35, 69, 47, 29, -1, -1, -1, -1, 80, -1, -1, 64, 41, -1, -1, -1, -1, -1, -1, 76, -1, -1, -1, -1, -1,
    -1, -1, 81, 70, 53, 59, -1, -1, -1, -1, -1, -1, -1, -1, -1, -1, -1, -1, -1, -1, -1, -1, -1, -1, -1, 71, 82, 65, -1,
    -1, -1, -1, -1, 77, -1, -1, 83, -1, -1,
)
SCATTER_ORDER = (
    -1, -1, -1, -1, -1, -1, 72, -1, -1, -1, -1, 78, -1, -1, -1, -1, -1, -1, -1, 66, -1, -1, -1, -1, -1, -1, -1, -1, 60,
    -1, 67, -1, 73, -1, -1, -1, -1, -1, -1, 79, -1, 68, -1, -1, 54, -1, -1, -1, -1, -1, -1, 48, -1, -1, -1, -1, -1, -1,
    -1, 61, -1, 49, -1, -1, -1, -1, 36, -1, -1, -1, -1, -1, 50, -1, 42, 55, -1, -1, -1, -1, -1, -1, -1, -1, -1, 74, -1,
    24, -1, -1, 30, -1, 80, -1, -1, -1, -1, 12, -1, 25, -1, -1, 37, -1, -1, -1, -1, 43, -1, -1, 26, 62, -1, -1, 75, -1,
    -1, -1, -1, 31, -1, 81, -1, -1, -1, -1, 56, -1, 6, -1, -1, 13, 84, 76, 63, 82, 38, 44, 57, 7, 64, 32, 58, 14, 39,
    45, 0, 18, 33, 40, 8, 46, 15, 34, 1, 16, 19, 77, 85, 9, 83, 69, 10, 65, 2, 51, 59, 20, 86, 70, 41, 3, 47, 27, 21,
    35, 87, 52, 4, 17, 22, 11, 28, 71, 88, 53, 5, 23, 89, 29,
)


def play(order, steps, move):
    moved, left = set(), list(steps)
    for code in order:
        if code < 0:
            work, needs = left.pop(0)
            assert needs <= moved
            work()
        else:
            u, k = divmod(code, ROUNDS)
            move(u, k)
            if k == ROUNDS - 1:
                moved.add(u)
    assert not left


def forward_kernel(*refs):
    r = ForwardRefs(*refs)
    at = Place()
    h = at.h
    at.barrier(sibling=True)
    tokens = r.tok.shape[0]
    width = r.tok.shape[1]
    half = width // 2
    spans = [pl.ds(i, ROWS_AT_ONCE) for i in range(0, tokens, ROWS_AT_ONCE)]
    mine = pl.ds(pl.multiple_of(h * ROWS_AT_ONCE, ROWS_AT_ONCE), ROWS_AT_ONCE)
    others = pl.ds(pl.multiple_of((1 - h) * ROWS_AT_ONCE, ROWS_AT_ONCE), ROWS_AT_ONCE)
    gather = Gather(at, lambda u: r.g_small if u == SMALL else r.g.at[u], r.send, r.recv)

    copies = [
        pltpu.make_async_copy(r.small, r.g_small.at[at.z, at.y, at.x], r.local.at[0]),
        pltpu.make_async_copy(r.blocks, r.g.at[:, at.z, at.y, at.x], r.local.at[1]),
        pltpu.make_async_copy(r.tokens, r.tok.at[mine], r.local.at[2]),
        pltpu.make_async_copy(r.images, r.img.at[mine], r.local.at[3]),
    ]
    for copy in copies:
        copy.start()

    def share(rows):
        return [
            remote(source, target.at[rows], r.share_send.at[i], r.share_recv.at[i], at.sibling)
            for i, (source, target) in enumerate(((r.tokens, r.tok), (r.images, r.img)))
        ]

    for copy in share(mine):
        copy.start()

    keeps = []

    def keep(source, target):
        copy = pltpu.make_async_copy(source, target, r.keep.at[len(keeps)])
        keeps.append(copy)
        copy.start()

    def vector(n):
        return r.tab[pl.ds(n, 1), :]

    def own_vector(n):
        return r.tab[pl.ds(n, 1), pl.ds(pl.multiple_of(h * half, 128), half)]

    def start():
        for copy in copies[2:]:
            copy.wait()
        for copy in share(mine):
            copy.wait_send()
        for copy in share(others):
            copy.wait_recv()
        r.res[0] = r.tok[...].astype(jnp.float32)
        r.tab[...] = whole(r.g_small).astype(jnp.float32).T
        keep(r.tab, r.table)

    def norm(n):
        @pl.loop(0, tokens // 64, unroll=True)
        def _(i):
            rows = pl.ds(pl.multiple_of(i * 64, 64), 64)
            value, scale = norm_parts(r.res[n, rows, :])
            r.normed[rows, :] = lowest(value * vector(n) + vector(5 + n))

        keep(r.res.at[n], r.residuals.at[n])

    def quarter(l, u):
        away = (1 - h) * 2
        mine = pltpu.make_async_copy(
            r.g.at[u, pl.ds(h * 2, 2), :, :, :, pl.ds(half, half)],
            r.rowsw.at[l, :, :, :, :, pl.ds(pl.multiple_of(h * half, 128), half)],
            r.local.at[4 + l],
        )
        theirs = remote(
            r.g.at[u, pl.ds(away, 2), :, :, :, pl.ds(half, half)],
            r.rowsw.at[l, :, :, :, :, pl.ds(pl.multiple_of(h * half, 128), half)],
            r.quarter_send.at[l],
            r.quarter_recv.at[l],
            at.sibling,
        )
        return mine, theirs

    def start_quarter(l, u):
        mine, theirs = quarter(l, u)
        mine.start()
        theirs.start()

    def end_quarter(l, u):
        mine, theirs = quarter(l, u)
        mine.wait()
        theirs.wait()
        keep(r.rowsw.at[l], r.out_rows.at[l])

    def swap(e, i):
        rows = spans[i]
        return remote(
            r.give.at[e % 2, rows], r.take.at[e % 2, rows], r.swap_send.at[e, i], r.swap_recv.at[e, i], at.sibling
        )

    def offer(e, i, value):
        r.give[e % 2, spans[i], :] = lowest(value)
        swap(e, i).start()

    def join(e, i, n, bias):
        swap(e, i).wait()
        rows = spans[i]
        both = r.give[e % 2, rows, :].astype(jnp.float32) + r.take[e % 2, rows, :].astype(jnp.float32)
        r.res[n + 1, rows, :] = r.res[n, rows, :] + both + vector(5 + bias)

    def mix(l, u, query_bias, value_bias, i):
        rows = spans[i]
        value = r.normed[rows, :]
        both = mm(value, whole(r.g.at[u]))
        r.mix[l, rows, :half] = lowest(both[:, :half] + own_vector(5 + query_bias))
        r.mix[l, rows, half:width] = lowest(both[:, half:])
        r.mix[l, rows, width:] = lowest(
            mm(value, whole(r.g.at[u + 1, :, :, :, :, :half])) + own_vector(5 + value_bias)
        )

    def attend(l, blocks):
        @pl.loop(*blocks, unroll=True)
        def _(i):
            rows = pl.ds(pl.multiple_of(i * SPAN, SPAN), SPAN)
            bias = r.causal[i]
            bias = jnp.concatenate([bias, bias], axis=0)
            for j in range(half // 128):
                lanes = [pl.ds(part * half + j * 128, 128) for part in range(3)]
                queries, keys, values = [r.mix[l, rows, lane] for lane in lanes]
                scores = mm_back(two_heads(queries * SCALING), keys) + bias
                shares = lowest(softmax_of(scores, 1))
                r.att[l, rows, pl.ds(j * 128, 128)] = lowest(mm(beside(shares), two_heads(values)))

    def project_out(l, e, a, i):
        value = r.att[a, spans[i], :]
        offer(e, i, mm(value, whole(r.rowsw.at[a])))

    def up(l, u, s, i):
        rows = spans[i]
        value = mm(r.normed[rows, :], whole(r.g.at[u])) + vector(21 + 2 * l + s)
        r.hid[l, rows, pl.ds(s * width, width)] = value
        r.act[rows, pl.ds(s * width, width)] = lowest(gelu(value))

    def down(u, s, i, e):
        rows = spans[i]
        value = mm(r.act[rows, pl.ds(s * width, width)], whole(r.g.at[u]))
        if s == 0:
            r.acc[rows, :] = value
        else:
            offer(e, i, r.acc[rows, :] + value)

    def picture_pair(i):
        rows = spans[i]
        value = mm(r.img[rows, :], whole(r.g.at[9]))
        r.pr[rows, :half] = lowest(value[:, :half])
        r.pr[rows, half:] = lowest(value[:, half:] + own_vector(5 + 14))

    def cross_queries(i):
        rows = spans[i]
        r.qc[rows, :] = lowest(mm(r.normed[rows, :], whole(r.g.at[8, :, :, :, :, :half])) + own_vector(5 + 13))

    def cross(blocks):
        @pl.loop(*blocks, unroll=True)
        def _(i):
            rows = pl.ds(pl.multiple_of(i * SPAN, SPAN), SPAN)
            bias = picture_bias(r.choice[rows, :])
            bias = jnp.concatenate([bias, bias], axis=0)
            for j in range(half // 128):
                keys = r.pr[:, pl.ds(j * 128, 128)]
                values = r.pr[:, pl.ds(half + j * 128, 128)]
                scores = mm_back(two_heads(r.qc[rows, pl.ds(j * 128, 128)] * SCALING), keys) + bias
                shares = lowest(softmax_of(scores, 1))
                r.att[2, rows, pl.ds(j * 128, 128)] = lowest(mm(beside(shares), two_heads(values)))

    segments = []

    def add(needs, work, *args):
        segments.append((partial(work, *args), frozenset(needs)))

    def add_attention(l, n, u, e, biases, rest):
        add({SMALL, u, u + 1}, start_quarter, l, u + 1)
        add(rest, norm, n)
        for i in (0, 1):
            add(rest, mix, l, u, biases[0], biases[1], i)
        for i in (0, 1):
            add(rest, attend, l, (2 * i, 2 * i + 2))
        add(rest, end_quarter, l, u + 1)
        add(rest, keep, r.mix.at[l], r.mixed.at[l])
        for i in (0, 1):
            add(rest, project_out, l, e, l, i)
        add(rest, keep, r.att.at[l], r.attended.at[l])
        for i in (0, 1):
            add(rest, join, e, i, n, biases[2])

    def add_feed(l, n, u, e, bias):
        add((), norm, n)
        for s in (0, 1):
            for i in (0, 1):
                add({u + s}, up, l, u + s, s, i)
        add((), keep, r.hid.at[l], r.hidden.at[l])
        for s in (0, 1):
            for i in (0, 1):
                add({u + 2 + s}, down, u + 2 + s, s, i, e)
        if e < 4:
            for i in (0, 1):
                add((), join, e, i, n, bias)

    add({SMALL}, start)
    add_attention(0, 0, 0, 0, (5, 6, 7), ())
    add_feed(0, 1, 2, 1, 8)
    add_attention(1, 2, 6, 2, (9, 10, 11), ())
    add({9}, picture_pair, 0)
    add((), picture_pair, 1)
    add((), keep, r.pr, r.pair)
    add({8}, start_quarter, 2, 8)
    add((), norm, 3)
    for i in (0, 1):
        add((), cross_queries, i)
    add((), keep, r.qc, r.queries)
    for i in range(4):
        add((), cross, (i, i + 1))
    add((), end_quarter, 2, 8)
    for i in (0, 1):
        add((), project_out, 2, 3, 2, i)
    add((), keep, r.att.at[2], r.attended.at[2])
    for i in (0, 1):
        add((), join, 3, i, 3, 15)
    add_feed(1, 4, 10, 4, 12)

    for copy in copies[:2]:
        copy.wait()

    def move(u, k):
        gather.round(u, k)
        if k == ROUNDS - 1 and u != SMALL:
            keep(r.g.at[u], r.full.at[u])

    play(GATHER_ORDER, segments, move)
    for i in (0, 1):
        swap(4, i).wait()
    both = r.give[0, mine, :].astype(jnp.float32) + r.take[0, mine, :].astype(jnp.float32)
    r.layer_out[...] = r.res[4, mine, :] + both + vector(5 + 12)
    for u in range(UNITS + 1):
        gather.drain(u)
    for copy in keeps:
        copy.wait()


def forward(blocks, small, tokens, images, causal, choice):
    units, rows, width = blocks.shape
    count = 2 * tokens.shape[0]
    half = width // 2
    bf, fl = jnp.bfloat16, jnp.float32
    shape = jax.ShapeDtypeStruct
    dma = pltpu.SemaphoreType.DMA
    outs = (
        shape((units, 4, 2, 2, rows, width), bf),
        shape((128, width), fl),
        shape((5, count, width), fl),
        shape((2, count, width + half), bf),
        shape((3, count, half), bf),
        shape((count, half), bf),
        shape((count, width), bf),
        shape((2, count, 2 * width), fl),
        shape((3, 2, 2, 2, rows, width), bf),
        shape((count // 2, width), fl),
    )
    anywhere, here = pl.BlockSpec(memory_space=pl.ANY), pl.BlockSpec(memory_space=pltpu.VMEM)
    return pl.pallas_call(
        forward_kernel,
        out_shape=outs,
        in_specs=[anywhere] * 4 + [here] * 2,
        out_specs=[anywhere] * 9 + [here],
        scratch_shapes=[
            pltpu.VMEM((units, 4, 2, 2, rows, width), bf),
            pltpu.VMEM((4, 2, 2) + small.shape, bf),
            pltpu.VMEM((128, width), fl),
            pltpu.VMEM((5, count, width), fl),
            pltpu.VMEM((count, width), bf),
            pltpu.VMEM((2, count, width + half), bf),
            pltpu.VMEM((3, count, half), bf),
            pltpu.VMEM((count, half), bf),
            pltpu.VMEM((count, width), bf),
            pltpu.VMEM((2, count, 2 * width), fl),
            pltpu.VMEM((count, 2 * width), bf),
            pltpu.VMEM((count, width), fl),
            pltpu.VMEM((2, count, width), bf),
            pltpu.VMEM((2, count, width), bf),
            pltpu.VMEM((count, width), bf),
            pltpu.VMEM((count, width), bf),
            pltpu.VMEM((3, 2, 2, 2, rows, width), bf),
            dma((units + 1, 8)),
            dma((units + 1, 8)),
            dma((8,)),
            dma((5, 2)),
            dma((5, 2)),
            dma((3,)),
            dma((3,)),
            dma((40,)),
            dma((2,)),
            dma((2,)),
        ],
        compiler_params=pltpu.CompilerParams(collective_id=0, has_side_effects=True, vmem_limit_bytes=60 << 20),
    )(blocks, small, tokens, images, causal, choice)


BACK_UNITS = (12, 13, 10, 11, 9, 8, 6, 7, 4, 5, 2, 3, 0, 1, SMALL)
OUT_UNITS = (8, 7, 1)


def gelu_parts(value):
    square = value * value
    bent = jnp.tanh(value * (GELU_A + (GELU_A * GELU_B) * square))
    rise = 0.5 + 0.5 * bent
    slope = rise + (0.5 * value) * (1.0 - bent * bent) * (GELU_A + (3.0 * GELU_A * GELU_B) * square)
    return value * rise, slope


def backward_kernel(*refs, pick, spares):
    named = len(BackRefs._fields)
    r = BackRefs(*refs[:named])
    spare = pick(refs[named:])
    at = Place()
    h = at.h
    at.barrier(sibling=True)
    tokens, width = r.branch.shape
    half = width // 2
    spans = [pl.ds(i, ROWS_AT_ONCE) for i in range(0, tokens, ROWS_AT_ONCE)]
    mine = pl.ds(pl.multiple_of(h * ROWS_AT_ONCE, ROWS_AT_ONCE), ROWS_AT_ONCE)
    others = pl.ds(pl.multiple_of((1 - h) * ROWS_AT_ONCE, ROWS_AT_ONCE), ROWS_AT_ONCE)
    own_lanes = pl.ds(pl.multiple_of(h * half, 128), half)
    other_lanes = pl.ds(pl.multiple_of((1 - h) * half, 128), half)
    scatter = Scatter(at, lambda u: r.small if u == SMALL else r.g.at[u], spare, r.send, r.recv)

    loads = {}

    def fetch(name, source, target):
        copy = pltpu.make_async_copy(source, target, r.load.at[len(loads)])
        loads[name] = copy
        copy.start()

    def need(name):
        copy = loads[name]
        if copy is not None:
            copy.wait()
            loads[name] = None
            if name in shared:
                share(name, mine).wait_send()
                share(name, others).wait_recv()

    shared = {"cotangent": (0, r.cotangent, r.branch), "images": (1, r.images, r.img)}

    def share(name, rows):
        i, source, target = shared[name]
        return remote(source, target.at[rows], r.share_send.at[i], r.share_recv.at[i], at.sibling)

    def fetch_shared(name):
        i, source, target = shared[name]
        fetch(name, source, target.at[mine])
        share(name, mine).start()

    def fetch_unit(u):
        if u in OUT_UNITS:
            fetch(("g", u), r.full.at[u, :, :, :, :, pl.ds(0, half)], r.g.at[u, :, :, :, :, pl.ds(0, half)])
        else:
            fetch(("g", u), r.full.at[u], r.g.at[u])

    def fetch_residual(n, slot):
        fetch(("res", n), r.residuals.at[n], r.res.at[slot])

    def fetch_hidden(l):
        for s in (0, 1):
            fetch(("hid", l, s), r.hidden.at[l, :, pl.ds(s * width, width)], r.hid.at[s])

    def fetch_mixed(l):
        fetch(("mix", l), r.mixed.at[l], r.mix)

    fetch("table", r.table, r.tab)
    fetch_shared("cotangent")
    fetch_unit(12)
    fetch_hidden(1)
    fetch_unit(13)
    fetch_residual(4, 0)
    fetch_unit(10)
    fetch_unit(11)
    fetch("rows", r.out_rows, r.rowsw)
    fetch("queries", r.queries, r.qc)
    fetch("pair", r.pair, r.pr)
    fetch_residual(3, 1)
    fetch("attended", r.attended, r.att)
    fetch_shared("images")
    for u in (9, 8):
        fetch_unit(u)
    fetch_mixed(1)
    for u in (6, 7, 4, 5, 2, 3, 0, 1):
        fetch_unit(u)

    def vector(n):
        return r.tab[pl.ds(n, 1), :]

    def add_row(n, value):
        r.sums[pl.ds(n, 1), :] += jnp.sum(value, axis=0, keepdims=True)

    def add_own(n, value):
        r.sums[pl.ds(n, 1), own_lanes] += jnp.sum(value, axis=0, keepdims=True)

    def start():
        need("cotangent")
        r.sums[...] = jnp.zeros_like(r.sums)
        r.dx[...] = r.branch[...].astype(jnp.float32)

    def norm(n, slot):
        need(("res", n))
        need("table")

        @pl.loop(0, tokens // 64, unroll=True)
        def _(i):
            rows = pl.ds(pl.multiple_of(i * 64, 64), 64)
            value, scale = norm_parts(r.res[slot, rows, :])
            r.res[slot, rows, :] = value
            r.scale[rows, :] = scale
            r.normed[rows, :] = lowest(value * vector(n) + vector(5 + n))

    def begin_branch(bias):
        @pl.loop(0, tokens // 64, init_carry=jnp.zeros((1, width), jnp.float32), unroll=True)
        def total(i, carry):
            rows = pl.ds(pl.multiple_of(i * 64, 64), 64)
            value = lowest(r.dx[rows, :])
            r.branch[rows, :] = value
            return carry + jnp.sum(value.astype(jnp.float32), axis=0, keepdims=True)

        r.sums[pl.ds(5 + bias, 1), :] = total

    def swap(e, i):
        rows = spans[i]
        return remote(
            r.give.at[e % 2, rows], r.take.at[e % 2, rows], r.swap_send.at[e, i], r.swap_recv.at[e, i], at.sibling
        )

    def offer(e, i, value):
        r.give[e % 2, spans[i], :] = lowest(value)
        swap(e, i).start()

    def join(e, i, n, slot):
        swap(e, i).wait()
        base = i * ROWS_AT_ONCE
        gain = vector(n)
        zero = jnp.zeros((1, width), jnp.float32)

        @pl.loop(0, ROWS_AT_ONCE // 64, init_carry=(zero, zero), unroll=True)
        def totals(k, carry):
            rows = pl.ds(pl.multiple_of(base + k * 64, 64), 64)
            given = r.give[e % 2, rows, :].astype(jnp.float32) + r.take[e % 2, rows, :].astype(jnp.float32)
            value = r.res[slot, rows, :]
            product = given * value
            scaled = given * gain
            first = jnp.mean(scaled, axis=1, keepdims=True)
            second = jnp.mean(product * gain, axis=1, keepdims=True)
            r.dx[rows, :] += r.scale[rows, :] * (scaled - first - value * second)
            return (
                carry[0] + jnp.sum(product, axis=0, keepdims=True),
                carry[1] + jnp.sum(given, axis=0, keepdims=True),
            )

        r.sums[pl.ds(n, 1), :] += totals[0]
        r.sums[pl.ds(5 + n, 1), :] += totals[1]

    def store_rows(u, part, value, lanes=slice(None)):
        value = lowest(value)
        r.g[u, 2 * part : 2 * part + 2, :, :, :, lanes] = value.reshape((2, 2, 2, -1) + value.shape[1:])

    def feed_hidden(l, u, s, i):
        need(("g", u))
        need(("hid", l, s))
        rows, lanes = spans[i], pl.ds(s * width, width)
        back = mm_back(r.branch[rows, :], whole(r.g.at[u]))
        active, slope = gelu_parts(r.hid[s, rows, :])
        value = lowest(back * slope)
        r.act[rows, lanes] = lowest(active)
        r.dhid[rows, lanes] = value
        add_row(21 + 2 * l + s, value.astype(jnp.float32))

    def feed_down(u, s, part):
        lanes = pl.ds(s * width + part * half, half)
        store_rows(u, part, mm_rows(r.act[:, lanes], r.branch[...]))

    def feed_normed(u, i, e):
        need(("g", u))
        need(("g", u + 1))
        rows = spans[i]
        value = mm_back(r.dhid[rows, :width], whole(r.g.at[u]))
        offer(e, i, value + mm_back(r.dhid[rows, width:], whole(r.g.at[u + 1])))

    def feed_up(u, s, part):
        lanes = pl.ds(s * width, width)
        store_rows(u, part, mm_rows(r.normed[:, pl.ds(part * half, half)], r.dhid[:, lanes]))

    def attended_back(a, i):
        need("rows")
        r.datt[spans[i], :] = lowest(mm_back(r.branch[spans[i], :], whole(r.rowsw.at[a])))

    def near_copy(a, u):
        return pltpu.make_async_copy(
            r.og.at[:, :, :, :, own_lanes],
            r.g.at[u, pl.ds(2 * h, 2), :, :, :, pl.ds(half, half)],
            r.quarter_local.at[a],
        )

    def far_copy(a, u, rows_of):
        return remote(
            r.og.at[:, :, :, :, other_lanes],
            r.g.at[u, pl.ds(2 * rows_of, 2), :, :, :, pl.ds(half, half)],
            r.quarter_send.at[a],
            r.quarter_recv.at[a],
            at.sibling,
        )

    def out_gradient(a, u):
        need("attended")
        value = lowest(mm_rows(r.att[a], r.branch[...]))
        r.og[...] = value.reshape(r.og.shape)
        near_copy(a, u).start()
        far_copy(a, u, h).start()

    def end_quarter(a, u):
        near_copy(a, u).wait()
        far_copy(a, u, h).wait_send()
        far_copy(a, u, 1 - h).wait_recv()


    def attend_back(l, blocks):
        need(("mix", l))

        @pl.loop(*blocks, unroll=True)
        def _(b):
            rows = pl.ds(pl.multiple_of(b * SPAN, SPAN), SPAN)
            bias = r.causal[b].T
            bias = jnp.concatenate([bias, bias], axis=1)
            for j in range(half // 128):
                lanes = [pl.ds(part * half + j * 128, 128) for part in range(3)]
                queries, keys, values = [r.mix[rows, lane] for lane in lanes]
                queries = two_heads(queries * SCALING)
                given = two_heads(r.datt[rows, pl.ds(j * 128, 128)])
                shares = softmax_of(mm_back(keys, queries) + bias, 0)
                share_adjoint = mm_back(values, given)
                score_adjoint = lowest(shares * (share_adjoint - jnp.sum(shares * share_adjoint, axis=0, keepdims=True)))
                r.dhid[rows, lanes[0]] = lowest(mm_rows(below(score_adjoint), two_heads(keys * SCALING)))
                r.dhid[rows, lanes[1]] = lowest(mm(score_adjoint, queries))
                r.dhid[rows, lanes[2]] = lowest(mm(lowest(shares), given))

    def mixed_normed(u, e, i, biases):
        need(("g", u))
        need(("g", u + 1))
        rows = spans[i]
        value = mm_back(r.dhid[rows, :width], whole(r.g.at[u]))
        value += mm_back(r.dhid[rows, pl.ds(width, half)], whole(r.g.at[u + 1, :, :, :, :, pl.ds(0, half)]))
        offer(e, i, value)

    def mixed_sums(biases):
        add_own(5 + biases[0], r.dhid[:, :half].astype(jnp.float32))
        add_own(5 + biases[1], r.dhid[:, pl.ds(width, half)].astype(jnp.float32))

    def mixed_gradient(u, part):
        store_rows(u, part, mm_rows(r.normed[:, pl.ds(part * half, half)], r.dhid[:, :width]))

    def value_gradient(u, part):
        value = mm_rows(r.normed[:, pl.ds(part * half, half)], r.dhid[:, pl.ds(width, half)])
        store_rows(u, part, value, pl.ds(0, half))

    def cross_back(b):
        need("queries")
        need("pair")
        rows = pl.ds(b * SPAN, SPAN)
        bias = picture_bias(r.choice[rows, :]).T
        bias = jnp.concatenate([bias, bias], axis=1)
        for j in range(half // 128):
            lanes = pl.ds(j * 128, 128)
            value_lanes = pl.ds(half + j * 128, 128)
            keys, values = r.pr[:, lanes], r.pr[:, value_lanes]
            queries = two_heads(r.qc[rows, lanes] * SCALING)
            given = two_heads(r.datt[rows, lanes])
            shares = softmax_of(mm_back(keys, queries) + bias, 0)
            share_adjoint = mm_back(values, given)
            score_adjoint = lowest(shares * (share_adjoint - jnp.sum(shares * share_adjoint, axis=0, keepdims=True)))
            r.act[rows, lanes] = lowest(mm_rows(below(score_adjoint), two_heads(keys * SCALING)))
            key_adjoint = mm(score_adjoint, queries)
            value_adjoint = mm(lowest(shares), given)
            if b == 0:
                r.hid[0, :, lanes] = key_adjoint
                r.hid[0, :, value_lanes] = value_adjoint
            else:
                r.hid[0, :, lanes] += key_adjoint
                r.hid[0, :, value_lanes] += value_adjoint

    def pair_adjoint():
        r.dhid[:, :width] = lowest(r.hid[0])
        add_own(5 + 13, r.act[:, :half].astype(jnp.float32))
        add_own(5 + 14, r.dhid[:, pl.ds(half, half)].astype(jnp.float32))

    def query_normed(e, i):
        need(("g", 8))
        offer(e, i, mm_back(r.act[spans[i], pl.ds(0, half)], whole(r.g.at[8, :, :, :, :, pl.ds(0, half)])))

    def query_gradient(part):
        value = mm_rows(r.normed[:, pl.ds(part * half, half)], r.act[:, pl.ds(0, half)])
        store_rows(8, part, value, pl.ds(0, half))

    def pic_swap():
        return remote(r.pic_give, r.pic_take, r.swap_send.at[5, 0], r.swap_recv.at[5, 0], at.sibling)

    def picture_back():
        need(("g", 9))
        r.pic_give[...] = lowest(mm_back(r.dhid[others, pl.ds(0, width)], whole(r.g.at[9])))
        pic_swap().start()

    def picture_own():
        r.hid[1, pl.ds(0, ROWS_AT_ONCE), :] = mm_back(r.dhid[mine, pl.ds(0, width)], whole(r.g.at[9]))

    def picture_copy():
        return pltpu.make_async_copy(r.hid.at[1, pl.ds(0, ROWS_AT_ONCE)], r.image_out, r.store.at[UNITS])

    def picture_join():
        pic_swap().wait()
        r.hid[1, pl.ds(0, ROWS_AT_ONCE), :] += r.pic_take[...].astype(jnp.float32)
        picture_copy().start()

    def pair_gradient(part):
        need("images")
        store_rows(9, part, mm_rows(r.img[:, pl.ds(part * half, half)], r.dhid[:, pl.ds(0, width)]))

    def picture_end():
        picture_copy().wait()
        fetch_hidden(0)

    def small_total():
        r.small[...] = r.sums[...].T.reshape(r.small.shape)

    def token_copy():
        return pltpu.make_async_copy(r.dx.at[mine], r.token_out, r.store.at[UNITS + 1])

    segments, ready = [], set()

    def add(work, *args, finished=()):
        def step():
            work(*args)
            ready.update(finished)

        segments.append((step, frozenset()))

    def add_feed(l, n, slot, u, e, bias, after):
        add(begin_branch, bias)
        for s in (0, 1):
            for i in (0, 1):
                add(feed_hidden, l, u + 2 + s, s, i)
            for part in (0, 1):
                add(feed_down, u + 2 + s, s, part, finished=(u + 2 + s,) if part else ())
        for i in (0, 1):
            add(feed_normed, u, i, e)
        add(norm, n, slot)
        for s in (0, 1):
            for part in (0, 1):
                add(feed_up, u + s, s, part, finished=(u + s,) if part else ())
        for i in (0, 1):
            add(join, e, i, n, slot)
        for work in after:
            add(*work)

    def add_attention(l, n, slot, u, e, biases, after):
        add(begin_branch, biases[2])
        for i in (0, 1):
            add(attended_back, l, i)
        add(out_gradient, l, u + 1)
        add(attend_back, l, (0, 2))
        add(attend_back, l, (2, 4))
        for i in (0, 1):
            add(mixed_normed, u, e, i, biases)
        add(norm, n, slot)
        for part in (0, 1):
            add(mixed_gradient, u, part, finished=(u,) if part else ())
        for part in (0, 1):
            add(value_gradient, u + 1, part)
        add(end_quarter, l, u + 1, finished=(u + 1,))
        add(mixed_sums, biases)
        for i in (0, 1):
            add(join, e, i, n, slot)
        for work in after:
            add(*work)

    add(start)
    add_feed(1, 4, 0, 10, 0, 12, [(fetch_residual, 2, 0)])
    add(begin_branch, 15)
    for i in (0, 1):
        add(attended_back, 2, i)
    add(out_gradient, 2, 8)
    for b in range(tokens // SPAN):
        add(cross_back, b)
    add(pair_adjoint)
    for i in (0, 1):
        add(query_normed, 1, i)
    add(picture_back)
    add(picture_own)
    for part in (0, 1):
        add(pair_gradient, part, finished=(9,) if part else ())
    add(norm, 3, 1)
    for part in (0, 1):
        add(query_gradient, part)
    add(end_quarter, 2, 8, finished=(8,))
    for i in (0, 1):
        add(join, 1, i, 3, 1)
    add(picture_join)
    add(fetch_residual, 1, 1)
    add_attention(1, 2, 0, 6, 2, (9, 10, 11), [(picture_end,), (fetch_residual, 0, 0), (fetch_mixed, 0)])
    add_feed(0, 1, 1, 2, 3, 8, [])
    add_attention(0, 0, 0, 0, 4, (5, 6, 7), [])
    add(small_total, finished=(SMALL,))
    add(lambda: token_copy().start())

    def end_unit(u):
        if u == SMALL:
            r.small_out[...] = r.small[at.z, at.y, at.x]
        else:
            pltpu.make_async_copy(r.g.at[u, at.z, at.y, at.x], r.sums_out.at[u], r.store.at[u]).start()

    def move(u, k):
        assert u in ready
        scatter.round(u, k, end_unit)

    play(SCATTER_ORDER, segments, move)
    for u in BACK_UNITS:
        scatter.drain(u)
        if u != SMALL:
            pltpu.make_async_copy(r.g.at[u, at.z, at.y, at.x], r.sums_out.at[u], r.store.at[u]).wait()
    token_copy().wait()


def backward(full, table, residuals, mixed, attended, queries, pair, hidden, out_rows, cotangent, images, causal, choice):
    units, rows, width = full.shape[0], full.shape[4], full.shape[5]
    count = 2 * cotangent.shape[0]
    half = width // 2
    bf, fl = jnp.bfloat16, jnp.float32
    shape = jax.ShapeDtypeStruct
    dma = pltpu.SemaphoreType.DMA
    shapes, pick = spare_shapes(rows, width, 128)
    anywhere, here = pl.BlockSpec(memory_space=pl.ANY), pl.BlockSpec(memory_space=pltpu.VMEM)
    return pl.pallas_call(
        partial(backward_kernel, pick=pick, spares=len(shapes)),
        out_shape=(
            shape((units, rows, width), bf),
            shape((rows, 128), fl),
            shape((count // 2, width), fl),
            shape((count // 2, width), fl),
        ),
        in_specs=[anywhere] * 11 + [here] * 2,
        out_specs=[anywhere, here, anywhere, anywhere],
        scratch_shapes=[
            pltpu.VMEM(full.shape, bf),
            pltpu.VMEM((128, width), fl),
            pltpu.VMEM((count, width), fl),
            pltpu.VMEM((count, width), bf),
            pltpu.VMEM((2, count, width), fl),
            pltpu.VMEM((count, 1), fl),
            pltpu.VMEM((count, width), bf),
            pltpu.VMEM((2, count, width), fl),
            pltpu.VMEM((count, 2 * width), bf),
            pltpu.VMEM((count, 2 * width), bf),
            pltpu.VMEM((count, width + half), bf),
            pltpu.VMEM((3, count, half), bf),
            pltpu.VMEM((count, half), bf),
            pltpu.VMEM((count, half), bf),
            pltpu.VMEM((count, width), bf),
            pltpu.VMEM(out_rows.shape, bf),
            pltpu.VMEM((count, width), bf),
            pltpu.VMEM((2, count, width), bf),
            pltpu.VMEM((2, count, width), bf),
            pltpu.VMEM((count // 2, width), bf),
            pltpu.VMEM((count // 2, width), bf),
            pltpu.VMEM(out_rows.shape[1:], bf),
            pltpu.VMEM((128, width), fl),
            pltpu.VMEM((4, 2, 2, rows, 128), fl),
            dma((units + 1, 8)),
            dma((units + 1, 8)),
            dma((6, 2)),
            dma((6, 2)),
            dma((3,)),
            dma((3,)),
            dma((3,)),
            dma((40,)),
            dma((units + 2,)),
            dma((2,)),
            dma((2,)),
            *shapes,
        ],
        compiler_params=pltpu.CompilerParams(collective_id=1, has_side_effects=True, vmem_limit_bytes=63 << 20),
    )(full, table, residuals, mixed, attended, queries, pair, hidden, out_rows, cotangent, images, causal, choice)


def swap_cores(value):
    return lax.ppermute(value, "heads", [(0, 1), (1, 0)])


def both_cores(value, member):
    other = swap_cores(value)
    return jnp.stack([jnp.where(member == 0, value, other), jnp.where(member == 0, other, value)])


def to_units(member, self_weight, self_out_weight, up_weight, query_weight, pair_weight, cross_out_weight):
    width = self_weight.shape[1 + 1] // 3
    half = width // 2
    rows = self_weight.shape[1]
    own = slice(member * half, member * half + half)
    value = slice(width + member * half, width + member * half + half)
    units = []
    for layer in (0, 1):
        weight = self_weight[layer]
        units.append(jnp.concatenate([weight[:, own], weight[:, value]], axis=1))
        units.append(jnp.concatenate([weight[:, 2 * width + member * half : 2 * width + member * half + half], self_out_weight[layer][:, own]], axis=1))
        up = up_weight[layer].reshape(rows, CHIPS, 2, 2, -1)[:, :, member]
        units.append(up[:, :, 0].reshape(rows, width))
        units.append(up[:, :, 1].reshape(rows, width))
    units.append(jnp.concatenate([query_weight[:, own], cross_out_weight[:, own]], axis=1))
    units.append(jnp.concatenate([pair_weight[:, own], pair_weight[:, value]], axis=1))
    return jnp.stack(units)


UNIT_OF_PIECE = (0, 1, 2, 3, 6, 7, 10, 11, 8, 9)


def chip_blocks(member, pieces, down_weight):
    theirs, ours = (
        jnp.where(member == 0, pieces[1], pieces[0]),
        jnp.where(member == 0, pieces[0], pieces[1]),
    )
    rows = jnp.concatenate(list(both_rows(member, ours, swap_cores(theirs))), axis=1)
    down = down_weight.reshape(2, 2, rows.shape[1], rows.shape[2])
    order = {u: rows[i] for i, u in enumerate(UNIT_OF_PIECE)}
    order.update({4: down[0, 0], 5: down[0, 1], 12: down[1, 0], 13: down[1, 1]})
    return jnp.stack([order[u] for u in range(UNITS)])


def both_rows(member, ours, other):
    return jnp.where(member == 0, ours, other), jnp.where(member == 0, other, ours)


def chip_program(
    tokens,
    images,
    segment_labels,
    image_index,
    cotangent,
    norm_gain,
    vector_bias,
    up_bias,
    self_weight,
    self_out_weight,
    up_weight,
    down_weight,
    query_weight,
    pair_weight,
    cross_out_weight,
):
    member = lax.axis_index("heads")
    rows, length, width = tokens.shape
    half = width // 2
    slim = self_weight.shape[1]
    matrices = (self_weight, self_out_weight, up_weight, query_weight, pair_weight, cross_out_weight)
    blocks = chip_blocks(member, [to_units(m, *matrices) for m in (0, 1)], down_weight)
    vectors = jnp.concatenate([norm_gain, vector_bias], axis=0)
    vectors = jnp.concatenate(list(both_cores(vectors, member)), axis=1)
    vectors = jnp.concatenate([vectors, up_bias.reshape(4, 2 * slim)], axis=0)
    small = jnp.pad(vectors, ((0, 128 - vectors.shape[0]), (0, 0))).T
    own_tokens, own_images, own_cotangent = (value.reshape(-1, width) for value in (tokens, images, cotangent))
    chip_rows = segment_labels.shape[0]
    labels = jnp.arange(image_index.shape[1])
    caption_image = jnp.sum(
        jnp.where(segment_labels[:, :, None] == labels[None, None, :], image_index[:, None, :], 0), axis=-1, dtype=jnp.int32
    )
    count = chip_rows * length
    span_rows = SPAN // length
    row_of = jnp.arange(SPAN) // length
    same = row_of[:, None] == row_of[None, :]
    span_labels = segment_labels.reshape(-1, SPAN)
    causal = (span_labels[:, :, None] == span_labels[:, None, :]) & (same & (jnp.arange(SPAN)[:, None] >= jnp.arange(SPAN)[None, :]))[None]
    causal = jnp.where(causal, 0.0, masked_score).astype(jnp.float32)
    choice = jnp.broadcast_to(caption_image.reshape(count, 1).astype(jnp.float32), (count, 128))
    full, table, residuals, mixed, attended, queries, pair, hidden, out_rows, layer_out = forward(
        blocks, small, own_tokens, own_images, causal, choice
    )
    sums, small_sums, token_gradient, image_gradient = backward(
        full, table, residuals, mixed, attended, queries, pair, hidden, out_rows, own_cotangent, own_images, causal, choice
    )
    outs = finish(member, sums.astype(jnp.float32), small_sums, slim, width)
    mine = (layer_out.reshape(rows, length, width), token_gradient.reshape(rows, length, width), image_gradient[None])
    return mine + outs


def finish(member, sums, small_sums, slim, width):
    half = width // 2
    pieces = jnp.stack([sums[u] for u in UNIT_OF_PIECE]).reshape(len(UNIT_OF_PIECE), 2, slim, width)
    ours, theirs = pieces[:, member], pieces[:, 1 - member]
    both = jnp.stack(list(both_rows(member, ours, swap_cores(theirs))))

    def halves(piece, side):
        return jnp.concatenate([both[0, piece][:, side * half : (side + 1) * half], both[1, piece][:, side * half : (side + 1) * half]], axis=1)

    def up(piece):
        parts = [both[:, piece + s].reshape(2, slim, CHIPS, 2 * slim) for s in (0, 1)]
        return jnp.stack(parts, axis=0).transpose(2, 3, 1, 0, 4).reshape(slim, 4 * width)

    self_weight = jnp.stack([jnp.concatenate([halves(p, 0), halves(p, 1), halves(p + 1, 0)], axis=1) for p in (0, 4)])
    self_out = jnp.stack([halves(p, 1) for p in (1, 5)])
    up_gradient = jnp.stack([up(2), up(6)])
    down = jnp.stack([jnp.concatenate([sums[u], sums[u + 1]]) for u in (4, 12)])
    pair = jnp.concatenate([halves(9, 0), halves(9, 1)], axis=1)
    table = small_sums.T
    shared = table[:21]
    other = swap_cores(shared)
    split = jnp.zeros((21, 1), bool).at[jnp.array([5 + n for n in (5, 6, 9, 10, 13, 14)])].set(True)
    shared = jnp.where(split, shared + other, shared)
    shared = lax.dynamic_slice_in_dim(shared, member * slim, slim, 1)
    up_bias = table[21:25].reshape(2, 4 * slim)
    return (shared[:5], shared[5:], up_bias, self_weight, self_out, up_gradient, down, halves(8, 0), pair, halves(8, 1))


def solution(mesh):
    in_specs = (
        P(("dp", "heads"), None, None),
        P(("dp", "heads"), None, None),
        P("dp", None),
        P("dp", None),
        P(("dp", "heads"), None, None),
        P(None, ("dp", "heads")),
        P(None, ("dp", "heads")),
        P(None, ("dp", "heads")),
        P(None, ("dp", "heads"), None),
        P(None, ("dp", "heads"), None),
        P(None, ("dp", "heads"), None),
        P(None, ("dp", "heads"), None),
        P(("dp", "heads"), None),
        P(("dp", "heads"), None),
        P(("dp", "heads"), None),
    )
    out_specs = (
        P(("dp", "heads"), None, None),
        P(("dp", "heads"), None, None),
        P(("dp", "heads"), None, None),
        P(None, ("dp", "heads")),
        P(None, ("dp", "heads")),
        P(None, ("dp", "heads")),
        P(None, ("dp", "heads"), None),
        P(None, ("dp", "heads"), None),
        P(None, ("dp", "heads"), None),
        P(None, ("dp", "heads"), None),
        P(("dp", "heads"), None),
        P(("dp", "heads"), None),
        P(("dp", "heads"), None),
    )
    dp, cores = mesh.shape["dp"], mesh.shape["heads"]
    program = chip_program if (dp, cores) == (CHIPS, 2) else per_device
    return jax.shard_map(
        program, mesh=mesh, in_specs=in_specs, out_specs=out_specs, check_vma=False
    )
```

```python
from functools import partial
import math
from typing import Any, NamedTuple

import jax
import jax.numpy as jnp
from jax import lax
from jax.experimental import pallas as pl
from jax.experimental.pallas import tpu as pltpu
from jax.sharding import PartitionSpec as P

HEADS = 12
HEAD = 64


masked_score = -1e30


def layer_norm(residual, gain, shift):
    center = residual - jnp.mean(residual, axis=-1, keepdims=True)
    variance = jnp.mean(center * center, axis=-1, keepdims=True)
    return center * lax.rsqrt(variance + 1e-05) * gain + shift


def project(left, weight):
    return jnp.einsum("rld,de->rle", left, weight, preferred_element_type=jnp.float32)


def weight_adjoint(left, adjoint):
    return jnp.einsum("rld,rle->de", left, adjoint, preferred_element_type=jnp.float32)


def project_back(adjoint, weight):
    return jnp.einsum("rle,de->rld", adjoint, weight, preferred_element_type=jnp.float32)


def column_total(adjoint):
    return jnp.sum(adjoint, axis=(0, 1), dtype=jnp.float32)


def norm_back(residual, gain, shift, adjoint):
    unused, pull = jax.vjp(layer_norm, residual, gain, shift)
    return pull(adjoint)


def rows_to_heads(pieces):
    return lax.all_to_all(pieces, "heads", split_axis=3, concat_axis=0, tiled=True)


def heads_to_rows(pieces):
    return lax.all_to_all(pieces, "heads", split_axis=0, concat_axis=3, tiled=True)


def adjoint_to_heads(pieces):
    return lax.all_to_all(pieces, "heads", split_axis=3, concat_axis=0, tiled=True)


def adjoint_to_rows(pieces):
    return lax.all_to_all(pieces, "heads", split_axis=0, concat_axis=3, tiled=True)


def softmax_parts(scores):
    peak = jnp.max(scores, axis=-1, keepdims=True)
    log_total = peak + jnp.log(jnp.sum(jnp.exp(scores - peak), axis=-1, keepdims=True))
    return (jnp.exp(scores - log_total), log_total)


def softmax_back(shares, adjoint):
    return (shares * (adjoint - jnp.sum(shares * adjoint, axis=-1, keepdims=True))).astype(
        jnp.bfloat16
    )


def self_scores(queries, keys, allowed):
    scores = jnp.einsum(
        "rqhd,rkhd->rhqk", queries, keys, preferred_element_type=jnp.float32
    ) * HEAD ** (-0.5)
    return jnp.where(allowed[:, None], scores, masked_score)


def self_heads_forward(queries, keys, values, allowed):
    shares, log_total = softmax_parts(self_scores(queries, keys, allowed))
    attended = jnp.einsum(
        "rhqk,rkhd->rqhd", shares.astype(jnp.bfloat16), values, preferred_element_type=jnp.float32
    )
    return (attended.astype(jnp.bfloat16), log_total)


def self_heads_back(queries, keys, values, allowed, log_total, adjoint):
    shares = jnp.exp(self_scores(queries, keys, allowed) - log_total)
    value_adjoint = jnp.einsum(
        "rhqk,rqhd->rkhd", shares.astype(jnp.bfloat16), adjoint, preferred_element_type=jnp.float32
    )
    share_adjoint = jnp.einsum(
        "rqhd,rkhd->rhqk", adjoint, values, preferred_element_type=jnp.float32
    )
    score_adjoint = softmax_back(shares, share_adjoint)
    scale = HEAD ** (-0.5)
    query_adjoint = (
        jnp.einsum("rhqk,rkhd->rqhd", score_adjoint, keys, preferred_element_type=jnp.float32)
        * scale
    )
    key_adjoint = (
        jnp.einsum("rhqk,rqhd->rkhd", score_adjoint, queries, preferred_element_type=jnp.float32)
        * scale
    )
    return (
        query_adjoint.astype(jnp.bfloat16),
        key_adjoint.astype(jnp.bfloat16),
        value_adjoint.astype(jnp.bfloat16),
    )


def cross_scores(queries, image_keys, chosen):
    rows, length, heads, head_size = queries.shape
    scores = jnp.einsum(
        "rqhd,gkhd->rhqgk", queries, image_keys, preferred_element_type=jnp.float32
    ) * HEAD ** (-0.5)
    scores = jnp.where(chosen[:, None, :, :, None], scores, masked_score)
    return scores.reshape(rows, heads, length, -1)


def block_rows(rows, length):
    return math.gcd(rows, max(1, 512 // length))


def cross_heads_forward(queries, image_keys, image_values, chosen):
    rows, length, heads, head_size = queries.shape
    block = block_rows(rows, length)
    flat_values = image_values.reshape(-1, heads, head_size)

    def one_block(inputs):
        block_queries, block_chosen = inputs
        shares, log_total = softmax_parts(cross_scores(block_queries, image_keys, block_chosen))
        attended = jnp.einsum(
            "rhqc,chd->rqhd",
            shares.astype(jnp.bfloat16),
            flat_values,
            preferred_element_type=jnp.float32,
        )
        return (attended.astype(jnp.bfloat16), log_total)

    blocked = (
        queries.reshape(rows // block, block, length, heads, head_size),
        chosen.reshape(rows // block, block, length, -1),
    )
    attended, log_total = lax.map(one_block, blocked)
    return (attended.reshape(queries.shape), log_total)


def cross_heads_back(queries, image_keys, image_values, chosen, log_total, adjoint):
    rows, length, heads, head_size = queries.shape
    block = block_rows(rows, length)
    flat_keys = image_keys.reshape(-1, heads, head_size)
    flat_values = image_values.reshape(-1, heads, head_size)
    scale = HEAD ** (-0.5)

    def one_block(carry, inputs):
        key_total, value_total = carry
        block_queries, block_chosen, block_log, block_adjoint = inputs
        shares = jnp.exp(cross_scores(block_queries, image_keys, block_chosen) - block_log)
        value_total = value_total + jnp.einsum(
            "rhqc,rqhd->chd",
            shares.astype(jnp.bfloat16),
            block_adjoint,
            preferred_element_type=jnp.float32,
        )
        share_adjoint = jnp.einsum(
            "rqhd,chd->rhqc", block_adjoint, flat_values, preferred_element_type=jnp.float32
        )
        score_adjoint = softmax_back(shares, share_adjoint)
        key_total = (
            key_total
            + jnp.einsum(
                "rhqc,rqhd->chd", score_adjoint, block_queries, preferred_element_type=jnp.float32
            )
            * scale
        )
        query_adjoint = (
            jnp.einsum(
                "rhqc,chd->rqhd", score_adjoint, flat_keys, preferred_element_type=jnp.float32
            )
            * scale
        )
        return ((key_total, value_total), query_adjoint.astype(jnp.bfloat16))

    start = jnp.zeros(flat_keys.shape, jnp.float32)
    blocked = (
        queries.reshape(rows // block, block, length, heads, head_size),
        chosen.reshape(rows // block, block, length, -1),
        log_total,
        adjoint.reshape(rows // block, block, length, heads, head_size),
    )
    (key_total, value_total), query_adjoint = lax.scan(one_block, (start, start), blocked)
    return (
        query_adjoint.reshape(queries.shape),
        key_total.astype(jnp.bfloat16),
        value_total.astype(jnp.bfloat16),
    )


def self_forward(
    residual, allowed, gain, shift, weight, query_bias, value_bias, out_weight, out_bias, groups
):
    rows, length, width = residual.shape
    span = width // groups
    normed = layer_norm(residual, gain, shift).astype(jnp.bfloat16)
    offset = jnp.concatenate([query_bias, jnp.zeros_like(query_bias), value_bias])
    mixed = (project(normed, weight) + offset).astype(jnp.bfloat16)
    gathered = rows_to_heads(mixed.reshape(rows, length, 3, groups, span))
    gathered = gathered.reshape(rows * groups, length, 3, HEADS // groups, HEAD)
    queries, keys, values = (gathered[:, :, 0], gathered[:, :, 1], gathered[:, :, 2])
    attended, log_total = self_heads_forward(queries, keys, values, allowed)
    merged = heads_to_rows(attended.reshape(rows * groups, length, 1, 1, span)).reshape(
        rows, length, width
    )
    kept = (residual, normed, queries, keys, values, log_total, merged)
    return (residual + project(merged, out_weight) + out_bias, kept)


def self_backward(adjoint, kept, gain, shift, weight, out_weight, allowed, groups):
    residual, normed, queries, keys, values, log_total, merged = kept
    rows, length, width = residual.shape
    span = width // groups
    branch = adjoint.astype(jnp.bfloat16)
    out_bias_adjoint = column_total(branch)
    merged_adjoint = project_back(branch, out_weight).astype(jnp.bfloat16)
    head_adjoint = adjoint_to_heads(merged_adjoint.reshape(rows, length, 1, groups, span))
    head_adjoint = head_adjoint.reshape(rows * groups, length, HEADS // groups, HEAD)
    query_adjoint, key_adjoint, value_adjoint = self_heads_back(
        queries, keys, values, allowed, log_total, head_adjoint
    )
    stacked = jnp.stack([query_adjoint, key_adjoint, value_adjoint], axis=2).reshape(
        rows * groups, length, 3, 1, span
    )
    mixed_adjoint = adjoint_to_rows(stacked).reshape(rows, length, 3 * width)
    offset_adjoint = column_total(mixed_adjoint)
    residual_adjoint, gain_adjoint, shift_adjoint = norm_back(
        residual, gain, shift, project_back(mixed_adjoint, weight)
    )
    pairs = ((normed, mixed_adjoint), (merged, branch))
    small = (
        gain_adjoint,
        shift_adjoint,
        offset_adjoint[:width],
        offset_adjoint[2 * width :],
        out_bias_adjoint,
    )
    return (adjoint + residual_adjoint, pairs, small)


def cross_forward(
    residual,
    pictures,
    chosen,
    gain,
    shift,
    weight,
    query_bias,
    pair_matrix,
    value_bias,
    out_weight,
    out_bias,
    groups,
    member,
):
    rows, length, width = residual.shape
    span = width // groups
    key_weight = lax.dynamic_slice_in_dim(pair_matrix, member * span, span, 1)
    value_weight = lax.dynamic_slice_in_dim(pair_matrix, width + member * span, span, 1)
    value_shift = lax.dynamic_slice_in_dim(value_bias, member * span, span, 0)
    layout = (pictures.shape[0], pictures.shape[1], HEADS // groups, HEAD)
    image_keys = project(pictures, key_weight).astype(jnp.bfloat16).reshape(layout)
    image_values = (
        (project(pictures, value_weight) + value_shift).astype(jnp.bfloat16).reshape(layout)
    )
    normed = layer_norm(residual, gain, shift).astype(jnp.bfloat16)
    query_rows = (project(normed, weight) + query_bias).astype(jnp.bfloat16)
    queries = rows_to_heads(query_rows.reshape(rows, length, 1, groups, span))
    queries = queries.reshape(rows * groups, length, HEADS // groups, HEAD)
    attended, log_total = cross_heads_forward(queries, image_keys, image_values, chosen)
    merged = heads_to_rows(attended.reshape(rows * groups, length, 1, 1, span)).reshape(
        rows, length, width
    )
    kept = (residual, normed, queries, image_keys, image_values, log_total, merged)
    return (residual + project(merged, out_weight) + out_bias, kept)


def cross_backward(
    adjoint, kept, pictures, chosen, gain, shift, weight, pair_matrix, out_weight, groups, member
):
    residual, normed, queries, image_keys, image_values, log_total, merged = kept
    rows, length, width = residual.shape
    span = width // groups
    key_weight = lax.dynamic_slice_in_dim(pair_matrix, member * span, span, 1)
    value_weight = lax.dynamic_slice_in_dim(pair_matrix, width + member * span, span, 1)
    branch = adjoint.astype(jnp.bfloat16)
    out_bias_adjoint = column_total(branch)
    merged_adjoint = project_back(branch, out_weight).astype(jnp.bfloat16)
    head_adjoint = adjoint_to_heads(merged_adjoint.reshape(rows, length, 1, groups, span))
    head_adjoint = head_adjoint.reshape(rows * groups, length, HEADS // groups, HEAD)
    query_adjoint, key_adjoint, value_adjoint = cross_heads_back(
        queries, image_keys, image_values, chosen, log_total, head_adjoint
    )
    query_rows = adjoint_to_rows(query_adjoint.reshape(rows * groups, length, 1, 1, span)).reshape(
        rows, length, width
    )
    query_bias_adjoint = column_total(query_rows)
    residual_adjoint, gain_adjoint, shift_adjoint = norm_back(
        residual, gain, shift, project_back(query_rows, weight)
    )
    layout = (pictures.shape[0], pictures.shape[1], span)
    key_adjoint = key_adjoint.reshape(layout)
    value_adjoint = value_adjoint.reshape(layout)
    value_bias_adjoint = lax.dynamic_update_slice_in_dim(
        jnp.zeros((width,), jnp.float32), column_total(value_adjoint), member * span, 0
    )
    picture_adjoint = project_back(key_adjoint, key_weight) + project_back(
        value_adjoint, value_weight
    )
    pairs = ((normed, query_rows), (merged, branch), (key_adjoint, value_adjoint))
    small = (gain_adjoint, shift_adjoint, query_bias_adjoint, value_bias_adjoint, out_bias_adjoint)
    return (adjoint + residual_adjoint, pairs, small, picture_adjoint)


def feed_forward(residual, gain, shift, up_matrix, up_shift, down_matrix, down_shift):
    normed = layer_norm(residual, gain, shift).astype(jnp.bfloat16)
    hidden = project(normed, up_matrix) + up_shift
    active = jax.nn.gelu(hidden, approximate=True).astype(jnp.bfloat16)
    return (
        residual + project(active, down_matrix) + down_shift,
        (residual, normed, hidden, active),
    )


def feed_backward(adjoint, kept, gain, shift, up_matrix, down_matrix):
    residual, normed, hidden, active = kept
    branch = adjoint.astype(jnp.bfloat16)
    down_shift_adjoint = column_total(branch)
    unused, pull = jax.vjp(partial(jax.nn.gelu, approximate=True), hidden)
    hidden_adjoint = pull(project_back(branch, down_matrix))[0].astype(jnp.bfloat16)
    up_shift_adjoint = column_total(hidden_adjoint)
    residual_adjoint, gain_adjoint, shift_adjoint = norm_back(
        residual, gain, shift, project_back(hidden_adjoint, up_matrix)
    )
    pairs = ((normed, hidden_adjoint), (active, branch))
    small = (gain_adjoint, shift_adjoint, up_shift_adjoint, down_shift_adjoint)
    return (adjoint + residual_adjoint, pairs, small)


def per_device(
    tokens,
    images,
    segment_labels,
    image_index,
    cotangent,
    norm_gain,
    vector_bias,
    up_bias,
    self_weight,
    self_out_weight,
    up_weight,
    down_weight,
    query_weight,
    pair_weight,
    cross_out_weight,
):
    groups = lax.axis_size("heads")
    member = lax.axis_index("heads")
    everyone = lax.axis_size(("dp", "heads"))
    length = segment_labels.shape[1]
    position = jnp.arange(length)
    allowed = (segment_labels[:, :, None] == segment_labels[:, None, :]) & (
        position[:, None] >= position[None, :]
    )[None]
    labels = jnp.arange(image_index.shape[1])
    caption_image = jnp.sum(
        jnp.where(segment_labels[:, :, None] == labels[None, None, :], image_index[:, None, :], 0),
        axis=-1,
        dtype=jnp.int32,
    )
    pictures = lax.all_gather(images, "heads", axis=0, tiled=True)
    chosen = caption_image[:, :, None] == jnp.arange(pictures.shape[0])[None, None, :]
    first = (
        lax.all_gather(self_weight[0], ("dp", "heads"), axis=0, tiled=True),
        lax.all_gather(self_out_weight[0], ("dp", "heads"), axis=0, tiled=True),
        lax.all_gather(up_weight[0], ("dp", "heads"), axis=0, tiled=True),
        lax.all_gather(down_weight[0], ("dp", "heads"), axis=0, tiled=True),
        lax.all_gather(norm_gain, ("dp", "heads"), axis=1, tiled=True),
        lax.all_gather(vector_bias, ("dp", "heads"), axis=1, tiled=True),
        lax.all_gather(up_bias, ("dp", "heads"), axis=1, tiled=True),
    )
    gains = first[4].astype(jnp.float32)
    biases = first[5].astype(jnp.float32)
    up_biases = first[6].astype(jnp.float32)
    residual = tokens.astype(jnp.float32)
    residual, kept_self_one = self_forward(
        residual,
        allowed,
        gains[0],
        biases[0],
        first[0],
        biases[5],
        biases[6],
        first[1],
        biases[7],
        groups,
    )
    residual, kept_feed_one = feed_forward(
        residual, gains[1], biases[1], first[2], up_biases[0], first[3], biases[8]
    )
    second = (
        lax.all_gather(self_weight[1], ("dp", "heads"), axis=0, tiled=True),
        lax.all_gather(self_out_weight[1], ("dp", "heads"), axis=0, tiled=True),
        lax.all_gather(up_weight[1], ("dp", "heads"), axis=0, tiled=True),
        lax.all_gather(down_weight[1], ("dp", "heads"), axis=0, tiled=True),
        lax.all_gather(query_weight, ("dp", "heads"), axis=0, tiled=True),
        lax.all_gather(pair_weight, ("dp", "heads"), axis=0, tiled=True),
        lax.all_gather(cross_out_weight, ("dp", "heads"), axis=0, tiled=True),
    )
    residual, kept_self_two = self_forward(
        residual,
        allowed,
        gains[2],
        biases[2],
        second[0],
        biases[9],
        biases[10],
        second[1],
        biases[11],
        groups,
    )
    residual, kept_cross = cross_forward(
        residual,
        pictures,
        chosen,
        gains[3],
        biases[3],
        second[4],
        biases[13],
        second[5],
        biases[14],
        second[6],
        biases[15],
        groups,
        member,
    )
    residual, kept_feed_two = feed_forward(
        residual, gains[4], biases[4], second[2], up_biases[1], second[3], biases[12]
    )
    second = (
        lax.all_gather(self_weight[1], ("dp", "heads"), axis=0, tiled=True),
        lax.all_gather(self_out_weight[1], ("dp", "heads"), axis=0, tiled=True),
        lax.all_gather(up_weight[1], ("dp", "heads"), axis=0, tiled=True),
        lax.all_gather(down_weight[1], ("dp", "heads"), axis=0, tiled=True),
        lax.all_gather(query_weight, ("dp", "heads"), axis=0, tiled=True),
        lax.all_gather(pair_weight, ("dp", "heads"), axis=0, tiled=True),
        lax.all_gather(cross_out_weight, ("dp", "heads"), axis=0, tiled=True),
    )
    adjoint = cotangent.astype(jnp.float32)
    adjoint, feed_two, feed_two_small = feed_backward(
        adjoint, kept_feed_two, gains[4], biases[4], second[2], second[3]
    )
    adjoint, cross_pairs, cross_small, picture_adjoint = cross_backward(
        adjoint,
        kept_cross,
        pictures,
        chosen,
        gains[3],
        biases[3],
        second[4],
        second[5],
        second[6],
        groups,
        member,
    )
    image_gradient = lax.psum_scatter(
        picture_adjoint.astype(jnp.bfloat16), "heads", scatter_dimension=0, tiled=True
    ).astype(jnp.float32)
    adjoint, self_two, self_two_small = self_backward(
        adjoint, kept_self_two, gains[2], biases[2], second[0], second[1], allowed, groups
    )
    first = (
        lax.all_gather(self_weight[0], ("dp", "heads"), axis=0, tiled=True),
        lax.all_gather(self_out_weight[0], ("dp", "heads"), axis=0, tiled=True),
        lax.all_gather(up_weight[0], ("dp", "heads"), axis=0, tiled=True),
        lax.all_gather(down_weight[0], ("dp", "heads"), axis=0, tiled=True),
        lax.all_gather(norm_gain, ("dp", "heads"), axis=1, tiled=True),
    )
    back_gains = first[4].astype(jnp.float32)
    adjoint, feed_one, feed_one_small = feed_backward(
        adjoint, kept_feed_one, back_gains[1], biases[1], first[2], first[3]
    )
    adjoint, self_one, self_one_small = self_backward(
        adjoint, kept_self_one, back_gains[0], biases[0], first[0], first[1], allowed, groups
    )
    width = tokens.shape[2]
    hidden_width = feed_one[0][1].shape[2]
    span = width // groups
    row_pairs = (
        self_one[0],
        self_one[1],
        feed_one[0],
        self_two[0],
        self_two[1],
        feed_two[0],
        cross_pairs[0],
    )
    key_adjoint, value_adjoint = cross_pairs[2]
    blocks = []
    for left, right in row_pairs:
        blocks.append(weight_adjoint(left, right))
    pair_block = jnp.zeros(
        (width // everyone * lax.axis_size(("dp", "heads")), 2 * width), jnp.float32
    )
    pair_block = lax.dynamic_update_slice_in_dim(
        pair_block, weight_adjoint(pictures, key_adjoint), member * span, 1
    )
    pair_block = lax.dynamic_update_slice_in_dim(
        pair_block, weight_adjoint(pictures, value_adjoint), width + member * span, 1
    )
    blocks.append(pair_block)
    left, right = cross_pairs[1]
    blocks.append(weight_adjoint(left, right))
    row_sums = lax.psum_scatter(
        jnp.concatenate(blocks, axis=1), ("dp", "heads"), scatter_dimension=0, tiled=True
    )
    blocks = []
    for left, right in (feed_one[1], feed_two[1]):
        blocks.append(weight_adjoint(left, right))
    down_sums = lax.psum_scatter(
        jnp.concatenate(blocks, axis=1), ("dp", "heads"), scatter_dimension=0, tiled=True
    )
    down_sums = jnp.transpose(down_sums.reshape(down_sums.shape[0], 2, width), (1, 0, 2))
    columns = (
        3 * width,
        width,
        hidden_width,
        3 * width,
        width,
        hidden_width,
        width,
        2 * width,
        width,
    )
    pieces = []
    offset = 0
    for span_width in columns:
        pieces.append(row_sums[:, offset : offset + span_width])
        offset = offset + span_width
    gain_rows = jnp.stack(
        [self_one_small[0], feed_one_small[0], self_two_small[0], cross_small[0], feed_two_small[0]]
    )
    bias_rows = jnp.stack(
        [
            self_one_small[1],
            feed_one_small[1],
            self_two_small[1],
            cross_small[1],
            feed_two_small[1],
            self_one_small[2],
            self_one_small[3],
            self_one_small[4],
            feed_one_small[3],
            self_two_small[2],
            self_two_small[3],
            self_two_small[4],
            feed_two_small[3],
            cross_small[2],
            cross_small[3],
            cross_small[4],
        ]
    )
    up_rows = jnp.stack([feed_one_small[2], feed_two_small[2]])
    small_sums = (
        lax.psum_scatter(gain_rows, ("dp", "heads"), scatter_dimension=1, tiled=True),
        lax.psum_scatter(bias_rows, ("dp", "heads"), scatter_dimension=1, tiled=True),
        lax.psum_scatter(up_rows, ("dp", "heads"), scatter_dimension=1, tiled=True),
    )
    return (
        residual,
        adjoint,
        image_gradient,
        small_sums[0],
        small_sums[1],
        small_sums[2],
        jnp.stack([pieces[0], pieces[3]]),
        jnp.stack([pieces[1], pieces[4]]),
        jnp.stack([pieces[2], pieces[5]]),
        down_sums,
        pieces[6],
        pieces[7],
        pieces[8],
    )


MESH = pl.DeviceIdType.MESH
CHIPS = 16
UNITS = 14
SMALL = UNITS
GATHER_ROUTES = ("zyx", "zxy", "yxz", "zxy", "zyx", "zxy", "zyx", "xyz", "zyx", "zxy", "zyx", "xyz", "zxy", "yxz", "zxy")
SCATTER_ROUTES = ("zyx", "zyx", "zxy", "zxy", "yxz", "zyx", "zxy", "zyx", "xyz", "zyx", "zxy", "xyz", "zxy", "zyx", "zxy")
ROUNDS = 6


class Place:
    def __init__(self):
        dp = lax.axis_index("dp")
        self.dp = dp
        self.h = lax.axis_index("heads")
        self.x = lax.rem(dp, 2)
        self.y = lax.rem(dp // 2, 2)
        self.z = dp // 4
        self.to_x = (dp + 1 - 2 * self.x, self.h)
        self.to_y = (dp + 2 - 4 * self.y, self.h)
        self.above = (dp + 4, self.h)
        self.below = (dp - 4, self.h)
        self.sibling = (dp, 1 - self.h)

    def barrier(self, sibling=False):
        bar = pltpu.get_barrier_semaphore()

        def greet(device):
            pl.semaphore_signal(bar, inc=1, device_id=device, device_id_type=MESH)

        greet(self.to_x)
        greet(self.to_y)
        if sibling:
            greet(self.sibling)
        pl.when(self.z < 3)(lambda: greet(self.above))
        pl.when(self.z > 0)(lambda: greet(self.below))
        peers = (3 if sibling else 2) + jnp.where(self.z < 3, 1, 0) + jnp.where(self.z > 0, 1, 0)
        pl.semaphore_wait(bar, peers)


def remote(source, target, send, recv, device):
    return pltpu.make_async_remote_copy(
        src_ref=source,
        dst_ref=target,
        send_sem=send,
        recv_sem=recv,
        device_id=device,
        device_id_type=MESH,
    )


class Gather:
    def __init__(self, at, views, send, recv):
        self.at, self.views, self.send, self.recv = at, views, send, recv

    def hop(self, u, slot, piece, device):
        return remote(piece, piece, self.send.at[u, slot], self.recv.at[u, slot], device)

    def line(self, u, step, piece_of, act):
        at = self.at
        z = at.z
        if act == "send":

            @pl.when((z < 3) & (z >= step - 1))
            def _():
                self.hop(u, step - 1, piece_of(z - (step - 1)), at.above).start()

            @pl.when((z > 0) & (z + step - 1 <= 3))
            def _():
                self.hop(u, step + 2, piece_of(z + (step - 1)), at.below).start()

        elif act == "recv":

            @pl.when(z >= step)
            def _():
                self.hop(u, step - 1, piece_of(z - step), at.below).wait_recv()

            @pl.when(z + step <= 3)
            def _():
                self.hop(u, step + 2, piece_of(z + step), at.above).wait_recv()

        else:

            @pl.when((z < 3) & (z >= step - 1))
            def _():
                self.hop(u, step - 1, piece_of(z - (step - 1)), at.above).wait_send()

            @pl.when((z > 0) & (z + step - 1 <= 3))
            def _():
                self.hop(u, step + 2, piece_of(z + (step - 1)), at.below).wait_send()

    def cross(self, u, axis, first, act):
        at, view = self.at, self.views(u)
        x, y, z = at.x, at.y, at.z
        route = GATHER_ROUTES[u]
        if route[0] == "z":
            if axis == route[1]:
                mine, its = view.at[:, y, x], (view.at[:, y, 1 - x] if axis == "x" else view.at[:, 1 - y, x])
            elif axis == "x":
                mine, its = view.at[:, :, x], view.at[:, :, 1 - x]
            else:
                mine, its = view.at[:, y], view.at[:, 1 - y]
        elif axis == route[0]:
            mine, its = view.at[z, y, x], (view.at[z, y, 1 - x] if axis == "x" else view.at[z, 1 - y, x])
        elif axis == "x":
            mine, its = view.at[z, :, x], view.at[z, :, 1 - x]
        else:
            mine, its = view.at[z, y], view.at[z, 1 - y]
        slot, device = (6, at.to_x) if axis == "x" else (7, at.to_y)
        if act == "recv":
            self.hop(u, slot, its, device).wait_recv()
        elif act == "send":
            self.hop(u, slot, mine, device).start()
        else:
            self.hop(u, slot, mine, device).wait_send()

    def stages(self, u):
        at, view, route = self.at, self.views(u), GATHER_ROUTES[u]
        if route[0] == "z":
            along = partial(self.line, u, piece_of=lambda k: view.at[k, at.y, at.x])
            lines = [partial(along, step) for step in (1, 2, 3)]
            return lines + [partial(self.cross, u, route[1], None), partial(self.cross, u, route[2], None)]
        along = partial(self.line, u, piece_of=lambda k: view.at[k])
        lines = [partial(along, step) for step in (1, 2, 3)]
        return [partial(self.cross, u, route[0], None), partial(self.cross, u, route[1], None)] + lines

    def round(self, u, k):
        stages = self.stages(u)
        if k > 0:
            stages[k - 1](act="recv")
        if k < 5:
            stages[k](act="send")

    def drain(self, u):
        for stage in self.stages(u):
            stage(act="sent")


def add_blocks(total, extra, count):
    @pl.loop(0, count)
    def _(i):
        left, right = total(i), extra(i)
        left[...] = (left[...].astype(jnp.float32) + right[...].astype(jnp.float32)).astype(left.dtype)


class Scatter:
    def __init__(self, at, views, spare, send, recv):
        self.at, self.views, self.spare, self.send, self.recv = at, views, spare, send, recv

    def hop(self, u, slot, source, target, device):
        return remote(source, target, self.send.at[u, slot], self.recv.at[u, slot], device)

    def line(self, u, step, act):
        at = self.at
        z = at.z
        wide = SCATTER_ROUTES[u][0] != "z"
        view, up, down = self.views(u), self.spare(u, "up"), self.spare(u, "down")

        def piece(k):
            return view.at[k] if wide else view.at[k, at.y, at.x]

        def send_up():
            return self.hop(u, step - 1, piece(z + 4 - step), up.at[step - 1], at.above)

        def send_down():
            return self.hop(u, step + 2, piece(z + step - 4), down.at[step - 1], at.below)

        if act == "send":
            pl.when((z < 3) & (z <= step - 1))(lambda: send_up().start())
            pl.when((z > 0) & (z >= 4 - step))(lambda: send_down().start())
        elif act == "sent":
            pl.when((z < 3) & (z <= step - 1))(lambda: send_up().wait_send())
            pl.when((z > 0) & (z >= 4 - step))(lambda: send_down().wait_send())
        else:
            shape = (2, 2) if wide else (1,)

            def take(k, slots):
                if wide:
                    for i in (0, 1):
                        add_blocks(lambda j: view.at[k, i, j], lambda j: slots.at[step - 1, i, j], 2)
                else:
                    add_blocks(lambda j: view.at[k, at.y, at.x], lambda j: slots.at[step - 1], 1)

            @pl.when((z >= 1) & (z <= step))
            def _():
                self.hop(u, step - 1, piece(z), up.at[step - 1], at.below).wait_recv()
                take(z + 3 - step, up)

            @pl.when((z < 3) & (z >= 3 - step))
            def _():
                self.hop(u, step + 2, piece(z), down.at[step - 1], at.above).wait_recv()
                take(z + step - 3, down)

    def cross(self, u, axis, act):
        at, view, spare = self.at, self.views(u), self.spare(u, axis)
        x, y, z = at.x, at.y, at.z
        route = SCATTER_ROUTES[u]
        slot, device = (6, at.to_x) if axis == "x" else (7, at.to_y)
        if route[0] == "z":
            if axis == route[2]:
                its = view.at[:, :, 1 - x] if axis == "x" else view.at[:, 1 - y]

                def add():
                    for j in (0, 1):
                        if axis == "x":
                            add_blocks(lambda i: view.at[i, j, x], lambda i: spare.at[i, j], 4)
                        else:
                            add_blocks(lambda i: view.at[i, y, j], lambda i: spare.at[i, j], 4)
            else:
                its = view.at[:, y, 1 - x] if axis == "x" else view.at[:, 1 - y, x]

                def add():
                    add_blocks(lambda i: view.at[i, y, x], lambda i: spare.at[i], 4)
        elif axis == route[1]:
            its = view.at[z, :, 1 - x] if axis == "x" else view.at[z, 1 - y]

            def add():
                if axis == "x":
                    add_blocks(lambda i: view.at[z, i, x], lambda i: spare.at[i], 2)
                else:
                    add_blocks(lambda i: view.at[z, y, i], lambda i: spare.at[i], 2)
        else:
            its = view.at[z, y, 1 - x] if axis == "x" else view.at[z, 1 - y, x]

            def add():
                add_blocks(lambda i: view.at[z, y, x], lambda i: spare, 1)

        hop = self.hop(u, slot, its, spare, device)
        if act == "send":
            hop.start()
        elif act == "sent":
            hop.wait_send()
        else:
            hop.wait_recv()
            add()

    def stages(self, u):
        route = SCATTER_ROUTES[u]
        lines = [partial(self.line, u, step) for step in (1, 2, 3)]
        if route[0] == "z":
            return [partial(self.cross, u, route[2]), partial(self.cross, u, route[1])] + lines
        return lines + [partial(self.cross, u, route[1]), partial(self.cross, u, route[0])]

    def round(self, u, k, end):
        stages = self.stages(u)
        if k > 0:
            stages[k - 1](act="recv")
        if k < 5:
            stages[k](act="send")
        else:
            end(u)

    def drain(self, u):
        for stage in self.stages(u):
            stage(act="sent")


def spare_shapes(rows, width, small):
    narrow = [u for u in range(UNITS) if SCATTER_ROUTES[u][0] == "z"]
    wide = [u for u in range(UNITS) if SCATTER_ROUTES[u][0] != "z"]

    def of(count, tail, kind):
        return [
            pltpu.VMEM((count, 4, 2) + tail, kind),
            pltpu.VMEM((count, 4) + tail, kind),
            pltpu.VMEM((count, 3) + tail, kind),
            pltpu.VMEM((count, 3) + tail, kind),
        ]

    shapes = of(len(narrow), (rows, width), jnp.bfloat16)
    tail = (rows, width)
    shapes += [
        pltpu.VMEM((len(wide), 2) + tail, jnp.bfloat16),
        pltpu.VMEM((len(wide),) + tail, jnp.bfloat16),
        pltpu.VMEM((len(wide), 3, 2, 2) + tail, jnp.bfloat16),
        pltpu.VMEM((len(wide), 3, 2, 2) + tail, jnp.bfloat16),
    ]
    shapes += of(1, (rows, small), jnp.float32)

    def pick(refs):
        def spare(u, what):
            route = SCATTER_ROUTES[u]
            if u == SMALL:
                base, index = 8, 0
            elif route[0] == "z":
                base, index = 0, narrow.index(u)
            else:
                base, index = 4, wide.index(u)
            if what in "xy":
                first = route[2] if route[0] == "z" else route[1]
                slot = 0 if what == first else 1
            else:
                slot = 2 if what == "up" else 3
            return refs[base + slot].at[index]

        return spare

    return shapes, pick


class ForwardRefs(NamedTuple):
    blocks: Any
    small: Any
    tokens: Any
    images: Any
    causal: Any
    choice: Any
    full: Any
    table: Any
    residuals: Any
    mixed: Any
    attended: Any
    queries: Any
    pair: Any
    hidden: Any
    out_rows: Any
    layer_out: Any
    g: Any
    g_small: Any
    tab: Any
    res: Any
    normed: Any
    mix: Any
    att: Any
    qc: Any
    pr: Any
    hid: Any
    act: Any
    acc: Any
    give: Any
    take: Any
    img: Any
    tok: Any
    rowsw: Any
    send: Any
    recv: Any
    local: Any
    swap_send: Any
    swap_recv: Any
    quarter_send: Any
    quarter_recv: Any
    keep: Any
    share_send: Any
    share_recv: Any


class BackRefs(NamedTuple):
    full: Any
    table: Any
    residuals: Any
    mixed: Any
    attended: Any
    queries: Any
    pair: Any
    hidden: Any
    out_rows: Any
    cotangent: Any
    images: Any
    causal: Any
    choice: Any
    sums_out: Any
    small_out: Any
    token_out: Any
    image_out: Any
    g: Any
    tab: Any
    dx: Any
    branch: Any
    res: Any
    scale: Any
    normed: Any
    hid: Any
    dhid: Any
    act: Any
    mix: Any
    att: Any
    datt: Any
    qc: Any
    pr: Any
    rowsw: Any
    img: Any
    give: Any
    take: Any
    pic_give: Any
    pic_take: Any
    og: Any
    sums: Any
    small: Any
    send: Any
    recv: Any
    swap_send: Any
    swap_recv: Any
    quarter_send: Any
    quarter_recv: Any
    quarter_local: Any
    load: Any
    store: Any
    share_send: Any
    share_recv: Any


def lowest(value):
    return value.astype(jnp.bfloat16)


def mm(left, right):
    return jnp.dot(left, right, preferred_element_type=jnp.float32)


def mm_back(left, right):
    return lax.dot_general(left, right, (((1,), (1,)), ((), ())), preferred_element_type=jnp.float32)


def mm_rows(left, right):
    return lax.dot_general(left, right, (((0,), (0,)), ((), ())), preferred_element_type=jnp.float32)


def first_lanes(value):
    return lax.broadcasted_iota(jnp.int32, value.shape, 1) < HEAD


def two_heads(value):
    lanes = first_lanes(value)
    zero = jnp.zeros_like(value)
    return jnp.concatenate([jnp.where(lanes, value, zero), jnp.where(lanes, zero, value)], axis=0)


def beside(value):
    half = value.shape[0] // 2
    return jnp.concatenate([value[:half], value[half:]], axis=1)


def below(value):
    half = value.shape[1] // 2
    return jnp.concatenate([value[:, :half], value[:, half:]], axis=0)


def softmax_of(scores, axis):
    shares = jnp.exp(scores - jnp.max(scores, axis=axis, keepdims=True))
    return shares * (1.0 / jnp.sum(shares, axis=axis, keepdims=True))


SPAN = 128
SCALING = HEAD ** (-0.5)
ROWS_AT_ONCE = 256


def whole(ref):
    value = ref[...]
    return value.reshape(-1, value.shape[-1])


def picture_bias(choice, shown):
    parts = []
    for image in (0.0, 1.0):
        offset = jnp.where(choice == image, 0.0, masked_score)
        parts.append(jnp.broadcast_to(offset, (shown, choice.shape[1])))
    return jnp.concatenate(parts, axis=0)


def norm_parts(value):
    center = value - jnp.mean(value, axis=1, keepdims=True)
    variance = jnp.mean(center * center, axis=1, keepdims=True)
    scale = lax.rsqrt(variance + 1e-05)
    return center * scale, scale


GELU_A = math.sqrt(2 / math.pi)
GELU_B = 0.044715


def gelu(value):
    return 0.5 * value * (1.0 + jnp.tanh(GELU_A * (value + GELU_B * (value * value * value))))


GATHER_ORDER = (
    84, 18, 0, 12, 85, 42, 19, 6, 1, 30, 86, 24, 13, 20, 36, 43, 7, 2, 87, 66, 31, 21, 48, 25, 3, 54, 37, 8, 78, 32, 60,
    67, 49, 26, 9, 72, 88, 55, 38, 33, 22, 27, 79, 4, 61, 50, 39, 73, 56, 14, 51, 44, 10, 62, 57, 89, -1, 34, 15, 74,
    23, 28, 45, 63, 5, 40, 75, 16, 68, 52, 46, 11, -1, -1, -1, -1, -1, -1, 58, -1, -1, -1, -1, -1, -1, -1, 17, -1, -1,
    -1, -1, -1, -1, 35, 69, 47, 29, -1, -1, -1, -1, 80, -1, -1, 64, 41, -1, -1, -1, -1, -1, -1, 76, -1, -1, -1, -1, -1,
    -1, -1, 81, 70, 53, 59, -1, -1, -1, -1, -1, -1, -1, -1, -1, -1, -1, -1, -1, -1, -1, -1, -1, -1, -1, 71, 82, 65, -1,
    -1, -1, -1, -1, 77, -1, -1, 83, -1, -1,
)
SCATTER_ORDER = (
    -1, -1, -1, -1, -1, -1, 72, -1, -1, -1, -1, 78, -1, -1, -1, -1, -1, -1, -1, 66, -1, -1, -1, -1, -1, -1, -1, -1, 60,
    -1, 67, -1, 73, -1, -1, -1, -1, -1, -1, 79, -1, 68, -1, -1, 54, -1, -1, -1, -1, -1, -1, 48, -1, -1, -1, -1, -1, -1,
    -1, 61, -1, 49, -1, -1, -1, -1, 36, -1, -1, -1, -1, -1, 50, -1, 42, 55, -1, -1, -1, -1, -1, -1, -1, -1, -1, 74, -1,
    24, -1, -1, 30, -1, 80, -1, -1, -1, -1, 12, -1, 25, -1, -1, 37, -1, -1, -1, -1, 43, -1, -1, 26, 62, -1, -1, 75, -1,
    -1, -1, -1, 31, -1, 81, -1, -1, -1, -1, 56, -1, 6, -1, -1, 13, 84, 76, 63, 82, 38, 44, 57, 7, 64, 32, 58, 14, 39,
    45, 0, 18, 33, 40, 8, 46, 15, 34, 1, 16, 19, 77, 85, 9, 83, 69, 10, 65, 2, 51, 59, 20, 86, 70, 41, 3, 47, 27, 21,
    35, 87, 52, 4, 17, 22, 11, 28, 71, 88, 53, 5, 23, 89, 29,
)


def play(order, steps, move):
    moved, left = set(), list(steps)
    for code in order:
        if code < 0:
            work, needs = left.pop(0)
            assert needs <= moved
            work()
        else:
            u, k = divmod(code, ROUNDS)
            move(u, k)
            if k == ROUNDS - 1:
                moved.add(u)
    assert not left


def forward_kernel(*refs):
    r = ForwardRefs(*refs)
    at = Place()
    h = at.h
    at.barrier(sibling=True)
    tokens = r.tok.shape[0]
    width = r.tok.shape[1]
    half = width // 2
    spans = [pl.ds(i, ROWS_AT_ONCE) for i in range(0, tokens, ROWS_AT_ONCE)]
    mine = pl.ds(pl.multiple_of(h * ROWS_AT_ONCE, ROWS_AT_ONCE), ROWS_AT_ONCE)
    others = pl.ds(pl.multiple_of((1 - h) * ROWS_AT_ONCE, ROWS_AT_ONCE), ROWS_AT_ONCE)
    gather = Gather(at, lambda u: r.g_small if u == SMALL else r.g.at[u], r.send, r.recv)

    copies = [
        pltpu.make_async_copy(r.small, r.g_small.at[at.z, at.y, at.x], r.local.at[0]),
        pltpu.make_async_copy(r.blocks, r.g.at[:, at.z, at.y, at.x], r.local.at[1]),
        pltpu.make_async_copy(r.tokens, r.tok.at[mine], r.local.at[2]),
        pltpu.make_async_copy(r.images, r.img.at[mine], r.local.at[3]),
    ]
    for copy in copies:
        copy.start()

    def share(rows):
        return [
            remote(source, target.at[rows], r.share_send.at[i], r.share_recv.at[i], at.sibling)
            for i, (source, target) in enumerate(((r.tokens, r.tok), (r.images, r.img)))
        ]

    for copy in share(mine):
        copy.start()

    keeps = []

    def keep(source, target):
        copy = pltpu.make_async_copy(source, target, r.keep.at[len(keeps)])
        keeps.append(copy)
        copy.start()

    def vector(n):
        return r.tab[pl.ds(n, 1), :]

    def own_vector(n):
        return r.tab[pl.ds(n, 1), pl.ds(pl.multiple_of(h * half, 128), half)]

    def start():
        for copy in copies[2:]:
            copy.wait()
        for copy in share(mine):
            copy.wait_send()
        for copy in share(others):
            copy.wait_recv()
        r.res[0] = r.tok[...].astype(jnp.float32)
        r.tab[...] = whole(r.g_small).astype(jnp.float32).T
        keep(r.tab, r.table)

    def norm(n):
        @pl.loop(0, tokens // 64, unroll=True)
        def _(i):
            rows = pl.ds(pl.multiple_of(i * 64, 64), 64)
            value, scale = norm_parts(r.res[n, rows, :])
            r.normed[rows, :] = lowest(value * vector(n) + vector(5 + n))

        keep(r.res.at[n], r.residuals.at[n])

    def quarter(l, u):
        away = (1 - h) * 2
        mine = pltpu.make_async_copy(
            r.g.at[u, pl.ds(h * 2, 2), :, :, :, pl.ds(half, half)],
            r.rowsw.at[l, :, :, :, :, pl.ds(pl.multiple_of(h * half, 128), half)],
            r.local.at[4 + l],
        )
        theirs = remote(
            r.g.at[u, pl.ds(away, 2), :, :, :, pl.ds(half, half)],
            r.rowsw.at[l, :, :, :, :, pl.ds(pl.multiple_of(h * half, 128), half)],
            r.quarter_send.at[l],
            r.quarter_recv.at[l],
            at.sibling,
        )
        return mine, theirs

    def start_quarter(l, u):
        mine, theirs = quarter(l, u)
        mine.start()
        theirs.start()

    def end_quarter(l, u):
        mine, theirs = quarter(l, u)
        mine.wait()
        theirs.wait()
        keep(r.rowsw.at[l], r.out_rows.at[l])

    def swap(e, i):
        rows = spans[i]
        return remote(
            r.give.at[e % 2, rows], r.take.at[e % 2, rows], r.swap_send.at[e, i], r.swap_recv.at[e, i], at.sibling
        )

    def offer(e, i, value):
        r.give[e % 2, spans[i], :] = lowest(value)
        swap(e, i).start()

    def join(e, i, n, bias):
        swap(e, i).wait()
        rows = spans[i]
        both = r.give[e % 2, rows, :].astype(jnp.float32) + r.take[e % 2, rows, :].astype(jnp.float32)
        r.res[n + 1, rows, :] = r.res[n, rows, :] + both + vector(5 + bias)

    def mix(l, u, query_bias, value_bias, i):
        rows = spans[i]
        value = r.normed[rows, :]
        both = mm(value, whole(r.g.at[u]))
        r.mix[l, rows, :half] = lowest(both[:, :half] + own_vector(5 + query_bias))
        r.mix[l, rows, half:width] = lowest(both[:, half:])
        r.mix[l, rows, width:] = lowest(
            mm(value, whole(r.g.at[u + 1, :, :, :, :, :half])) + own_vector(5 + value_bias)
        )

    def attend(l, blocks):
        @pl.loop(*blocks, unroll=True)
        def _(i):
            rows = pl.ds(pl.multiple_of(i * SPAN, SPAN), SPAN)
            bias = r.causal[i]
            bias = jnp.concatenate([bias, bias], axis=0)
            for j in range(half // 128):
                lanes = [pl.ds(part * half + j * 128, 128) for part in range(3)]
                queries, keys, values = [r.mix[l, rows, lane] for lane in lanes]
                scores = mm_back(two_heads(queries * SCALING), keys) + bias
                shares = lowest(softmax_of(scores, 1))
                r.att[l, rows, pl.ds(j * 128, 128)] = lowest(mm(beside(shares), two_heads(values)))

    def project_out(l, e, a, i):
        value = r.att[a, spans[i], :]
        offer(e, i, mm(value, whole(r.rowsw.at[a])))

    def up(l, u, s, i):
        rows = spans[i]
        value = mm(r.normed[rows, :], whole(r.g.at[u])) + vector(21 + 2 * l + s)
        r.hid[l, rows, pl.ds(s * width, width)] = value
        r.act[rows, pl.ds(s * width, width)] = lowest(gelu(value))

    def down(u, s, i, e):
        rows = spans[i]
        value = mm(r.act[rows, pl.ds(s * width, width)], whole(r.g.at[u]))
        if s == 0:
            r.acc[rows, :] = value
        else:
            offer(e, i, r.acc[rows, :] + value)

    def picture_pair(i):
        rows = spans[i]
        value = mm(r.img[rows, :], whole(r.g.at[9]))
        r.pr[rows, :half] = lowest(value[:, :half])
        r.pr[rows, half:] = lowest(value[:, half:] + own_vector(5 + 14))

    def cross_queries(i):
        rows = spans[i]
        r.qc[rows, :] = lowest(mm(r.normed[rows, :], whole(r.g.at[8, :, :, :, :, :half])) + own_vector(5 + 13))

    def cross(blocks):
        @pl.loop(*blocks, unroll=True)
        def _(i):
            rows = pl.ds(pl.multiple_of(i * SPAN, SPAN), SPAN)
            bias = picture_bias(r.choice[pl.ds(i, 1), :], r.pr.shape[0] // 2).T
            bias = jnp.concatenate([bias, bias], axis=0)
            for j in range(half // 128):
                keys = r.pr[:, pl.ds(j * 128, 128)]
                values = r.pr[:, pl.ds(half + j * 128, 128)]
                scores = mm_back(two_heads(r.qc[rows, pl.ds(j * 128, 128)] * SCALING), keys) + bias
                shares = lowest(softmax_of(scores, 1))
                r.att[2, rows, pl.ds(j * 128, 128)] = lowest(mm(beside(shares), two_heads(values)))

    segments = []

    def add(needs, work, *args):
        segments.append((partial(work, *args), frozenset(needs)))

    def add_attention(l, n, u, e, biases, rest):
        add({SMALL, u, u + 1}, start_quarter, l, u + 1)
        add(rest, norm, n)
        for i in (0, 1):
            add(rest, mix, l, u, biases[0], biases[1], i)
        for i in (0, 1):
            add(rest, attend, l, (2 * i, 2 * i + 2))
        add(rest, end_quarter, l, u + 1)
        add(rest, keep, r.mix.at[l], r.mixed.at[l])
        for i in (0, 1):
            add(rest, project_out, l, e, l, i)
        add(rest, keep, r.att.at[l], r.attended.at[l])
        for i in (0, 1):
            add(rest, join, e, i, n, biases[2])

    def add_feed(l, n, u, e, bias):
        add((), norm, n)
        for s in (0, 1):
            for i in (0, 1):
                add({u + s}, up, l, u + s, s, i)
        add((), keep, r.hid.at[l], r.hidden.at[l])
        for s in (0, 1):
            for i in (0, 1):
                add({u + 2 + s}, down, u + 2 + s, s, i, e)
        if e < 4:
            for i in (0, 1):
                add((), join, e, i, n, bias)

    add({SMALL}, start)
    add_attention(0, 0, 0, 0, (5, 6, 7), ())
    add_feed(0, 1, 2, 1, 8)
    add_attention(1, 2, 6, 2, (9, 10, 11), ())
    add({9}, picture_pair, 0)
    add((), picture_pair, 1)
    add((), keep, r.pr, r.pair)
    add({8}, start_quarter, 2, 8)
    add((), norm, 3)
    for i in (0, 1):
        add((), cross_queries, i)
    add((), keep, r.qc, r.queries)
    for i in range(4):
        add((), cross, (i, i + 1))
    add((), end_quarter, 2, 8)
    for i in (0, 1):
        add((), project_out, 2, 3, 2, i)
    add((), keep, r.att.at[2], r.attended.at[2])
    for i in (0, 1):
        add((), join, 3, i, 3, 15)
    add_feed(1, 4, 10, 4, 12)

    for copy in copies[:2]:
        copy.wait()

    def move(u, k):
        gather.round(u, k)
        if k == ROUNDS - 1 and u != SMALL:
            keep(r.g.at[u], r.full.at[u])

    play(GATHER_ORDER, segments, move)
    for i in (0, 1):
        swap(4, i).wait()
    both = r.give[0, mine, :].astype(jnp.float32) + r.take[0, mine, :].astype(jnp.float32)
    r.layer_out[...] = r.res[4, mine, :] + both + vector(5 + 12)
    for u in range(UNITS + 1):
        gather.drain(u)
    for copy in keeps:
        copy.wait()


def forward(blocks, small, tokens, images, causal, choice):
    units, rows, width = blocks.shape
    count = 2 * tokens.shape[0]
    half = width // 2
    bf, fl = jnp.bfloat16, jnp.float32
    shape = jax.ShapeDtypeStruct
    dma = pltpu.SemaphoreType.DMA
    outs = (
        shape((units, 4, 2, 2, rows, width), bf),
        shape((128, width), fl),
        shape((5, count, width), fl),
        shape((2, count, width + half), bf),
        shape((3, count, half), bf),
        shape((count, half), bf),
        shape((count, width), bf),
        shape((2, count, 2 * width), fl),
        shape((3, 2, 2, 2, rows, width), bf),
        shape((count // 2, width), fl),
    )
    anywhere, here = pl.BlockSpec(memory_space=pl.ANY), pl.BlockSpec(memory_space=pltpu.VMEM)
    return pl.pallas_call(
        forward_kernel,
        out_shape=outs,
        in_specs=[anywhere] * 4 + [here] * 2,
        out_specs=[anywhere] * 9 + [here],
        scratch_shapes=[
            pltpu.VMEM((units, 4, 2, 2, rows, width), bf),
            pltpu.VMEM((4, 2, 2) + small.shape, bf),
            pltpu.VMEM((128, width), fl),
            pltpu.VMEM((5, count, width), fl),
            pltpu.VMEM((count, width), bf),
            pltpu.VMEM((2, count, width + half), bf),
            pltpu.VMEM((3, count, half), bf),
            pltpu.VMEM((count, half), bf),
            pltpu.VMEM((count, width), bf),
            pltpu.VMEM((2, count, 2 * width), fl),
            pltpu.VMEM((count, 2 * width), bf),
            pltpu.VMEM((count, width), fl),
            pltpu.VMEM((2, count, width), bf),
            pltpu.VMEM((2, count, width), bf),
            pltpu.VMEM((count, width), bf),
            pltpu.VMEM((count, width), bf),
            pltpu.VMEM((3, 2, 2, 2, rows, width), bf),
            dma((units + 1, 8)),
            dma((units + 1, 8)),
            dma((8,)),
            dma((5, 2)),
            dma((5, 2)),
            dma((3,)),
            dma((3,)),
            dma((40,)),
            dma((2,)),
            dma((2,)),
        ],
        compiler_params=pltpu.CompilerParams(collective_id=0, has_side_effects=True, vmem_limit_bytes=60 << 20),
    )(blocks, small, tokens, images, causal, choice)


BACK_UNITS = (12, 13, 10, 11, 9, 8, 6, 7, 4, 5, 2, 3, 0, 1, SMALL)
OUT_UNITS = (8, 7, 1)


def gelu_parts(value):
    square = value * value
    bent = jnp.tanh(value * (GELU_A + (GELU_A * GELU_B) * square))
    rise = 0.5 + 0.5 * bent
    slope = rise + (0.5 * value) * (1.0 - bent * bent) * (GELU_A + (3.0 * GELU_A * GELU_B) * square)
    return value * rise, slope


def backward_kernel(*refs, pick, spares):
    named = len(BackRefs._fields)
    r = BackRefs(*refs[:named])
    spare = pick(refs[named:])
    at = Place()
    h = at.h
    at.barrier(sibling=True)
    tokens, width = r.branch.shape
    half = width // 2
    spans = [pl.ds(i, ROWS_AT_ONCE) for i in range(0, tokens, ROWS_AT_ONCE)]
    mine = pl.ds(pl.multiple_of(h * ROWS_AT_ONCE, ROWS_AT_ONCE), ROWS_AT_ONCE)
    others = pl.ds(pl.multiple_of((1 - h) * ROWS_AT_ONCE, ROWS_AT_ONCE), ROWS_AT_ONCE)
    own_lanes = pl.ds(pl.multiple_of(h * half, 128), half)
    other_lanes = pl.ds(pl.multiple_of((1 - h) * half, 128), half)
    scatter = Scatter(at, lambda u: r.small if u == SMALL else r.g.at[u], spare, r.send, r.recv)

    loads = {}

    def fetch(name, source, target):
        copy = pltpu.make_async_copy(source, target, r.load.at[len(loads)])
        loads[name] = copy
        copy.start()

    def need(name):
        copy = loads[name]
        if copy is not None:
            copy.wait()
            loads[name] = None
            if name in shared:
                share(name, mine).wait_send()
                share(name, others).wait_recv()

    shared = {"cotangent": (0, r.cotangent, r.branch), "images": (1, r.images, r.img)}

    def share(name, rows):
        i, source, target = shared[name]
        return remote(source, target.at[rows], r.share_send.at[i], r.share_recv.at[i], at.sibling)

    def fetch_shared(name):
        i, source, target = shared[name]
        fetch(name, source, target.at[mine])
        share(name, mine).start()

    def fetch_unit(u):
        if u in OUT_UNITS:
            fetch(("g", u), r.full.at[u, :, :, :, :, pl.ds(0, half)], r.g.at[u, :, :, :, :, pl.ds(0, half)])
        else:
            fetch(("g", u), r.full.at[u], r.g.at[u])

    def fetch_residual(n, slot):
        fetch(("res", n), r.residuals.at[n], r.res.at[slot])

    def fetch_hidden(l):
        for s in (0, 1):
            fetch(("hid", l, s), r.hidden.at[l, :, pl.ds(s * width, width)], r.hid.at[s])

    def fetch_mixed(l):
        fetch(("mix", l), r.mixed.at[l], r.mix)

    fetch("table", r.table, r.tab)
    fetch_shared("cotangent")
    fetch_unit(12)
    fetch_hidden(1)
    fetch_unit(13)
    fetch_residual(4, 0)
    fetch_unit(10)
    fetch_unit(11)
    fetch("rows", r.out_rows, r.rowsw)
    fetch("queries", r.queries, r.qc)
    fetch("pair", r.pair, r.pr)
    fetch_residual(3, 1)
    fetch("attended", r.attended, r.att)
    fetch_shared("images")
    for u in (9, 8):
        fetch_unit(u)
    fetch_mixed(1)
    for u in (6, 7, 4, 5, 2, 3, 0, 1):
        fetch_unit(u)

    def vector(n):
        return r.tab[pl.ds(n, 1), :]

    def add_row(n, value):
        r.sums[pl.ds(n, 1), :] += jnp.sum(value, axis=0, keepdims=True)

    def add_own(n, value):
        r.sums[pl.ds(n, 1), own_lanes] += jnp.sum(value, axis=0, keepdims=True)

    def start():
        need("cotangent")
        r.sums[...] = jnp.zeros_like(r.sums)
        r.dx[...] = r.branch[...].astype(jnp.float32)

    def norm(n, slot):
        need(("res", n))
        need("table")

        @pl.loop(0, tokens // 64, unroll=True)
        def _(i):
            rows = pl.ds(pl.multiple_of(i * 64, 64), 64)
            value, scale = norm_parts(r.res[slot, rows, :])
            r.res[slot, rows, :] = value
            r.scale[rows, :] = scale
            r.normed[rows, :] = lowest(value * vector(n) + vector(5 + n))

    def begin_branch(bias):
        @pl.loop(0, tokens // 64, init_carry=jnp.zeros((1, width), jnp.float32), unroll=True)
        def total(i, carry):
            rows = pl.ds(pl.multiple_of(i * 64, 64), 64)
            value = lowest(r.dx[rows, :])
            r.branch[rows, :] = value
            return carry + jnp.sum(value.astype(jnp.float32), axis=0, keepdims=True)

        r.sums[pl.ds(5 + bias, 1), :] = total

    def swap(e, i):
        rows = spans[i]
        return remote(
            r.give.at[e % 2, rows], r.take.at[e % 2, rows], r.swap_send.at[e, i], r.swap_recv.at[e, i], at.sibling
        )

    def offer(e, i, value):
        r.give[e % 2, spans[i], :] = lowest(value)
        swap(e, i).start()

    def join(e, i, n, slot):
        swap(e, i).wait()
        base = i * ROWS_AT_ONCE
        gain = vector(n)
        zero = jnp.zeros((1, width), jnp.float32)

        @pl.loop(0, ROWS_AT_ONCE // 64, init_carry=(zero, zero), unroll=True)
        def totals(k, carry):
            rows = pl.ds(pl.multiple_of(base + k * 64, 64), 64)
            given = r.give[e % 2, rows, :].astype(jnp.float32) + r.take[e % 2, rows, :].astype(jnp.float32)
            value = r.res[slot, rows, :]
            product = given * value
            scaled = given * gain
            first = jnp.mean(scaled, axis=1, keepdims=True)
            second = jnp.mean(product * gain, axis=1, keepdims=True)
            r.dx[rows, :] += r.scale[rows, :] * (scaled - first - value * second)
            return (
                carry[0] + jnp.sum(product, axis=0, keepdims=True),
                carry[1] + jnp.sum(given, axis=0, keepdims=True),
            )

        r.sums[pl.ds(n, 1), :] += totals[0]
        r.sums[pl.ds(5 + n, 1), :] += totals[1]

    def store_rows(u, part, value, lanes=slice(None)):
        value = lowest(value)
        r.g[u, 2 * part : 2 * part + 2, :, :, :, lanes] = value.reshape((2, 2, 2, -1) + value.shape[1:])

    def feed_hidden(l, u, s, i):
        need(("g", u))
        need(("hid", l, s))
        rows, lanes = spans[i], pl.ds(s * width, width)
        back = mm_back(r.branch[rows, :], whole(r.g.at[u]))
        active, slope = gelu_parts(r.hid[s, rows, :])
        value = lowest(back * slope)
        r.act[rows, lanes] = lowest(active)
        r.dhid[rows, lanes] = value
        add_row(21 + 2 * l + s, value.astype(jnp.float32))

    def feed_down(u, s, part):
        lanes = pl.ds(s * width + part * half, half)
        store_rows(u, part, mm_rows(r.act[:, lanes], r.branch[...]))

    def feed_normed(u, i, e):
        need(("g", u))
        need(("g", u + 1))
        rows = spans[i]
        value = mm_back(r.dhid[rows, :width], whole(r.g.at[u]))
        offer(e, i, value + mm_back(r.dhid[rows, width:], whole(r.g.at[u + 1])))

    def feed_up(u, s, part):
        lanes = pl.ds(s * width, width)
        store_rows(u, part, mm_rows(r.normed[:, pl.ds(part * half, half)], r.dhid[:, lanes]))

    def attended_back(a, i):
        need("rows")
        r.datt[spans[i], :] = lowest(mm_back(r.branch[spans[i], :], whole(r.rowsw.at[a])))

    def near_copy(a, u):
        return pltpu.make_async_copy(
            r.og.at[:, :, :, :, own_lanes],
            r.g.at[u, pl.ds(2 * h, 2), :, :, :, pl.ds(half, half)],
            r.quarter_local.at[a],
        )

    def far_copy(a, u, rows_of):
        return remote(
            r.og.at[:, :, :, :, other_lanes],
            r.g.at[u, pl.ds(2 * rows_of, 2), :, :, :, pl.ds(half, half)],
            r.quarter_send.at[a],
            r.quarter_recv.at[a],
            at.sibling,
        )

    def out_gradient(a, u):
        need("attended")
        value = lowest(mm_rows(r.att[a], r.branch[...]))
        r.og[...] = value.reshape(r.og.shape)
        near_copy(a, u).start()
        far_copy(a, u, h).start()

    def end_quarter(a, u):
        near_copy(a, u).wait()
        far_copy(a, u, h).wait_send()
        far_copy(a, u, 1 - h).wait_recv()


    def attend_back(l, blocks):
        need(("mix", l))

        @pl.loop(*blocks, unroll=True)
        def _(b):
            rows = pl.ds(pl.multiple_of(b * SPAN, SPAN), SPAN)
            bias = r.causal[b].T
            bias = jnp.concatenate([bias, bias], axis=1)
            for j in range(half // 128):
                lanes = [pl.ds(part * half + j * 128, 128) for part in range(3)]
                queries, keys, values = [r.mix[rows, lane] for lane in lanes]
                queries = two_heads(queries * SCALING)
                given = two_heads(r.datt[rows, pl.ds(j * 128, 128)])
                shares = softmax_of(mm_back(keys, queries) + bias, 0)
                share_adjoint = mm_back(values, given)
                score_adjoint = lowest(shares * (share_adjoint - jnp.sum(shares * share_adjoint, axis=0, keepdims=True)))
                r.dhid[rows, lanes[0]] = lowest(mm_rows(below(score_adjoint), two_heads(keys * SCALING)))
                r.dhid[rows, lanes[1]] = lowest(mm(score_adjoint, queries))
                r.dhid[rows, lanes[2]] = lowest(mm(lowest(shares), given))

    def mixed_normed(u, e, i, biases):
        need(("g", u))
        need(("g", u + 1))
        rows = spans[i]
        value = mm_back(r.dhid[rows, :width], whole(r.g.at[u]))
        value += mm_back(r.dhid[rows, pl.ds(width, half)], whole(r.g.at[u + 1, :, :, :, :, pl.ds(0, half)]))
        offer(e, i, value)

    def mixed_sums(biases):
        add_own(5 + biases[0], r.dhid[:, :half].astype(jnp.float32))
        add_own(5 + biases[1], r.dhid[:, pl.ds(width, half)].astype(jnp.float32))

    def mixed_gradient(u, part):
        store_rows(u, part, mm_rows(r.normed[:, pl.ds(part * half, half)], r.dhid[:, :width]))

    def value_gradient(u, part):
        value = mm_rows(r.normed[:, pl.ds(part * half, half)], r.dhid[:, pl.ds(width, half)])
        store_rows(u, part, value, pl.ds(0, half))

    def cross_back(b):
        need("queries")
        need("pair")
        rows = pl.ds(b * SPAN, SPAN)
        bias = picture_bias(r.choice[pl.ds(b, 1), :], r.pr.shape[0] // 2)
        bias = jnp.concatenate([bias, bias], axis=1)
        for j in range(half // 128):
            lanes = pl.ds(j * 128, 128)
            value_lanes = pl.ds(half + j * 128, 128)
            keys, values = r.pr[:, lanes], r.pr[:, value_lanes]
            queries = two_heads(r.qc[rows, lanes] * SCALING)
            given = two_heads(r.datt[rows, lanes])
            shares = softmax_of(mm_back(keys, queries) + bias, 0)
            share_adjoint = mm_back(values, given)
            score_adjoint = lowest(shares * (share_adjoint - jnp.sum(shares * share_adjoint, axis=0, keepdims=True)))
            r.act[rows, lanes] = lowest(mm_rows(below(score_adjoint), two_heads(keys * SCALING)))
            key_adjoint = mm(score_adjoint, queries)
            value_adjoint = mm(lowest(shares), given)
            if b == 0:
                r.hid[0, :, lanes] = key_adjoint
                r.hid[0, :, value_lanes] = value_adjoint
            else:
                r.hid[0, :, lanes] += key_adjoint
                r.hid[0, :, value_lanes] += value_adjoint

    def pair_adjoint():
        r.dhid[:, :width] = lowest(r.hid[0])
        add_own(5 + 13, r.act[:, :half].astype(jnp.float32))
        add_own(5 + 14, r.dhid[:, pl.ds(half, half)].astype(jnp.float32))

    def query_normed(e, i):
        need(("g", 8))
        offer(e, i, mm_back(r.act[spans[i], pl.ds(0, half)], whole(r.g.at[8, :, :, :, :, pl.ds(0, half)])))

    def query_gradient(part):
        value = mm_rows(r.normed[:, pl.ds(part * half, half)], r.act[:, pl.ds(0, half)])
        store_rows(8, part, value, pl.ds(0, half))

    def pic_swap():
        return remote(r.pic_give, r.pic_take, r.swap_send.at[5, 0], r.swap_recv.at[5, 0], at.sibling)

    def picture_back():
        need(("g", 9))
        r.pic_give[...] = lowest(mm_back(r.dhid[others, pl.ds(0, width)], whole(r.g.at[9])))
        pic_swap().start()

    def picture_own():
        r.hid[1, pl.ds(0, ROWS_AT_ONCE), :] = mm_back(r.dhid[mine, pl.ds(0, width)], whole(r.g.at[9]))

    def picture_copy():
        return pltpu.make_async_copy(r.hid.at[1, pl.ds(0, ROWS_AT_ONCE)], r.image_out, r.store.at[UNITS])

    def picture_join():
        pic_swap().wait()
        r.hid[1, pl.ds(0, ROWS_AT_ONCE), :] += r.pic_take[...].astype(jnp.float32)
        picture_copy().start()

    def pair_gradient(part):
        need("images")
        store_rows(9, part, mm_rows(r.img[:, pl.ds(part * half, half)], r.dhid[:, pl.ds(0, width)]))

    def picture_end():
        picture_copy().wait()
        fetch_hidden(0)

    def small_total():
        r.small[...] = r.sums[...].T.reshape(r.small.shape)

    def token_copy():
        return pltpu.make_async_copy(r.dx.at[mine], r.token_out, r.store.at[UNITS + 1])

    segments, ready = [], set()

    def add(work, *args, finished=()):
        def step():
            work(*args)
            ready.update(finished)

        segments.append((step, frozenset()))

    def add_feed(l, n, slot, u, e, bias, after):
        add(begin_branch, bias)
        for s in (0, 1):
            for i in (0, 1):
                add(feed_hidden, l, u + 2 + s, s, i)
            for part in (0, 1):
                add(feed_down, u + 2 + s, s, part, finished=(u + 2 + s,) if part else ())
        for i in (0, 1):
            add(feed_normed, u, i, e)
        add(norm, n, slot)
        for s in (0, 1):
            for part in (0, 1):
                add(feed_up, u + s, s, part, finished=(u + s,) if part else ())
        for i in (0, 1):
            add(join, e, i, n, slot)
        for work in after:
            add(*work)

    def add_attention(l, n, slot, u, e, biases, after):
        add(begin_branch, biases[2])
        for i in (0, 1):
            add(attended_back, l, i)
        add(out_gradient, l, u + 1)
        add(attend_back, l, (0, 2))
        add(attend_back, l, (2, 4))
        for i in (0, 1):
            add(mixed_normed, u, e, i, biases)
        add(norm, n, slot)
        for part in (0, 1):
            add(mixed_gradient, u, part, finished=(u,) if part else ())
        for part in (0, 1):
            add(value_gradient, u + 1, part)
        add(end_quarter, l, u + 1, finished=(u + 1,))
        add(mixed_sums, biases)
        for i in (0, 1):
            add(join, e, i, n, slot)
        for work in after:
            add(*work)

    add(start)
    add_feed(1, 4, 0, 10, 0, 12, [(fetch_residual, 2, 0)])
    add(begin_branch, 15)
    for i in (0, 1):
        add(attended_back, 2, i)
    add(out_gradient, 2, 8)
    for b in range(tokens // SPAN):
        add(cross_back, b)
    add(pair_adjoint)
    for i in (0, 1):
        add(query_normed, 1, i)
    add(picture_back)
    add(picture_own)
    for part in (0, 1):
        add(pair_gradient, part, finished=(9,) if part else ())
    add(norm, 3, 1)
    for part in (0, 1):
        add(query_gradient, part)
    add(end_quarter, 2, 8, finished=(8,))
    for i in (0, 1):
        add(join, 1, i, 3, 1)
    add(picture_join)
    add(fetch_residual, 1, 1)
    add_attention(1, 2, 0, 6, 2, (9, 10, 11), [(picture_end,), (fetch_residual, 0, 0), (fetch_mixed, 0)])
    add_feed(0, 1, 1, 2, 3, 8, [])
    add_attention(0, 0, 0, 0, 4, (5, 6, 7), [])
    add(small_total, finished=(SMALL,))
    add(lambda: token_copy().start())

    def end_unit(u):
        if u == SMALL:
            r.small_out[...] = r.small[at.z, at.y, at.x]
        else:
            pltpu.make_async_copy(r.g.at[u, at.z, at.y, at.x], r.sums_out.at[u], r.store.at[u]).start()

    def move(u, k):
        assert u in ready
        scatter.round(u, k, end_unit)

    play(SCATTER_ORDER, segments, move)
    for u in BACK_UNITS:
        scatter.drain(u)
        if u != SMALL:
            pltpu.make_async_copy(r.g.at[u, at.z, at.y, at.x], r.sums_out.at[u], r.store.at[u]).wait()
    token_copy().wait()


def backward(full, table, residuals, mixed, attended, queries, pair, hidden, out_rows, cotangent, images, causal, choice):
    units, rows, width = full.shape[0], full.shape[4], full.shape[5]
    count = 2 * cotangent.shape[0]
    half = width // 2
    bf, fl = jnp.bfloat16, jnp.float32
    shape = jax.ShapeDtypeStruct
    dma = pltpu.SemaphoreType.DMA
    shapes, pick = spare_shapes(rows, width, 128)
    anywhere, here = pl.BlockSpec(memory_space=pl.ANY), pl.BlockSpec(memory_space=pltpu.VMEM)
    return pl.pallas_call(
        partial(backward_kernel, pick=pick, spares=len(shapes)),
        out_shape=(
            shape((units, rows, width), bf),
            shape((rows, 128), fl),
            shape((count // 2, width), fl),
            shape((count // 2, width), fl),
        ),
        in_specs=[anywhere] * 11 + [here] * 2,
        out_specs=[anywhere, here, anywhere, anywhere],
        scratch_shapes=[
            pltpu.VMEM(full.shape, bf),
            pltpu.VMEM((128, width), fl),
            pltpu.VMEM((count, width), fl),
            pltpu.VMEM((count, width), bf),
            pltpu.VMEM((2, count, width), fl),
            pltpu.VMEM((count, 1), fl),
            pltpu.VMEM((count, width), bf),
            pltpu.VMEM((2, count, width), fl),
            pltpu.VMEM((count, 2 * width), bf),
            pltpu.VMEM((count, 2 * width), bf),
            pltpu.VMEM((count, width + half), bf),
            pltpu.VMEM((3, count, half), bf),
            pltpu.VMEM((count, half), bf),
            pltpu.VMEM((count, half), bf),
            pltpu.VMEM((count, width), bf),
            pltpu.VMEM(out_rows.shape, bf),
            pltpu.VMEM((count, width), bf),
            pltpu.VMEM((2, count, width), bf),
            pltpu.VMEM((2, count, width), bf),
            pltpu.VMEM((count // 2, width), bf),
            pltpu.VMEM((count // 2, width), bf),
            pltpu.VMEM(out_rows.shape[1:], bf),
            pltpu.VMEM((128, width), fl),
            pltpu.VMEM((4, 2, 2, rows, 128), fl),
            dma((units + 1, 8)),
            dma((units + 1, 8)),
            dma((6, 2)),
            dma((6, 2)),
            dma((3,)),
            dma((3,)),
            dma((3,)),
            dma((40,)),
            dma((units + 2,)),
            dma((2,)),
            dma((2,)),
            *shapes,
        ],
        compiler_params=pltpu.CompilerParams(collective_id=1, has_side_effects=True, vmem_limit_bytes=63 << 20),
    )(full, table, residuals, mixed, attended, queries, pair, hidden, out_rows, cotangent, images, causal, choice)


def swap_cores(value):
    return lax.ppermute(value, "heads", [(0, 1), (1, 0)])


def both_cores(value, member):
    other = swap_cores(value)
    return jnp.stack([jnp.where(member == 0, value, other), jnp.where(member == 0, other, value)])


def to_units(member, self_weight, self_out_weight, up_weight, query_weight, pair_weight, cross_out_weight):
    width = self_weight.shape[1 + 1] // 3
    half = width // 2
    rows = self_weight.shape[1]
    own = slice(member * half, member * half + half)
    value = slice(width + member * half, width + member * half + half)
    units = []
    for layer in (0, 1):
        weight = self_weight[layer]
        units.append(jnp.concatenate([weight[:, own], weight[:, value]], axis=1))
        units.append(jnp.concatenate([weight[:, 2 * width + member * half : 2 * width + member * half + half], self_out_weight[layer][:, own]], axis=1))
        up = up_weight[layer].reshape(rows, CHIPS, 2, 2, -1)[:, :, member]
        units.append(up[:, :, 0].reshape(rows, width))
        units.append(up[:, :, 1].reshape(rows, width))
    units.append(jnp.concatenate([query_weight[:, own], cross_out_weight[:, own]], axis=1))
    units.append(jnp.concatenate([pair_weight[:, own], pair_weight[:, value]], axis=1))
    return jnp.stack(units)


UNIT_OF_PIECE = (0, 1, 2, 3, 6, 7, 10, 11, 8, 9)


def chip_blocks(member, pieces, down_weight):
    theirs, ours = (
        jnp.where(member == 0, pieces[1], pieces[0]),
        jnp.where(member == 0, pieces[0], pieces[1]),
    )
    rows = jnp.concatenate(list(both_rows(member, ours, swap_cores(theirs))), axis=1)
    down = down_weight.reshape(2, 2, rows.shape[1], rows.shape[2])
    order = {u: rows[i] for i, u in enumerate(UNIT_OF_PIECE)}
    order.update({4: down[0, 0], 5: down[0, 1], 12: down[1, 0], 13: down[1, 1]})
    return jnp.stack([order[u] for u in range(UNITS)])


def both_rows(member, ours, other):
    return jnp.where(member == 0, ours, other), jnp.where(member == 0, other, ours)


def chip_program(
    tokens,
    images,
    segment_labels,
    image_index,
    cotangent,
    norm_gain,
    vector_bias,
    up_bias,
    self_weight,
    self_out_weight,
    up_weight,
    down_weight,
    query_weight,
    pair_weight,
    cross_out_weight,
):
    member = lax.axis_index("heads")
    rows, length, width = tokens.shape
    half = width // 2
    slim = self_weight.shape[1]
    matrices = (self_weight, self_out_weight, up_weight, query_weight, pair_weight, cross_out_weight)
    blocks = chip_blocks(member, [to_units(m, *matrices) for m in (0, 1)], down_weight)
    vectors = jnp.concatenate([norm_gain, vector_bias], axis=0)
    vectors = jnp.concatenate(list(both_cores(vectors, member)), axis=1)
    vectors = jnp.concatenate([vectors, up_bias.reshape(4, 2 * slim)], axis=0)
    small = jnp.pad(vectors, ((0, 128 - vectors.shape[0]), (0, 0))).T
    own_tokens, own_images, own_cotangent = (value.reshape(-1, width) for value in (tokens, images, cotangent))
    chip_rows = segment_labels.shape[0]
    labels = jnp.arange(image_index.shape[1])
    caption_image = jnp.sum(
        jnp.where(segment_labels[:, :, None] == labels[None, None, :], image_index[:, None, :], 0), axis=-1, dtype=jnp.int32
    )
    count = chip_rows * length
    span_rows = SPAN // length
    row_of = jnp.arange(SPAN) // length
    same = row_of[:, None] == row_of[None, :]
    span_labels = segment_labels.reshape(-1, SPAN)
    causal = (span_labels[:, :, None] == span_labels[:, None, :]) & (same & (jnp.arange(SPAN)[:, None] >= jnp.arange(SPAN)[None, :]))[None]
    causal = jnp.where(causal, 0.0, masked_score).astype(jnp.float32)
    choice = caption_image.reshape(count // SPAN, SPAN).astype(jnp.float32)
    full, table, residuals, mixed, attended, queries, pair, hidden, out_rows, layer_out = forward(
        blocks, small, own_tokens, own_images, causal, choice
    )
    sums, small_sums, token_gradient, image_gradient = backward(
        full, table, residuals, mixed, attended, queries, pair, hidden, out_rows, own_cotangent, own_images, causal, choice
    )
    outs = finish(member, sums.astype(jnp.float32), small_sums, slim, width)
    mine = (layer_out.reshape(rows, length, width), token_gradient.reshape(rows, length, width), image_gradient[None])
    return mine + outs


def finish(member, sums, small_sums, slim, width):
    half = width // 2
    pieces = jnp.stack([sums[u] for u in UNIT_OF_PIECE]).reshape(len(UNIT_OF_PIECE), 2, slim, width)
    ours, theirs = pieces[:, member], pieces[:, 1 - member]
    both = jnp.stack(list(both_rows(member, ours, swap_cores(theirs))))

    def halves(piece, side):
        return jnp.concatenate([both[0, piece][:, side * half : (side + 1) * half], both[1, piece][:, side * half : (side + 1) * half]], axis=1)

    def up(piece):
        parts = [both[:, piece + s].reshape(2, slim, CHIPS, 2 * slim) for s in (0, 1)]
        return jnp.stack(parts, axis=0).transpose(2, 3, 1, 0, 4).reshape(slim, 4 * width)

    self_weight = jnp.stack([jnp.concatenate([halves(p, 0), halves(p, 1), halves(p + 1, 0)], axis=1) for p in (0, 4)])
    self_out = jnp.stack([halves(p, 1) for p in (1, 5)])
    up_gradient = jnp.stack([up(2), up(6)])
    down = jnp.stack([jnp.concatenate([sums[u], sums[u + 1]]) for u in (4, 12)])
    pair = jnp.concatenate([halves(9, 0), halves(9, 1)], axis=1)
    table = small_sums.T
    shared = table[:21]
    other = swap_cores(shared)
    split = jnp.zeros((21, 1), bool).at[jnp.array([5 + n for n in (5, 6, 9, 10, 13, 14)])].set(True)
    shared = jnp.where(split, shared + other, shared)
    shared = lax.dynamic_slice_in_dim(shared, member * slim, slim, 1)
    up_bias = table[21:25].reshape(2, 4 * slim)
    return (shared[:5], shared[5:], up_bias, self_weight, self_out, up_gradient, down, halves(8, 0), pair, halves(8, 1))


def solution(mesh):
    in_specs = (
        P(("dp", "heads"), None, None),
        P(("dp", "heads"), None, None),
        P("dp", None),
        P("dp", None),
        P(("dp", "heads"), None, None),
        P(None, ("dp", "heads")),
        P(None, ("dp", "heads")),
        P(None, ("dp", "heads")),
        P(None, ("dp", "heads"), None),
        P(None, ("dp", "heads"), None),
        P(None, ("dp", "heads"), None),
        P(None, ("dp", "heads"), None),
        P(("dp", "heads"), None),
        P(("dp", "heads"), None),
        P(("dp", "heads"), None),
    )
    out_specs = (
        P(("dp", "heads"), None, None),
        P(("dp", "heads"), None, None),
        P(("dp", "heads"), None, None),
        P(None, ("dp", "heads")),
        P(None, ("dp", "heads")),
        P(None, ("dp", "heads")),
        P(None, ("dp", "heads"), None),
        P(None, ("dp", "heads"), None),
        P(None, ("dp", "heads"), None),
        P(None, ("dp", "heads"), None),
        P(("dp", "heads"), None),
        P(("dp", "heads"), None),
        P(("dp", "heads"), None),
    )
    dp, cores = mesh.shape["dp"], mesh.shape["heads"]
    program = chip_program if (dp, cores) == (CHIPS, 2) else per_device
    return jax.shard_map(
        program, mesh=mesh, in_specs=in_specs, out_specs=out_specs, check_vma=False
    )
```
